32 devices in a mesh: head: 2 (over x), blk: 16 (over z, y, core).
Axes of the slice: x: 2, y: 2, z: 4, core: 2. Of those that a mesh axis runs over, the one named last changes fastest.
Arguments:
- tokens: bfloat16 [4096, 768], P(('head', 'blk')), may hold values from -6 to 6
- query_weight: bfloat16 [768, 768], P(('head', 'blk')), may hold values from -0.21875 to 0.21875
- query_bias: bfloat16 [768], P(('head', 'blk')), may hold values from -3 to 3
- key_weight: bfloat16 [768, 768], P(('head', 'blk')), may hold values from -0.21875 to 0.21875
- value_weight: bfloat16 [768, 768], P(('head', 'blk')), may hold values from -0.21875 to 0.21875
- value_bias: bfloat16 [768], P(('head', 'blk')), may hold values from -3 to 3
- output_weight: bfloat16 [768, 768], P(('head', 'blk')), may hold values from -6 to 6
- output_bias: bfloat16 [768], P(('head', 'blk')), may hold values from -3 to 3
- first_gain: bfloat16 [768], P(('head', 'blk')), may hold values from 0.099609375 to 1.8984375
- first_shift: bfloat16 [768], P(('head', 'blk')), may hold values from -3 to 3
- inner_weight: bfloat16 [768, 3072], P(('head', 'blk')), may hold values from -0.21875 to 0.21875
- inner_bias: bfloat16 [3072], P(('head', 'blk')), may hold values from -3 to 3
- outer_weight: bfloat16 [3072, 768], P(('head', 'blk')), may hold values from -0.109375 to 0.109375
- outer_bias: bfloat16 [768], P(('head', 'blk')), may hold values from -3 to 3
- second_gain: bfloat16 [768], P(('head', 'blk')), may hold values from 0.099609375 to 1.8984375
- second_shift: bfloat16 [768], P(('head', 'blk')), may hold values from -3 to 3
- doc_starts: int32 [16], replicated, may hold values from 0 to 4095, as said below
- out_grad: bfloat16 [4096, 768], P(('head', 'blk')), may hold values from -6 to 6
Outputs:
- layer_out: bfloat16 [4096, 768], P(('head', 'blk'))
- tokens_grad: bfloat16 [4096, 768], P(('head', 'blk'))
- query_weight_grad: float32 [768, 768], P(('head', 'blk'))
- query_bias_grad: float32 [768], P(('head', 'blk'))
- key_weight_grad: float32 [768, 768], P(('head', 'blk'))
- value_weight_grad: float32 [768, 768], P(('head', 'blk'))
- value_bias_grad: float32 [768], P(('head', 'blk'))
- output_weight_grad: float32 [768, 768], P(('head', 'blk'))
- output_bias_grad: float32 [768], P(('head', 'blk'))
- first_gain_grad: float32 [768], P(('head', 'blk'))
- first_shift_grad: float32 [768], P(('head', 'blk'))
- inner_weight_grad: float32 [768, 3072], P(('head', 'blk'))
- inner_bias_grad: float32 [3072], P(('head', 'blk'))
- outer_weight_grad: float32 [3072, 768], P(('head', 'blk'))
- outer_bias_grad: float32 [768], P(('head', 'blk'))
- second_gain_grad: float32 [768], P(('head', 'blk'))
- second_shift_grad: float32 [768], P(('head', 'blk'))
The draws below stay inside these ranges and needn't reach their ends.
Inputs may be any that keep to these rules, and one draw needn't show every extreme that they name: doc_starts rises strictly, begins with 0 and ends with 4095; one entry equals 2048, so no document crosses position 2048; one document begins before position 128 and ends at or after position 1920.
All inputs are finite; a program needn't handle non-finite values.
Results may differ from the reference program's by a relative error of at most 0.025.
Values may be sent and summed in bfloat16 or wider, within the bound.
A program may use at most 256 MiB of HBM per device.

```python
import math
import jax
import jax.numpy as jnp
from jax import lax

D = 768
HEADS = 12
HEAD_DIM = 64
FF = 3072
TOK_DEV = 128
NDOC = 16
HALF = 2048
TOKENS = 4096


def draw_doc_starts(key, part):
    head_key = jax.random.fold_in(key, 101)
    end_key = jax.random.fold_in(key, 202)
    tail_key = jax.random.fold_in(key, 303)
    head_picks = jnp.sort(jax.random.permutation(head_key, TOK_DEV - 1)[:2].astype(jnp.int32) + 1)
    long_end = jax.random.randint(end_key, (1,), HALF - TOK_DEV + 1, HALF).astype(jnp.int32)
    tail_picks = jnp.sort(jax.random.permutation(tail_key, HALF - 2)[:NDOC - 6].astype(jnp.int32) + HALF + 1)
    first_entry = jnp.zeros((1,), jnp.int32)
    middle_entry = jnp.full((1,), HALF, jnp.int32)
    last_entry = jnp.full((1,), TOKENS - 1, jnp.int32)
    return jnp.concatenate([first_entry, head_picks, long_end, middle_entry, tail_picks, last_entry]).astype(jnp.int32)


def level_of(rng, dims, cuts, smallest, top_value):
    def one(position, shards_of):
        steps = jax.random.uniform(jax.random.fold_in(jax.random.fold_in(rng, 6), position), (shards_of,), jnp.float32, smallest / len(cuts), top_value / len(cuts))
        return jnp.repeat(jnp.exp(steps), dims[position] // shards_of).reshape((-1,) + (1,) * (len(dims) - position - 1))

    factor_of = one(*cuts[0])
    for cut in cuts[1:]:
        factor_of = factor_of * one(*cut)
    return factor_of


def noise(stream_key, shape, scale, limit, shards=(), held_as=jnp.bfloat16):
    drawn = scale * jax.random.normal(stream_key, shape, jnp.float32)
    if shards:
        drawn = drawn * level_of(stream_key, shape, shards, -0.22, 0.18)
    return jnp.clip(drawn, -limit, limit).astype(held_as)


def setup_inputs(seed: int = 0) -> dict:
    streams_of = jax.random.split(jax.random.key(seed), 19)
    tokens = noise(streams_of[0], (TOKENS, D), 1.0, 6.0, ((0, 32),))
    query_weight = noise(streams_of[1], (D, D), D ** -0.5, 0.21875, ((0, 32),))
    query_bias = noise(streams_of[2], (D,), 0.5, 3.0, ((0, 32),))
    key_weight = noise(streams_of[3], (D, D), D ** -0.5, 0.21875, ((0, 32),))
    value_weight = noise(streams_of[4], (D, D), D ** -0.5, 0.21875, ((0, 32),))
    value_bias = noise(streams_of[5], (D,), 0.5, 3.0, ((0, 32),))
    output_weight = noise(streams_of[6], (D, D), 1.0, 6.0, ((0, 32),))
    output_bias = noise(streams_of[7], (D,), 0.5, 3.0, ((0, 32),))
    first_gain = jnp.clip(1.0 + 0.18 * jax.random.normal(streams_of[8], (D,), jnp.float32), 0.099609375, 1.8984375).astype(jnp.bfloat16)
    first_shift = noise(streams_of[9], (D,), 0.5, 3.0, ((0, 32),))
    inner_weight = noise(streams_of[10], (D, FF), D ** -0.5, 0.21875, ((0, 32),))
    inner_bias = noise(streams_of[11], (FF,), 0.5, 3.0, ((0, 32),))
    outer_weight = noise(streams_of[12], (FF, D), FF ** -0.5, 0.109375, ((0, 32),))
    outer_bias = noise(streams_of[13], (D,), 0.5, 3.0, ((0, 32),))
    second_gain = jnp.clip(1.0 + 0.18 * jax.random.normal(streams_of[14], (D,), jnp.float32), 0.099609375, 1.8984375).astype(jnp.bfloat16)
    second_shift = noise(streams_of[15], (D,), 0.5, 3.0, ((0, 32),))
    doc_starts = draw_doc_starts(jax.random.fold_in(streams_of[18], 71), 0)
    out_grad = noise(streams_of[17], (TOKENS, D), 1.0, 6.0, ((0, 32),))
    return dict(tokens=tokens, query_weight=query_weight, query_bias=query_bias, key_weight=key_weight, value_weight=value_weight, value_bias=value_bias, output_weight=output_weight, output_bias=output_bias, first_gain=first_gain, first_shift=first_shift, inner_weight=inner_weight, inner_bias=inner_bias, outer_weight=outer_weight, outer_bias=outer_bias, second_gain=second_gain, second_shift=second_shift, doc_starts=doc_starts, out_grad=out_grad)


@jax.custom_vjp
def low(v):
    return lax.optimization_barrier(v.astype(jnp.bfloat16)).astype(jnp.float32)

@jax.custom_vjp
def low_back(v):
    return v

def low_keep(v):
    return (low(v), None)

def low_pass(kept, grad):
    return (grad,)

def back_keep(v):
    return (v, None)

def back_low(kept, grad):
    return (low(grad),)
low.defvjp(low_keep, low_pass)
low_back.defvjp(back_keep, back_low)
HIGHEST_PRECISION = lax.Precision.HIGHEST
LN_EPS = 1e-12
MASKED_SCORE = -1e+30

def product(left_side, right_side):
    return jnp.dot(left_side, right_side, precision=HIGHEST_PRECISION, preferred_element_type=jnp.float32)

def norm_layer(residual, scale_gain, shift_bias):
    row_mean = lax.optimization_barrier(jnp.mean(residual, axis=-1, keepdims=True))
    centred = residual - row_mean
    variance = lax.optimization_barrier(jnp.mean(centred * centred, axis=-1, keepdims=True))
    return centred * lax.rsqrt(variance + LN_EPS) * scale_gain + shift_bias

def attend_half(query_rows, key_rows, value_rows, doc_index):
    row_count = query_rows.shape[0]
    block_rows = math.gcd(row_count, 512)
    query_blocks = query_rows.reshape(row_count // block_rows, block_rows, HEADS, HEAD_DIM)
    doc_blocks = doc_index.reshape(row_count // block_rows, block_rows)

    @jax.checkpoint
    def one_block(operands):
        query_block, doc_block = operands
        scores = jnp.einsum('qhd,khd->hqk', query_block, key_rows, precision=HIGHEST_PRECISION) * HEAD_DIM ** (-0.5)
        scores = low_back(scores)
        allowed = (doc_block[:, None] == doc_index[None, :])[None, :, :]
        scores = jnp.where(allowed, scores, MASKED_SCORE)
        weights = low(jax.nn.softmax(scores, axis=-1))
        return jnp.einsum('hqk,khd->qhd', weights, value_rows, precision=HIGHEST_PRECISION)
    outputs = lax.map(one_block, (query_blocks, doc_blocks))
    return outputs.reshape(row_count, HEADS * HEAD_DIM)

def layer_forward(doc_index, inputs, params):
    query_weight, query_bias, key_weight, value_weight, value_bias, output_weight, output_bias, first_gain, first_shift, inner_weight, inner_bias, outer_weight, outer_bias, second_gain, second_shift = params
    queries = low_back(low(product(inputs, query_weight) + query_bias))
    key_values = low_back(low(product(inputs, key_weight)))
    values = low_back(low(product(inputs, value_weight) + value_bias))
    query_halves = queries.reshape(2, HALF, HEADS, HEAD_DIM)
    key_halves = key_values.reshape(2, HALF, HEADS, HEAD_DIM)
    value_halves = values.reshape(2, HALF, HEADS, HEAD_DIM)
    doc_halves = doc_index.reshape(2, HALF)
    pieces = []
    for half_index in range(2):
        pieces.append(attend_half(query_halves[half_index], key_halves[half_index], value_halves[half_index], doc_halves[half_index]))
    attended = low_back(low(jnp.concatenate(pieces, axis=0)))
    branch = low_back(product(attended, output_weight) + output_bias)
    hidden = norm_layer(inputs + branch, first_gain, first_shift)
    inner_value = low_back(product(low(hidden), inner_weight) + inner_bias)
    activated = low(jax.nn.gelu(inner_value, approximate=False))
    outer_value = low_back(product(activated, outer_weight) + outer_bias)
    return norm_layer(hidden + outer_value, second_gain, second_shift)

def reference(tokens, query_weight, query_bias, key_weight, value_weight, value_bias, output_weight, output_bias, first_gain, first_shift, inner_weight, inner_bias, outer_weight, outer_bias, second_gain, second_shift, doc_starts, out_grad):
    positions = jnp.arange(TOKENS, dtype=jnp.int32)
    doc_index = lax.optimization_barrier(jnp.sum((doc_starts[None, :] <= positions[:, None]).astype(jnp.int32), axis=1)) - 1
    params = tuple((member.astype(jnp.float32) for member in (query_weight, query_bias, key_weight, value_weight, value_bias, output_weight, output_bias, first_gain, first_shift, inner_weight, inner_bias, outer_weight, outer_bias, second_gain, second_shift)))

    def wrapped(inputs, params_in):
        return layer_forward(doc_index, inputs, params_in)
    layer_value, pullback = jax.vjp(wrapped, tokens.astype(jnp.float32), params)
    tokens_grad, grads = pullback(out_grad.astype(jnp.float32))
    return (layer_value.astype(jnp.bfloat16), tokens_grad.astype(jnp.bfloat16), grads[0], grads[1], grads[2], grads[3], grads[4], grads[5], grads[6], grads[7], grads[8], grads[9], grads[10], grads[11], grads[12], grads[13], grads[14])
```

```python
from functools import partial

import jax
import jax.numpy as jnp
from jax import lax
from jax.experimental import pallas as pl
from jax.experimental.pallas import tpu as pltpu
from jax.sharding import PartitionSpec as P

HEAD_DIM = 64


LN_EPS = 1e-12
MASKED_SCORE = -1e30


def doc_numbers(doc_starts, positions):
    covered = (doc_starts[None, :] <= positions[:, None]).astype(jnp.int32)
    return (jnp.sum(covered, axis=1) - 1).astype(jnp.float32)


def dense_product(left_side, right_side):
    return jnp.dot(left_side, right_side, preferred_element_type=jnp.float32)


def product_back(left_side, right_side):
    return lax.dot_general(
        left_side, right_side, (((1,), (1,)), ((), ())), preferred_element_type=jnp.float32
    )


def product_left(left_side, right_side):
    return lax.dot_general(
        left_side, right_side, (((0,), (0,)), ((), ())), preferred_element_type=jnp.float32
    )


def norm_forward(residual, scale_gain, shift_bias):
    row_mean = jnp.mean(residual, axis=-1, keepdims=True)
    centred = residual - row_mean
    variance = jnp.mean(centred * centred, axis=-1, keepdims=True)
    inverse = lax.rsqrt(variance + LN_EPS)
    normed = centred * inverse
    return (normed * scale_gain + shift_bias, normed, inverse)


def norm_backward(grad_output, normed, inverse, scale_gain):
    grad_normed = grad_output * scale_gain
    first_term = jnp.mean(grad_normed, axis=-1, keepdims=True)
    second_term = jnp.mean(grad_normed * normed, axis=-1, keepdims=True)
    grad_input = inverse * (grad_normed - first_term - normed * second_term)
    return (grad_input, jnp.sum(grad_output * normed, axis=0), jnp.sum(grad_output, axis=0))


def split_blocks(rows_array, block_rows):
    return rows_array.reshape(-1, block_rows, rows_array.shape[1] // HEAD_DIM, HEAD_DIM)


def blocks_to_rows(blocked):
    reordered = jnp.transpose(blocked, (0, 2, 1, 3))
    return reordered.reshape(-1, blocked.shape[1] * blocked.shape[3])


def block_scores(query_block, key_block, query_docs, key_docs):
    scores = jnp.einsum(
        "qhd,khd->hqk", query_block, key_block, preferred_element_type=jnp.float32
    ) * HEAD_DIM ** (-0.5)
    allowed = (query_docs[:, None] == key_docs[None, :])[None, :, :]
    return (scores, allowed)


def intersecting(first_docs, second_docs):
    return jnp.logical_and(
        jnp.max(first_docs) >= jnp.min(second_docs), jnp.min(first_docs) <= jnp.max(second_docs)
    )


def keep_state(carried):
    return carried


def forward_update(carried, query_block, query_docs, key_block, value_block, key_docs):
    running_max, row_total, accumulated = carried
    scores, allowed = block_scores(query_block, key_block, query_docs, key_docs)
    scores = jnp.where(allowed, scores, MASKED_SCORE)
    new_max = jnp.maximum(running_max, jnp.max(scores, axis=2))
    decay_factor = jnp.exp(running_max - new_max)
    weights = jnp.where(allowed, jnp.exp(scores - new_max[:, :, None]), 0.0)
    row_total = row_total * decay_factor + jnp.sum(weights, axis=2)
    update = jnp.einsum(
        "hqk,khd->hqd",
        weights.astype(jnp.bfloat16),
        value_block,
        preferred_element_type=jnp.float32,
    )
    return (new_max, row_total, accumulated * decay_factor[:, :, None] + update)


def forward_folder(query_blocks, doc_blocks):
    block_rows = query_blocks.shape[1]

    def forward_fold_step(carried_in, pieces, start_row):
        key_piece, value_piece, key_doc_piece = pieces
        key_blocks = split_blocks(key_piece, block_rows)
        value_blocks = split_blocks(value_piece, block_rows)
        key_doc_blocks = key_doc_piece.astype(jnp.float32).reshape(-1, block_rows)

        def forward_one_block(block_index, carried):
            key_docs = key_doc_blocks[block_index]
            results = []
            for query_index in range(query_blocks.shape[0]):
                current = tuple((member[query_index] for member in carried))
                update = partial(
                    forward_update,
                    query_block=query_blocks[query_index],
                    query_docs=doc_blocks[query_index],
                    key_block=key_blocks[block_index],
                    value_block=value_blocks[block_index],
                    key_docs=key_docs,
                )
                results.append(
                    lax.cond(
                        intersecting(doc_blocks[query_index], key_docs), update, keep_state, current
                    )
                )
            return tuple((jnp.stack([entry[member] for entry in results]) for member in range(3)))

        return lax.fori_loop(0, key_blocks.shape[0], forward_one_block, carried_in)

    return forward_fold_step


def query_grad_update(
    grad_query,
    query_block,
    query_docs,
    grad_block,
    log_total,
    delta_rows,
    key_block,
    value_block,
    key_docs,
):
    scores, allowed = block_scores(query_block, key_block, query_docs, key_docs)
    probs = jnp.where(allowed, jnp.exp(scores - log_total[:, :, None]), 0.0)
    grad_probs = jnp.einsum(
        "qhd,khd->hqk", grad_block, value_block, preferred_element_type=jnp.float32
    )
    grad_scores = (probs * (grad_probs - delta_rows[:, :, None])).astype(jnp.bfloat16)
    return grad_query + jnp.einsum(
        "hqk,khd->hqd", grad_scores, key_block, preferred_element_type=jnp.float32
    ) * HEAD_DIM ** (-0.5)


def query_grad_folder(query_blocks, doc_blocks, grad_blocks, log_blocks, delta_blocks):
    block_rows = query_blocks.shape[1]

    def query_fold_step(carried_in, pieces, start_row):
        key_piece, value_piece, key_doc_piece = pieces
        key_blocks = split_blocks(key_piece, block_rows)
        value_blocks = split_blocks(value_piece, block_rows)
        key_doc_blocks = key_doc_piece.astype(jnp.float32).reshape(-1, block_rows)

        def query_one_block(block_index, carried):
            key_docs = key_doc_blocks[block_index]
            results = []
            for query_index in range(query_blocks.shape[0]):
                update = partial(
                    query_grad_update,
                    query_block=query_blocks[query_index],
                    query_docs=doc_blocks[query_index],
                    grad_block=grad_blocks[query_index],
                    log_total=log_blocks[query_index],
                    delta_rows=delta_blocks[query_index],
                    key_block=key_blocks[block_index],
                    value_block=value_blocks[block_index],
                    key_docs=key_docs,
                )
                results.append(
                    lax.cond(
                        intersecting(doc_blocks[query_index], key_docs),
                        update,
                        keep_state,
                        carried[query_index],
                    )
                )
            return jnp.stack(results)

        return lax.fori_loop(0, key_blocks.shape[0], query_one_block, carried_in)

    return query_fold_step


def key_grad_update(
    carried,
    key_block,
    value_block,
    key_docs,
    query_block,
    grad_block,
    log_total,
    delta_rows,
    query_docs,
):
    grad_key, grad_value = carried
    scores, allowed = block_scores(query_block, key_block, query_docs, key_docs)
    probs = jnp.where(allowed, jnp.exp(scores - log_total[:, :, None]), 0.0)
    grad_value = grad_value + jnp.einsum(
        "hqk,qhd->hkd", probs.astype(jnp.bfloat16), grad_block, preferred_element_type=jnp.float32
    )
    grad_probs = jnp.einsum(
        "qhd,khd->hqk", grad_block, value_block, preferred_element_type=jnp.float32
    )
    grad_scores = (probs * (grad_probs - delta_rows[:, :, None])).astype(jnp.bfloat16)
    grad_key = grad_key + jnp.einsum(
        "hqk,qhd->hkd", grad_scores, query_block, preferred_element_type=jnp.float32
    ) * HEAD_DIM ** (-0.5)
    return (grad_key, grad_value)


def key_grad_folder(key_blocks, value_blocks, doc_blocks):
    block_rows = key_blocks.shape[1]

    def key_fold_step(carried_in, pieces, start_row):
        query_piece, grad_piece, log_piece, delta_piece, doc_piece = pieces
        query_blocks = split_blocks(query_piece.astype(jnp.bfloat16), block_rows)
        grad_blocks = split_blocks(grad_piece.astype(jnp.bfloat16), block_rows)
        log_blocks = jnp.transpose(log_piece.reshape(-1, block_rows, log_piece.shape[1]), (0, 2, 1))
        delta_blocks = jnp.transpose(
            delta_piece.reshape(-1, block_rows, delta_piece.shape[1]), (0, 2, 1)
        )
        query_doc_blocks = doc_piece.reshape(-1, block_rows)

        def key_one_block(block_index, carried):
            query_docs = query_doc_blocks[block_index]
            results = []
            for key_index in range(key_blocks.shape[0]):
                current = (carried[0][key_index], carried[1][key_index])
                update = partial(
                    key_grad_update,
                    key_block=key_blocks[key_index],
                    value_block=value_blocks[key_index],
                    key_docs=doc_blocks[key_index],
                    query_block=query_blocks[block_index],
                    grad_block=grad_blocks[block_index],
                    log_total=log_blocks[block_index],
                    delta_rows=delta_blocks[block_index],
                    query_docs=query_docs,
                )
                results.append(
                    lax.cond(
                        intersecting(query_docs, doc_blocks[key_index]), update, keep_state, current
                    )
                )
            return (
                jnp.stack([entry[0] for entry in results]),
                jnp.stack([entry[1] for entry in results]),
            )

        return lax.fori_loop(0, query_blocks.shape[0], key_one_block, carried_in)

    return key_fold_step


def attention_forward(query_rows, key_rows, value_rows, row_docs, block_rows):
    query_blocks = split_blocks(query_rows, block_rows)
    doc_blocks = row_docs.reshape(-1, block_rows)
    block_count = query_blocks.shape[0]
    head_count = query_blocks.shape[2]
    send_docs = row_docs.astype(jnp.bfloat16)
    start_state = (
        jnp.full((block_count, head_count, block_rows), MASKED_SCORE, jnp.float32),
        jnp.zeros((block_count, head_count, block_rows), jnp.float32),
        jnp.zeros((block_count, head_count, block_rows, HEAD_DIM), jnp.float32),
    )
    fold_forward = forward_folder(query_blocks, doc_blocks)
    running_max, row_total, accumulated = fold_forward(
        start_state,
        (
            lax.all_gather(key_rows, "blk", axis=0, tiled=True),
            lax.all_gather(value_rows, "blk", axis=0, tiled=True),
            lax.all_gather(send_docs, "blk", axis=0, tiled=True),
        ),
        jnp.int32(0),
    )
    head_outputs = blocks_to_rows(accumulated / row_total[:, :, :, None]).astype(jnp.bfloat16)
    log_total = running_max + jnp.log(row_total)
    return (head_outputs, log_total)


def attention_backward(
    grad_rows, head_outputs, log_total, query_rows, key_rows, value_rows, row_docs, block_rows
):
    query_blocks = split_blocks(query_rows, block_rows)
    key_blocks = split_blocks(key_rows, block_rows)
    value_blocks = split_blocks(value_rows, block_rows)
    doc_blocks = row_docs.reshape(-1, block_rows)
    block_count = query_blocks.shape[0]
    head_count = query_blocks.shape[2]
    send_docs = row_docs.astype(jnp.bfloat16)
    grad_blocks = split_blocks(grad_rows, block_rows)
    output_blocks = split_blocks(head_outputs, block_rows)
    delta_blocks = jnp.einsum(
        "nqhd,nqhd->nhq", grad_blocks.astype(jnp.float32), output_blocks.astype(jnp.float32)
    )
    log_rows = jnp.transpose(log_total, (0, 2, 1)).reshape(-1, head_count)
    delta_rows = jnp.transpose(delta_blocks, (0, 2, 1)).reshape(-1, head_count)
    fold_queries = query_grad_folder(query_blocks, doc_blocks, grad_blocks, log_total, delta_blocks)
    fold_keys = key_grad_folder(key_blocks, value_blocks, doc_blocks)
    query_start = jnp.zeros((block_count, head_count, block_rows, HEAD_DIM), jnp.float32)
    key_start = (query_start, query_start)
    query_send = (
        query_rows.astype(jnp.float32),
        grad_rows.astype(jnp.float32),
        log_rows,
        delta_rows,
        row_docs,
    )
    grad_query_state = fold_queries(
        query_start,
        (
            lax.all_gather(key_rows, "blk", axis=0, tiled=True),
            lax.all_gather(value_rows, "blk", axis=0, tiled=True),
            lax.all_gather(send_docs, "blk", axis=0, tiled=True),
        ),
        jnp.int32(0),
    )
    grad_key_state, grad_value_state = fold_keys(
        key_start,
        (
            lax.all_gather(query_send[0], "blk", axis=0, tiled=True),
            lax.all_gather(query_send[1], "blk", axis=0, tiled=True),
            lax.all_gather(query_send[2], "blk", axis=0, tiled=True),
            lax.all_gather(query_send[3], "blk", axis=0, tiled=True),
            lax.all_gather(query_send[4], "blk", axis=0, tiled=True),
        ),
        jnp.int32(0),
    )
    return (
        blocks_to_rows(grad_query_state).astype(jnp.bfloat16),
        blocks_to_rows(grad_key_state).astype(jnp.bfloat16),
        blocks_to_rows(grad_value_state).astype(jnp.bfloat16),
    )


def data_layer(tokens, full, row_docs, out_grad, block_rows):
    (
        full_query,
        full_query_bias,
        full_key,
        full_value,
        full_value_bias,
        full_output,
        full_output_bias,
        full_first_gain,
        full_first_shift,
        full_inner,
        full_inner_bias,
        full_outer,
        full_outer_bias,
        full_second_gain,
        full_second_shift,
    ) = full
    queries = (dense_product(tokens, full_query) + full_query_bias.astype(jnp.float32)).astype(
        jnp.bfloat16
    )
    keys_local = dense_product(tokens, full_key).astype(jnp.bfloat16)
    values_local = (dense_product(tokens, full_value) + full_value_bias.astype(jnp.float32)).astype(
        jnp.bfloat16
    )
    query_rows, key_rows, value_rows = (
        lax.all_to_all(queries, "head", split_axis=1, concat_axis=0, tiled=True),
        lax.all_to_all(keys_local, "head", split_axis=1, concat_axis=0, tiled=True),
        lax.all_to_all(values_local, "head", split_axis=1, concat_axis=0, tiled=True),
    )
    head_outputs, log_total = attention_forward(
        query_rows, key_rows, value_rows, row_docs, block_rows
    )
    attended = lax.all_to_all(head_outputs, "head", split_axis=0, concat_axis=1, tiled=True)
    branch = dense_product(attended, full_output) + full_output_bias.astype(jnp.float32)
    hidden, first_normed, first_inverse = norm_forward(
        tokens.astype(jnp.float32) + branch,
        full_first_gain.astype(jnp.float32),
        full_first_shift.astype(jnp.float32),
    )
    hidden_low = hidden.astype(jnp.bfloat16)
    inner_value = dense_product(hidden_low, full_inner) + full_inner_bias.astype(jnp.float32)
    activated_full, gelu_pullback = jax.vjp(partial(jax.nn.gelu, approximate=False), inner_value)
    activated = activated_full.astype(jnp.bfloat16)
    outer_value = dense_product(activated, full_outer) + full_outer_bias.astype(jnp.float32)
    layer_full, second_normed, second_inverse = norm_forward(
        hidden + outer_value,
        full_second_gain.astype(jnp.float32),
        full_second_shift.astype(jnp.float32),
    )
    layer_out = layer_full.astype(jnp.bfloat16)
    grad_output = out_grad.astype(jnp.float32)
    grad_resid2, second_gain_term, second_shift_term = norm_backward(
        grad_output, second_normed, second_inverse, full_second_gain.astype(jnp.float32)
    )
    grad_outer = grad_resid2.astype(jnp.bfloat16)
    outer_weight_term = product_left(activated, grad_outer)
    outer_bias_term = jnp.sum(grad_outer.astype(jnp.float32), axis=0)
    grad_inner = gelu_pullback(product_back(grad_outer, full_outer))[0].astype(jnp.bfloat16)
    inner_weight_term = product_left(hidden_low, grad_inner)
    inner_bias_term = jnp.sum(grad_inner.astype(jnp.float32), axis=0)
    grad_hidden = grad_resid2 + product_back(grad_inner, full_inner)
    grad_resid1, first_gain_term, first_shift_term = norm_backward(
        grad_hidden, first_normed, first_inverse, full_first_gain.astype(jnp.float32)
    )
    grad_branch = grad_resid1.astype(jnp.bfloat16)
    output_weight_term = product_left(attended, grad_branch)
    output_bias_term = jnp.sum(grad_branch.astype(jnp.float32), axis=0)
    grad_attended = product_back(grad_branch, full_output).astype(jnp.bfloat16)
    grad_rows = lax.all_to_all(grad_attended, "head", split_axis=1, concat_axis=0, tiled=True)
    grad_query_rows, grad_key_rows, grad_value_rows = attention_backward(
        grad_rows, head_outputs, log_total, query_rows, key_rows, value_rows, row_docs, block_rows
    )
    grad_queries, grad_keys, grad_values = (
        lax.all_to_all(grad_query_rows, "head", split_axis=0, concat_axis=1, tiled=True),
        lax.all_to_all(grad_key_rows, "head", split_axis=0, concat_axis=1, tiled=True),
        lax.all_to_all(grad_value_rows, "head", split_axis=0, concat_axis=1, tiled=True),
    )
    query_weight_term = product_left(tokens, grad_queries)
    query_bias_term = jnp.sum(grad_queries.astype(jnp.float32), axis=0)
    key_weight_term = product_left(tokens, grad_keys)
    value_weight_term = product_left(tokens, grad_values)
    value_bias_term = jnp.sum(grad_values.astype(jnp.float32), axis=0)
    tokens_grad = (
        grad_resid1
        + product_back(grad_queries, full_query)
        + product_back(grad_keys, full_key)
        + product_back(grad_values, full_value)
    ).astype(jnp.bfloat16)
    summed = (
        lax.psum_scatter(query_weight_term, ("head", "blk"), scatter_dimension=0, tiled=True),
        lax.psum_scatter(query_bias_term, ("head", "blk"), scatter_dimension=0, tiled=True),
        lax.psum_scatter(key_weight_term, ("head", "blk"), scatter_dimension=0, tiled=True),
        lax.psum_scatter(value_weight_term, ("head", "blk"), scatter_dimension=0, tiled=True),
        lax.psum_scatter(value_bias_term, ("head", "blk"), scatter_dimension=0, tiled=True),
        lax.psum_scatter(output_weight_term, ("head", "blk"), scatter_dimension=0, tiled=True),
        lax.psum_scatter(output_bias_term, ("head", "blk"), scatter_dimension=0, tiled=True),
        lax.psum_scatter(first_gain_term, ("head", "blk"), scatter_dimension=0, tiled=True),
        lax.psum_scatter(first_shift_term, ("head", "blk"), scatter_dimension=0, tiled=True),
        lax.psum_scatter(inner_weight_term, ("head", "blk"), scatter_dimension=0, tiled=True),
        lax.psum_scatter(inner_bias_term, ("head", "blk"), scatter_dimension=0, tiled=True),
        lax.psum_scatter(outer_weight_term, ("head", "blk"), scatter_dimension=0, tiled=True),
        lax.psum_scatter(outer_bias_term, ("head", "blk"), scatter_dimension=0, tiled=True),
        lax.psum_scatter(second_gain_term, ("head", "blk"), scatter_dimension=0, tiled=True),
        lax.psum_scatter(second_shift_term, ("head", "blk"), scatter_dimension=0, tiled=True),
    )
    return (layer_out, tokens_grad) + tuple(summed)


def body(
    tokens,
    query_weight,
    query_bias,
    key_weight,
    value_weight,
    value_bias,
    output_weight,
    output_bias,
    first_gain,
    first_shift,
    inner_weight,
    inner_bias,
    outer_weight,
    outer_bias,
    second_gain,
    second_shift,
    doc_starts,
    out_grad,
):
    shards = (
        query_weight,
        query_bias,
        key_weight,
        value_weight,
        value_bias,
        output_weight,
        output_bias,
        first_gain,
        first_shift,
        inner_weight,
        inner_bias,
        outer_weight,
        outer_bias,
        second_gain,
        second_shift,
    )
    full = (
        lax.all_gather(shards[0], ("head", "blk"), axis=0, tiled=True),
        lax.all_gather(shards[1], ("head", "blk"), axis=0, tiled=True),
        lax.all_gather(shards[2], ("head", "blk"), axis=0, tiled=True),
        lax.all_gather(shards[3], ("head", "blk"), axis=0, tiled=True),
        lax.all_gather(shards[4], ("head", "blk"), axis=0, tiled=True),
        lax.all_gather(shards[5], ("head", "blk"), axis=0, tiled=True),
        lax.all_gather(shards[6], ("head", "blk"), axis=0, tiled=True),
        lax.all_gather(shards[7], ("head", "blk"), axis=0, tiled=True),
        lax.all_gather(shards[8], ("head", "blk"), axis=0, tiled=True),
        lax.all_gather(shards[9], ("head", "blk"), axis=0, tiled=True),
        lax.all_gather(shards[10], ("head", "blk"), axis=0, tiled=True),
        lax.all_gather(shards[11], ("head", "blk"), axis=0, tiled=True),
        lax.all_gather(shards[12], ("head", "blk"), axis=0, tiled=True),
        lax.all_gather(shards[13], ("head", "blk"), axis=0, tiled=True),
        lax.all_gather(shards[14], ("head", "blk"), axis=0, tiled=True),
    )
    tok_rows = tokens.shape[0]
    half_length = tok_rows * lax.axis_size("blk")
    blk_place = lax.axis_index("blk")
    offsets = jnp.arange(tok_rows, dtype=jnp.int32)
    row_positions = jnp.concatenate(
        [blk_place * tok_rows + offsets, half_length + blk_place * tok_rows + offsets]
    )
    row_docs = doc_numbers(doc_starts, row_positions)
    return data_layer(tokens, full, row_docs, out_grad, tok_rows)


MESH = pl.DeviceIdType.MESH
F32 = jnp.float32
BF16 = jnp.bfloat16
D = 768
QUARTER = 384
FF_CORE = 1536
HALF_ROWS = 2048
CHIP_ROWS = 256
CORE_HEADS = 6
PENALTY = -1e30


def nn(a, b):
    return lax.dot_general(a, b, (((1,), (0,)), ((), ())), preferred_element_type=F32)


def nt(a, b):
    return lax.dot_general(a, b, (((1,), (1,)), ((), ())), preferred_element_type=F32)


def tn(a, b):
    return lax.dot_general(a, b, (((0,), (0,)), ((), ())), preferred_element_type=F32)


def at_128(index):
    return pl.multiple_of(index, 128)


def at_16(index):
    return pl.multiple_of(index, 16)


def at_8(index):
    return pl.multiple_of(index, 8)


class Place:
    def __init__(self):
        self.x = lax.axis_index("head")
        b = lax.axis_index("blk")
        self.z = lax.div(b, 4)
        self.y = lax.rem(lax.div(b, 2), 2)
        self.c = lax.rem(b, 2)
        self.chip = self.x * 8 + self.z * 2 + self.y
        self.slot = self.y * 4 + self.z
        self.sibling = self.device(c=1 - self.c)
        self.side = {"x": self.device(x=1 - self.x), "y": self.device(y=1 - self.y)}

    def device(self, x=None, z=None, y=None, c=None):
        x = self.x if x is None else x
        z = self.z if z is None else z
        y = self.y if y is None else y
        c = self.c if c is None else c
        return (x, z * 4 + y * 2 + c)

    def up(self, k):
        return lax.rem(self.z + k, 4)

    def down(self, k):
        return lax.rem(self.z + 4 - k, 4)


class Sems:
    def __init__(self, send, recv):
        self.send, self.recv, self.used = send, recv, 0

    def take(self, count):
        first = self.used
        self.used += count
        assert self.used <= self.send.shape[0]
        return first


class Mover:
    def __init__(self, sems, count):
        self.sems, self.first, self.copies = sems, sems.take(count), {}

    def start(self, index, src, dst, device):
        place = self.first + index
        copy = pltpu.make_async_remote_copy(
            src,
            dst,
            self.sems.send.at[place],
            self.sems.recv.at[place],
            device_id=device,
            device_id_type=MESH,
        )
        copy.start()
        self.copies[index] = copy

    def arrived(self, index):
        self.copies[index].wait_recv()

    def sent(self):
        for index in sorted(self.copies):
            self.copies[index].wait_send()


class Gather(Mover):
    def __init__(self, place, sems, ref, rows, first, second):
        super().__init__(sems, 15)
        self.place, self.ref, self.rows = place, ref, rows
        self.first_axis, self.second_axis = first, second

    def piece(self, x, z, y, count=1):
        start = at_16((x * 8 + z * 2 + y) * self.rows)
        return self.ref.at[pl.ds(start, count * self.rows)]

    def along_z(self):
        p = self.place
        mine = self.piece(p.x, p.z, p.y)
        for k in (2, 1, 3):
            self.start(k - 1, mine, mine, p.device(z=p.up(k)))

    def forward(self, k):
        p = self.place
        if k:
            self.arrived(k - 1)
        part = self.piece(p.x, p.down(k), p.y)
        self.start(3 + k, part, part, p.side[self.first_axis])

    def forward_again(self, k):
        p = self.place
        self.arrived(3 + k)
        if self.first_axis == "y":
            part = self.piece(p.x, p.down(k), 0, 2)
            self.start(7 + 2 * k, part, part, p.side["x"])
        else:
            for xx in (0, 1):
                part = self.piece(xx, p.down(k), p.y)
                self.start(7 + 2 * k + xx, part, part, p.side["y"])

    def complete(self, k):
        self.arrived(7 + 2 * k)
        if self.first_axis == "x":
            self.arrived(8 + 2 * k)


class Reduce(Mover):
    def __init__(self, place, sems, ref, rows, first, slots):
        super().__init__(sems, 15)
        self.place, self.ref, self.rows, self.axis = place, ref, rows, first
        self.one, self.two, self.three = slots

    def rows_of(self, x, z, y, count=1):
        return pl.ds(at_8((x * 8 + z * 2 + y) * self.rows), count * self.rows)

    def send_one(self, k):
        p, R = self.place, self.rows
        zz = p.up(k)
        if self.axis == "x":
            part = self.ref.at[self.rows_of(1 - p.x, zz, 0, 2)]
            self.start(2 * k, part, self.one.at[k], p.side["x"])
        else:
            for xx in (0, 1):
                part = self.ref.at[self.rows_of(xx, zz, 1 - p.y)]
                self.start(2 * k + xx, part, self.one.at[k, pl.ds(xx * R, R)], p.side["y"])

    def add(self, where, term):
        self.ref[where] = (self.ref[where].astype(F32) + term.astype(F32)).astype(self.ref.dtype)

    def send_two(self, k):
        p, R = self.place, self.rows
        zz = p.up(k)
        if self.axis == "x":
            self.arrived(2 * k)
            self.add(self.rows_of(p.x, zz, 0, 2), self.one[k])
            part = self.ref.at[self.rows_of(p.x, zz, 1 - p.y)]
            self.start(8 + k, part, self.two.at[k], p.side["y"])
        else:
            for xx in (0, 1):
                self.arrived(2 * k + xx)
                self.add(self.rows_of(xx, zz, p.y), self.one[k, xx * R : (xx + 1) * R])
            part = self.ref.at[self.rows_of(1 - p.x, zz, p.y)]
            self.start(8 + k, part, self.two.at[k], p.side["x"])

    def send_three(self, k):
        p = self.place
        zz = p.up(k)
        self.arrived(8 + k)
        where = self.rows_of(p.x, zz, p.y)
        if k:
            self.add(where, self.two[k])
            self.start(12 + k - 1, self.ref.at[where], self.three.at[k - 1], p.device(z=zz))

    def result(self):
        p = self.place
        total = self.ref[self.rows_of(p.x, p.z, p.y)].astype(F32) + self.two[0].astype(F32)
        for k in (1, 2, 3):
            self.arrived(12 + k - 1)
            total = total + self.three[k - 1].astype(F32)
        return total


def row_mean(value):
    return jnp.sum(value, axis=1, keepdims=True) * (1.0 / D)


def normed_of(residual):
    centred = residual - row_mean(residual)
    inverse = lax.rsqrt(row_mean(centred * centred) + LN_EPS)
    return centred * inverse, inverse


def normed_back(grad_normed, normed, inverse):
    return inverse * (grad_normed - row_mean(grad_normed) - normed * row_mean(grad_normed * normed))


def lane_iota(shape):
    return lax.broadcasted_iota(jnp.int32, shape, len(shape) - 1)


def row_iota(shape):
    return lax.broadcasted_iota(jnp.int32, shape, 0)


SCRATCH = dict(
    X=((HALF_ROWS, D), BF16),
    WS=((512, 128), BF16),
    WA=((D, 1536), BF16),
    WI=((D, FF_CORE), BF16),
    WT=((2 * FF_CORE, QUARTER), BF16),
    WO=((QUARTER, D), BF16),
    WTR=((FF_CORE, D), BF16),
    OG=((CHIP_ROWS, D), BF16),
    SWAP_S=((24, 3072), F32),
    SWAP_R=((24, 3072), F32),
    QKV=((HALF_ROWS, 1152), BF16),
    QE=((HALF_ROWS, 128), BF16),
    KE=((HALF_ROWS, 128), BF16),
    ATT=((CHIP_ROWS, QUARTER), BF16),
    LSE=((CHIP_ROWS, 128), F32),
    DELTA=((CHIP_ROWS, 128), F32),
    VEC=((16, D), F32),
    BIN=((8, FF_CORE), F32),
    DO=((HALF_ROWS, QUARTER), BF16),
    STAT=((16, HALF_ROWS), F32),
    PX_S=((4, CHIP_ROWS, D), BF16),
    PX_R=((4, CHIP_ROWS, D), BF16),
    PART=((CHIP_ROWS, D), F32),
    HID=((CHIP_ROWS, D), F32),
    N1=((CHIP_ROWS, D), F32),
    HL=((CHIP_ROWS, D), BF16),
    ACT=((CHIP_ROWS, FF_CORE), BF16),
    GP=((CHIP_ROWS, FF_CORE), F32),
    GIN=((CHIP_ROWS, FF_CORE), BF16),
    GO=((CHIP_ROWS, D), BF16),
    GB=((CHIP_ROWS, D), BF16),
    DQKV=((CHIP_ROWS, 1152), BF16),
    SV=((16, D), F32),
    GI=((D, FF_CORE), BF16),
    GT=((2 * FF_CORE, QUARTER), BF16),
    GT_S=((FF_CORE, QUARTER), BF16),
    GW=((D, QUARTER), BF16),
    GW_S=((QUARTER, QUARTER), BF16),
    GA=((D, 1152), BF16),
    SG=((512, 128), F32),
    GI1=((4, 96, FF_CORE), BF16),
    GI2=((4, 48, FF_CORE), BF16),
    GI3=((3, 48, FF_CORE), BF16),
    GT1=((4, 384, QUARTER), BF16),
    GT2=((4, 192, QUARTER), BF16),
    GT3=((3, 192, QUARTER), BF16),
    GW1=((4, 96, QUARTER), BF16),
    GW2=((4, 48, QUARTER), BF16),
    GW3=((3, 48, QUARTER), BF16),
    GA1=((4, 96, 1152), BF16),
    GA2=((4, 48, 1152), BF16),
    GA3=((3, 48, 1152), BF16),
    SG1=((4, 64, 128), F32),
    SG2=((4, 32, 128), F32),
    SG3=((3, 32, 128), F32),
    FI=((48, FF_CORE), F32),
    FT=((192, QUARTER), F32),
    FW=((48, QUARTER), F32),
    FA=((48, 1152), F32),
    FS=((32, 128), F32),
    FI_R=((24, FF_CORE), F32),
    FT_R=((96, QUARTER), F32),
    FW_R=((24, QUARTER), F32),
    FA_R=((24, 1152), F32),
    FS_R=((16, 128), F32),
)
SEM_COUNT = 200


class Refs:
    pass


def layer_kernel(*refs):
    r = Refs()
    (
        r.tok, r.og, r.wq, r.wk, r.wv, r.wo, r.wi, r.wt, r.small, r.docs,
        r.out, r.tgrad, r.gq, r.gk, r.gv, r.go, r.gi, r.gt, r.gs,
    ) = refs[:19]
    for name, ref in zip(SCRATCH, refs[19:]):
        setattr(r, name, ref)
    sems = Sems(refs[-2], refs[-1])
    p = Place()
    c, other = p.c, 1 - p.c

    barrier = pltpu.get_barrier_semaphore()
    partners = [p.sibling, p.side["x"], p.side["y"]] + [p.device(z=p.up(k)) for k in (1, 2, 3)]
    for partner in partners:
        pl.semaphore_signal(barrier, inc=1, device_id=partner, device_id_type=MESH)
    pl.semaphore_wait(barrier, len(partners))

    swap = Mover(sems, 16)
    tok = Mover(sems, 15)
    chip_base = p.slot * CHIP_ROWS
    own_base = chip_base + 128 * c
    chip = pl.ds(at_128(chip_base), CHIP_ROWS)
    own_half = pl.ds(at_128(128 * c), 128)

    cols = [pl.ds(at_128(QUARTER * side), QUARTER) for side in (0, 1)]
    mine_cols = pl.ds(at_128(QUARTER * c), QUARTER)
    other_cols = pl.ds(at_128(QUARTER * other), QUARTER)
    for index, ref in enumerate((r.wq, r.wk, r.wv, r.wo)):
        r.SWAP_S[:, QUARTER * index : QUARTER * (index + 1)] = ref[:, other_cols].astype(F32)
    r.SWAP_S[:, 1536:3072] = r.wi[:, pl.ds(at_128(FF_CORE * other), FF_CORE)].astype(F32)
    swap.start(0, r.SWAP_S, r.SWAP_R, p.sibling)
    r.X[pl.ds(at_128(own_base), 128), :] = r.tok[...]

    def tok_piece(y, z, cc):
        return r.X.at[pl.ds(at_128((y * 4 + z) * CHIP_ROWS + 128 * cc), 128)]

    mine = tok_piece(p.y, p.z, c)
    for k in (2, 1, 3):
        tok.start(k - 1, mine, mine, p.device(z=p.up(k)))

    small_rows = r.WS.at[pl.ds(at_16(32 * p.chip + 16 * c), 16)]
    r.WS[pl.ds(at_16(32 * p.chip + 16 * c), 16), :] = r.small[...]
    swap.start(1, small_rows, small_rows, p.sibling)
    outer_rows = pl.ds(at_16(192 * p.chip + 96 * c), 96)
    r.WT[outer_rows, :] = r.wt[:, mine_cols]
    swap.start(2, r.wt.at[:, other_cols], r.WT.at[outer_rows], p.sibling)
    og_rows = r.OG.at[own_half]
    r.OG[own_half, :] = r.og[...]
    swap.start(3, og_rows, og_rows, p.sibling)

    gs = Gather(p, sems, r.WS, 32, "y", "x")
    ga = Gather(p, sems, r.WA, 48, "y", "x")
    gi = Gather(p, sems, r.WI, 48, "y", "x")
    gt = Gather(p, sems, r.WT, 192, "x", "y")

    swap.arrived(0)
    own_is_first = c == 0
    chip_weights = pl.ds(at_16(48 * p.chip), 48)
    for index, ref in enumerate((r.wq, r.wk, r.wv, r.wo)):
        where = slice(QUARTER * index, QUARTER * (index + 1))
        kept = ref[:, mine_cols].astype(F32)
        came = r.SWAP_R[:, where]
        both = jnp.concatenate(
            [jnp.where(own_is_first, kept, came), jnp.where(own_is_first, came, kept)], axis=0
        )
        r.WA[chip_weights, where] = both.astype(BF16)
    kept = r.wi[:, pl.ds(at_128(FF_CORE * c), FF_CORE)].astype(F32)
    came = r.SWAP_R[:, 1536:3072]
    both = jnp.concatenate(
        [jnp.where(own_is_first, kept, came), jnp.where(own_is_first, came, kept)], axis=0
    )
    r.WI[chip_weights, :] = both.astype(BF16)
    swap.arrived(1)
    ga.along_z()
    gs.along_z()

    starts, nexts = r.docs[0:1, :], r.docs[1:2, :]
    lanes = lane_iota((CHIP_ROWS, 128))
    for j in range(8):
        place = row_iota((CHIP_ROWS, 128)) + (p.x * HALF_ROWS + (j % 4) * 512 + (j // 4) * 256)
        inside = jnp.logical_and(place >= starts, place < nexts)
        rows = slice(j * CHIP_ROWS, (j + 1) * CHIP_ROWS)
        r.QE[rows, :] = jnp.where(inside, 1.0, 0.0).astype(BF16)
        r.KE[rows, :] = jnp.where(jnp.logical_or(inside, lanes >= 16), 0.0, PENALTY).astype(BF16)

    def tok_y(k):
        if k:
            tok.arrived(k - 1)
        part = tok_piece(p.y, p.down(k), c)
        tok.start(3 + k, part, part, p.side["y"])
        tok.start(7 + k, part, part, p.sibling)

    def tok_core(k):
        tok.arrived(3 + k)
        part = tok_piece(1 - p.y, p.down(k), c)
        tok.start(11 + k, part, part, p.sibling)

    tok_y(0)
    ga.forward(0)
    gs.forward(0)
    for k in (1, 2, 3):
        tok_y(k)
        ga.forward(k)
        gs.forward(k)
    for k in (0, 1, 2, 3):
        tok_core(k)
        ga.forward_again(k)
        gs.forward_again(k)
    gi.along_z()
    swap.arrived(2)
    gt.along_z()
    for k in range(4):
        gs.complete(k)
        ga.complete(k)
    for k in range(8):
        tok.arrived(7 + k)

    column = lane_iota((1, D))
    by_24, in_24 = lax.div(column, 24), lax.rem(column, 24)
    spread = jnp.where(row_iota((128, D)) == in_24, 1.0, 0.0).astype(BF16)
    spread_rows = nn(r.WS[...], spread)
    row = row_iota((512, 1))
    owner, kind = lax.shift_right_logical(row, 4), jnp.bitwise_and(row, 15)
    chosen = jnp.where(owner == by_24, spread_rows, 0.0)
    r.VEC[...] = jnp.sum(chosen.reshape(32, 16, D), axis=0)
    part_of = jnp.where(
        jnp.logical_and(kind >= 8, kind < 12), 4 * (owner - 16 * c) + kind - 8, -1000
    )
    for u in (0, 1):
        chosen = jnp.where(part_of - 32 * u == by_24, spread_rows, 0.0)
        r.BIN[0:1, D * u : D * (u + 1)] = jnp.sum(chosen, axis=0, keepdims=True)
    query_bias, value_bias = r.VEC[0:1, mine_cols], r.VEC[1:2, mine_cols]
    output_bias, first_gain, first_shift = r.VEC[2:3, :], r.VEC[3:4, :], r.VEC[4:5, :]
    outer_bias, second_gain, second_shift = r.VEC[5:6, :], r.VEC[6:7, :], r.VEC[7:8, :]

    row_set = pl.ds(at_128(QUARTER * c), QUARTER)
    other_set = pl.ds(at_128(QUARTER * other), QUARTER)
    o_cols = slice(1152, 1536)
    r.WO[:, mine_cols] = r.WA[row_set, o_cols]
    swap.start(4, r.WA.at[other_set, pl.ds(1152, QUARTER)], r.WO.at[:, mine_cols], p.sibling)

    bias = jnp.concatenate([query_bias, jnp.zeros_like(query_bias), value_bias], axis=1)

    def project(j, carry):
        rows = pl.ds(at_128(j * CHIP_ROWS), CHIP_ROWS)
        r.QKV[rows, :] = (nn(r.X[rows, :], r.WA[:, 0:1152]) + bias).astype(BF16)
        return carry

    lax.fori_loop(0, 8, project, 0)

    lanes128 = lane_iota((1, 128))
    in_head = [jnp.logical_and(lanes128 >= 64 * e, lanes128 < 64 * e + 64) for e in (0, 1)]

    def masked(value, e, scale=1.0):
        return jnp.where(in_head[e], value.astype(F32) * scale, 0.0).astype(BF16)

    def pair_cols(base, pair):
        return pl.ds(at_128(base + 128 * pair), 128)

    r.LSE[...] = jnp.zeros_like(r.LSE)
    r.DELTA[...] = jnp.zeros_like(r.DELTA)
    query_doc = r.QE[chip, :]

    def attend(pair, carry):
        queries = r.QKV[chip, pair_cols(0, pair)]
        keys = jnp.concatenate([r.QKV[:, pair_cols(QUARTER, pair)], r.KE[...]], axis=1)
        values = r.QKV[:, pair_cols(2 * QUARTER, pair)]
        outputs = []
        for e in (0, 1):
            query = jnp.concatenate([masked(queries, e, 0.125), query_doc], axis=1)
            scores = nt(query, keys)
            top = jnp.max(scores, axis=1, keepdims=True)
            weights = jnp.exp(scores - top)
            total = jnp.sum(weights, axis=1, keepdims=True)
            outputs.append(nn(weights.astype(BF16), values) / total)
            log_total = top + jnp.log(total)
            r.LSE[...] = jnp.where(lanes128 == 2 * pair + e, log_total, r.LSE[...])
        r.ATT[:, pair_cols(0, pair)] = jnp.where(in_head[0], outputs[0], outputs[1]).astype(BF16)
        return carry

    lax.fori_loop(0, 3, attend, 0)

    for k in range(4):
        gi.forward(k)
        gt.forward(k)
    for k in range(4):
        gi.forward_again(k)
        gt.forward_again(k)
    for k in range(4):
        gi.complete(k)
        gt.complete(k)
    outer_set = pl.ds(at_128(FF_CORE * c), FF_CORE)
    other_outer = pl.ds(at_128(FF_CORE * other), FF_CORE)
    swap.start(5, r.WT.at[other_outer], r.WTR.at[:, mine_cols], p.sibling)
    r.WTR[:, mine_cols] = r.WT[outer_set, :]

    swap.arrived(4)
    swap.arrived(3)

    def exchange(index, partial):
        r.PX_S[index] = partial.astype(BF16)
        swap.start(6 + index, r.PX_S.at[index], r.PX_R.at[index], p.sibling)

    branch = nn(r.ATT[...], r.WO[...])
    exchange(0, branch)
    swap.arrived(6)
    branch = branch + r.PX_R[0].astype(F32) + output_bias
    normed, first_inverse = normed_of(r.X[chip, :].astype(F32) + branch)
    r.N1[...] = normed
    hidden = normed * first_gain + first_shift
    r.HID[...] = hidden
    r.HL[...] = hidden.astype(BF16)

    swap.arrived(5)

    def inner_block(j, carry):
        where = pl.ds(at_128(j * QUARTER), QUARTER)
        value = nn(r.HL[...], r.WI[:, where]) + r.BIN[0:1, where]
        phi = 0.5 + 0.5 * lax.erf(value * (0.5**0.5))
        r.ACT[:, where] = (value * phi).astype(BF16)
        density = jnp.exp(value * value * -0.5) * 0.3989422804014327
        r.GP[:, where] = phi + value * density
        return carry

    lax.fori_loop(0, 4, inner_block, 0)

    def outer_block(j, carry):
        where = pl.ds(at_128(j * 256), 256)
        r.PART[:, where] = nn(r.ACT[...], r.WTR[:, where])
        return carry

    lax.fori_loop(0, 3, outer_block, 0)
    exchange(1, r.PART[...])
    swap.arrived(7)
    outer = r.PART[...] + r.PX_R[1].astype(F32) + outer_bias
    normed2, inverse2 = normed_of(r.HID[...] + outer)
    r.HID[...] = normed2 * second_gain + second_shift
    r.out[...] = r.HID[own_half, :].astype(BF16)
    grad_out = r.OG[...].astype(F32)
    grad_resid2 = normed_back(grad_out * second_gain, normed2, inverse2)
    r.HID[...] = grad_resid2
    grad_outer = grad_resid2.astype(BF16)
    r.GO[...] = grad_outer
    own_row = lax.shift_right_logical(row_iota((CHIP_ROWS, 1)), 7) == c

    def column_sum(value):
        return jnp.sum(jnp.where(own_row, value, 0.0), axis=0, keepdims=True)

    r.SV[...] = jnp.zeros_like(r.SV)
    r.SV[6:7, :] = column_sum(grad_out * normed2)
    r.SV[7:8, :] = column_sum(grad_out)
    r.SV[5:6, :] = column_sum(grad_outer.astype(F32))

    def inner_back(j, carry):
        where = pl.ds(at_128(j * QUARTER), QUARTER)
        grad = (nt(r.GO[...], r.WTR[where, :]) * r.GP[:, where]).astype(BF16)
        r.GIN[:, where] = grad
        r.BIN[1:2, where] = jnp.sum(grad.astype(F32), axis=0, keepdims=True)
        return carry

    lax.fori_loop(0, 4, inner_back, 0)
    for u in (0, 1):
        r.SV[pl.ds(8 + 2 * c + u, 1), :] = r.BIN[1:2, D * u : D * (u + 1)]

    def hidden_back(j, carry):
        where = pl.ds(at_128(j * 256), 256)
        r.PART[:, where] = nt(r.GIN[...], r.WI[where, :])
        return carry

    lax.fori_loop(0, 3, hidden_back, 0)
    exchange(2, r.PART[...])

    def outer_grads(j, carry):
        where = pl.ds(at_128(j * QUARTER), QUARTER)
        mine_rows = pl.ds(at_128(FF_CORE * c + j * QUARTER), QUARTER)
        r.GT_S[where, :] = tn(r.ACT[:, where], r.GO[:, other_cols]).astype(BF16)
        r.GT[mine_rows, :] = tn(r.ACT[:, where], r.GO[:, mine_cols]).astype(BF16)
        return carry

    lax.fori_loop(0, 4, outer_grads, 0)
    swap.start(10, r.GT_S, r.GT.at[outer_set], p.sibling)

    def inner_grads(j, carry):
        where = pl.ds(at_128(j * QUARTER), QUARTER)
        r.GI[:, where] = tn(r.HL[...], r.GIN[:, where]).astype(BF16)
        return carry

    lax.fori_loop(0, 4, inner_grads, 0)

    ri = Reduce(p, sems, r.GI, 48, "x", (r.GI1, r.GI2, r.GI3))
    rt = Reduce(p, sems, r.GT, 192, "y", (r.GT1, r.GT2, r.GT3))
    rw = Reduce(p, sems, r.GW, 48, "x", (r.GW1, r.GW2, r.GW3))
    ra = Reduce(p, sems, r.GA, 48, "y", (r.GA1, r.GA2, r.GA3))
    rs = Reduce(p, sems, r.SG, 32, "x", (r.SG1, r.SG2, r.SG3))

    swap.arrived(8)
    grad_hidden = r.HID[...] + r.PART[...] + r.PX_R[2].astype(F32)
    normed = r.N1[...]
    grad_resid1 = normed_back(grad_hidden * first_gain, normed, first_inverse)
    r.SV[3:4, :] = column_sum(grad_hidden * normed)
    r.SV[4:5, :] = column_sum(grad_hidden)
    r.HID[...] = grad_resid1
    grad_branch = grad_resid1.astype(BF16)
    r.GB[...] = grad_branch
    r.SV[2:3, :] = column_sum(grad_branch.astype(F32))
    grad_attended = nt(grad_branch, r.WO[...]).astype(BF16)
    r.DO[chip, :] = grad_attended
    attended = r.ATT[...].astype(F32)
    product = grad_attended.astype(F32) * attended
    for head in range(CORE_HEADS):
        pair = slice(128 * (head // 2), 128 * (head // 2) + 128)
        delta = jnp.sum(jnp.where(in_head[head % 2], product[:, pair], 0.0), axis=1, keepdims=True)
        r.DELTA[...] = jnp.where(lanes128 == head, delta, r.DELTA[...])
    chip_lanes = pl.ds(at_128(chip_base), CHIP_ROWS)
    r.STAT[0:8, chip_lanes] = jnp.transpose(r.LSE[...])[0:8, :]
    r.STAT[8:16, chip_lanes] = jnp.transpose(r.DELTA[...])[0:8, :]

    back = Mover(sems, 14)

    def back_rows(y, z):
        return r.DO.at[pl.ds(at_128((y * 4 + z) * CHIP_ROWS), CHIP_ROWS)]

    def back_stat(y, z):
        return r.STAT.at[:, pl.ds(at_128((y * 4 + z) * CHIP_ROWS), CHIP_ROWS)]

    for k in (2, 1, 3):
        back.start(k - 1, back_rows(p.y, p.z), back_rows(p.y, p.z), p.device(z=p.up(k)))
        back.start(7 + k - 1, back_stat(p.y, p.z), back_stat(p.y, p.z), p.device(z=p.up(k)))

    def back_y(k):
        if k:
            back.arrived(k - 1)
            back.arrived(7 + k - 1)
        rows, stat = back_rows(p.y, p.down(k)), back_stat(p.y, p.down(k))
        back.start(3 + k, rows, rows, p.side["y"])
        back.start(7 + 3 + k, stat, stat, p.side["y"])

    back_y(0)

    r.GW_S[...] = tn(r.ATT[...], r.GB[:, other_cols]).astype(BF16)
    r.GW[row_set, :] = tn(r.ATT[...], r.GB[:, mine_cols]).astype(BF16)
    swap.start(11, r.GW_S, r.GW.at[row_set], p.sibling)
    swap.arrived(10)
    swap.arrived(11)
    for k in (1, 2, 3, 0):
        ri.send_one(k)
        rt.send_one(k)
        rw.send_one(k)

    def query_back(pair, carry):
        queries = r.QKV[chip, pair_cols(0, pair)]
        keys = r.QKV[:, pair_cols(QUARTER, pair)]
        keys_doc = jnp.concatenate([keys, r.KE[...]], axis=1)
        values = r.QKV[:, pair_cols(2 * QUARTER, pair)]
        grads = r.DO[chip, pair_cols(0, pair)]
        outputs = []
        for e in (0, 1):
            pick = lanes128 == 2 * pair + e
            log_total = jnp.sum(jnp.where(pick, r.LSE[...], 0.0), axis=1, keepdims=True)
            delta = jnp.sum(jnp.where(pick, r.DELTA[...], 0.0), axis=1, keepdims=True)
            query = jnp.concatenate([masked(queries, e, 0.125), query_doc], axis=1)
            probs = jnp.exp(nt(query, keys_doc) - log_total)
            grad_probs = nt(masked(grads, e), values)
            grad_scores = (probs * (grad_probs - delta)).astype(BF16)
            outputs.append(nn(grad_scores, keys) * 0.125)
        r.DQKV[:, pair_cols(0, pair)] = jnp.where(in_head[0], outputs[0], outputs[1]).astype(BF16)
        return carry

    lax.fori_loop(0, 3, query_back, 0)
    for k in (1, 2, 3):
        back_y(k)
    for k in range(4):
        back.arrived(3 + k)
        back.arrived(10 + k)

    key_doc = r.KE[chip, :]

    def key_back(pair, carry):
        keys = r.QKV[chip, pair_cols(QUARTER, pair)]
        values = r.QKV[chip, pair_cols(2 * QUARTER, pair)]
        queries = r.QKV[:, pair_cols(0, pair)]
        queries_doc = jnp.concatenate([queries, r.QE[...]], axis=1)
        grads = r.DO[:, pair_cols(0, pair)]
        key_grads, value_grads = [], []
        for e in (0, 1):
            log_total = r.STAT[pl.ds(2 * pair + e, 1), :]
            delta = r.STAT[pl.ds(8 + 2 * pair + e, 1), :]
            key = jnp.concatenate([masked(keys, e, 0.125), key_doc], axis=1)
            probs = jnp.exp(nt(key, queries_doc) - log_total)
            value_grads.append(nn(probs.astype(BF16), grads))
            grad_probs = nt(masked(values, e), grads)
            grad_scores = (probs * (grad_probs - delta)).astype(BF16)
            key_grads.append(nn(grad_scores, queries) * 0.125)
        r.DQKV[:, pair_cols(QUARTER, pair)] = jnp.where(
            in_head[0], key_grads[0], key_grads[1]
        ).astype(BF16)
        r.DQKV[:, pair_cols(2 * QUARTER, pair)] = jnp.where(
            in_head[0], value_grads[0], value_grads[1]
        ).astype(BF16)
        return carry

    lax.fori_loop(0, 3, key_back, 0)

    def project_grads(j, carry):
        where = pl.ds(at_128(j * QUARTER), QUARTER)
        r.GA[:, where] = tn(r.X[chip, :], r.DQKV[:, where]).astype(BF16)
        return carry

    lax.fori_loop(0, 3, project_grads, 0)
    for k in (1, 2, 3, 0):
        ra.send_one(k)

    def tokens_back(j, carry):
        where = pl.ds(at_128(j * 256), 256)
        r.PART[:, where] = nt(r.DQKV[...], r.WA[where, 0:1152])
        return carry

    lax.fori_loop(0, 3, tokens_back, 0)
    sibling_half = pl.ds(at_128(128 * other), 128)
    r.PX_S[3, 0:128, :] = r.PART[sibling_half, :].astype(BF16)
    swap.start(9, r.PX_S.at[3, pl.ds(0, 128)], r.PX_R.at[3, pl.ds(0, 128)], p.sibling)

    r.SV[0:1, mine_cols] = jnp.sum(r.DQKV[:, 0:QUARTER].astype(F32), axis=0, keepdims=True)
    r.SV[1:2, mine_cols] = jnp.sum(r.DQKV[:, 2 * QUARTER :].astype(F32), axis=0, keepdims=True)
    by_96, in_96 = lax.div(column, 96), lax.rem(column, 96)
    gather_96 = jnp.where(row_iota((128, D)) == in_96, 1.0, 0.0).astype(BF16)
    sums = jnp.broadcast_to(r.SV[...].reshape(1, 16, D), (32, 16, D)).reshape(512, D)
    late = kind >= 8
    wanted = jnp.where(late, 8 * (kind - 8) + by_96, by_24) == owner
    sums = jnp.where(wanted, sums, 0.0)
    high = sums.astype(BF16)
    low_part = (sums - high.astype(F32)).astype(BF16)
    r.SG[...] = jnp.where(
        late,
        nt(high, gather_96) + nt(low_part, gather_96),
        nt(high, spread) + nt(low_part, spread),
    )
    for k in (1, 2, 3, 0):
        rs.send_one(k)

    for k in (1, 2, 3, 0):
        ri.send_two(k)
        rt.send_two(k)
        rw.send_two(k)
    for k in (1, 2, 3, 0):
        ra.send_two(k)
        rs.send_two(k)
    for k in (1, 2, 3, 0):
        ri.send_three(k)
        rt.send_three(k)
        rw.send_three(k)
    for k in (1, 2, 3, 0):
        ra.send_three(k)
        rs.send_three(k)

    last = Mover(sems, 5)
    finals = (
        (ri, r.FI, r.FI_R, 24),
        (rt, r.FT, r.FT_R, 96),
        (rw, r.FW, r.FW_R, 24),
        (ra, r.FA, r.FA_R, 24),
        (rs, r.FS, r.FS_R, 16),
    )
    for index, (reduce, total, came, rows) in enumerate(finals):
        total[...] = reduce.result()
        last.start(index, total.at[pl.ds(at_8(rows * other), rows)], came, p.sibling)

    swap.arrived(9)
    r.tgrad[...] = (
        r.HID[own_half, :] + r.PART[own_half, :] + r.PX_R[3, 0:128, :].astype(F32)
    ).astype(BF16)

    kept24 = pl.ds(at_8(24 * c), 24)
    last.arrived(0)
    r.gi[:, pl.ds(at_128(FF_CORE * c), FF_CORE)] = r.FI[kept24, :]
    r.gi[:, pl.ds(at_128(FF_CORE * other), FF_CORE)] = r.FI_R[...]
    last.arrived(1)
    r.gt[:, mine_cols] = r.FT[pl.ds(at_8(96 * c), 96), :]
    r.gt[:, other_cols] = r.FT_R[...]
    last.arrived(2)
    r.go[:, mine_cols] = r.FW[kept24, :]
    r.go[:, other_cols] = r.FW_R[...]
    last.arrived(3)
    for index, ref in enumerate((r.gq, r.gk, r.gv)):
        where = slice(QUARTER * index, QUARTER * (index + 1))
        ref[:, mine_cols] = r.FA[kept24, where]
        ref[:, other_cols] = r.FA_R[:, where]
    last.arrived(4)
    totals = r.FS[pl.ds(at_8(16 * c), 16), :] + r.FS_R[...]
    inner_total = totals[8:9] + totals[9:10] + totals[10:11] + totals[11:12]
    r.gs[0:8, :] = totals[0:8]
    r.gs[8:16, :] = jnp.broadcast_to(inner_total, (8, 128))

    for mover in (swap, tok, gs, ga, gi, gt, back, ri, rt, rw, ra, rs, last):
        mover.sent()


def slice_body(
    tokens, query_weight, query_bias, key_weight, value_weight, value_bias, output_weight, output_bias,
    first_gain, first_shift, inner_weight, inner_bias, outer_weight, outer_bias, second_gain,
    second_shift, doc_starts, out_grad,
):
    vectors = jnp.stack(
        [
            query_bias, value_bias, output_bias, first_gain, first_shift, outer_bias,
            second_gain, second_shift,
        ]
        + [inner_bias[24 * part : 24 * part + 24] for part in range(4)]
    )
    small = jnp.pad(vectors, ((0, 4), (0, 104)))
    far = jnp.int32(2**30)
    pad = jnp.full((128 - doc_starts.shape[0],), far)
    starts = jnp.concatenate([doc_starts, pad])
    nexts = jnp.concatenate([doc_starts[1:], far[None], pad])
    docs = jnp.concatenate([starts[None], nexts[None], jnp.zeros((6, 128), jnp.int32)])
    shape = jax.ShapeDtypeStruct
    vmem = pl.BlockSpec(memory_space=pltpu.VMEM)
    out_shapes = (
        shape((128, D), BF16), shape((128, D), BF16), shape((24, D), F32), shape((24, D), F32),
        shape((24, D), F32), shape((24, D), F32), shape((24, 3072), F32), shape((96, D), F32),
        shape((16, 128), F32),
    )
    out, tgrad, gq, gk, gv, go, gi, gt, gs = pl.pallas_call(
        layer_kernel,
        out_shape=out_shapes,
        in_specs=[vmem] * 10,
        out_specs=[vmem] * 9,
        scratch_shapes=[pltpu.VMEM(*entry) for entry in SCRATCH.values()]
        + [pltpu.SemaphoreType.DMA((SEM_COUNT,)), pltpu.SemaphoreType.DMA((SEM_COUNT,))],
        compiler_params=pltpu.CompilerParams(
            collective_id=0, has_side_effects=True, vmem_limit_bytes=62 * 2**20
        ),
        name="layer",
    )(
        tokens, out_grad, query_weight, key_weight, value_weight, output_weight, inner_weight,
        outer_weight, small, docs,
    )
    v = lambda row: gs[row, :24]
    return (
        out, tgrad, gq, v(0), gk, gv, v(1), go, v(2), v(3), v(4), gi, gs[8, :96], gt, v(5), v(6), v(7)
    )


def solution(mesh):
    rows, flat = P(("head", "blk"), None), P(("head", "blk"))
    in_specs = (
        rows, rows, flat, rows, rows, flat, rows, flat, flat, flat, rows, flat, rows, flat, flat, flat,
        P(), rows,
    )
    out_specs = (
        rows, rows, rows, flat, rows, rows, flat, rows, flat, flat, flat, rows, flat, rows, flat, flat,
        flat,
    )
    small_slice = mesh.shape["head"] == 2 and mesh.shape["blk"] == 16
    return jax.shard_map(
        slice_body if small_slice else body,
        mesh=mesh,
        in_specs=in_specs,
        out_specs=out_specs,
        check_vma=False,
    )
```

```python
from functools import partial

import jax
import jax.numpy as jnp
from jax import lax
from jax.experimental import pallas as pl
from jax.experimental.pallas import tpu as pltpu
from jax.sharding import PartitionSpec as P

HEAD_DIM = 64


LN_EPS = 1e-12
MASKED_SCORE = -1e30


def doc_numbers(doc_starts, positions):
    covered = (doc_starts[None, :] <= positions[:, None]).astype(jnp.int32)
    return (jnp.sum(covered, axis=1) - 1).astype(jnp.float32)


def dense_product(left_side, right_side):
    return jnp.dot(left_side, right_side, preferred_element_type=jnp.float32)


def product_back(left_side, right_side):
    return lax.dot_general(
        left_side, right_side, (((1,), (1,)), ((), ())), preferred_element_type=jnp.float32
    )


def product_left(left_side, right_side):
    return lax.dot_general(
        left_side, right_side, (((0,), (0,)), ((), ())), preferred_element_type=jnp.float32
    )


def norm_forward(residual, scale_gain, shift_bias):
    row_mean = jnp.mean(residual, axis=-1, keepdims=True)
    centred = residual - row_mean
    variance = jnp.mean(centred * centred, axis=-1, keepdims=True)
    inverse = lax.rsqrt(variance + LN_EPS)
    normed = centred * inverse
    return (normed * scale_gain + shift_bias, normed, inverse)


def norm_backward(grad_output, normed, inverse, scale_gain):
    grad_normed = grad_output * scale_gain
    first_term = jnp.mean(grad_normed, axis=-1, keepdims=True)
    second_term = jnp.mean(grad_normed * normed, axis=-1, keepdims=True)
    grad_input = inverse * (grad_normed - first_term - normed * second_term)
    return (grad_input, jnp.sum(grad_output * normed, axis=0), jnp.sum(grad_output, axis=0))


def split_blocks(rows_array, block_rows):
    return rows_array.reshape(-1, block_rows, rows_array.shape[1] // HEAD_DIM, HEAD_DIM)


def blocks_to_rows(blocked):
    reordered = jnp.transpose(blocked, (0, 2, 1, 3))
    return reordered.reshape(-1, blocked.shape[1] * blocked.shape[3])


def block_scores(query_block, key_block, query_docs, key_docs):
    scores = jnp.einsum(
        "qhd,khd->hqk", query_block, key_block, preferred_element_type=jnp.float32
    ) * HEAD_DIM ** (-0.5)
    allowed = (query_docs[:, None] == key_docs[None, :])[None, :, :]
    return (scores, allowed)


def intersecting(first_docs, second_docs):
    return jnp.logical_and(
        jnp.max(first_docs) >= jnp.min(second_docs), jnp.min(first_docs) <= jnp.max(second_docs)
    )


def keep_state(carried):
    return carried


def forward_update(carried, query_block, query_docs, key_block, value_block, key_docs):
    running_max, row_total, accumulated = carried
    scores, allowed = block_scores(query_block, key_block, query_docs, key_docs)
    scores = jnp.where(allowed, scores, MASKED_SCORE)
    new_max = jnp.maximum(running_max, jnp.max(scores, axis=2))
    decay_factor = jnp.exp(running_max - new_max)
    weights = jnp.where(allowed, jnp.exp(scores - new_max[:, :, None]), 0.0)
    row_total = row_total * decay_factor + jnp.sum(weights, axis=2)
    update = jnp.einsum(
        "hqk,khd->hqd",
        weights.astype(jnp.bfloat16),
        value_block,
        preferred_element_type=jnp.float32,
    )
    return (new_max, row_total, accumulated * decay_factor[:, :, None] + update)


def forward_folder(query_blocks, doc_blocks):
    block_rows = query_blocks.shape[1]

    def forward_fold_step(carried_in, pieces, start_row):
        key_piece, value_piece, key_doc_piece = pieces
        key_blocks = split_blocks(key_piece, block_rows)
        value_blocks = split_blocks(value_piece, block_rows)
        key_doc_blocks = key_doc_piece.astype(jnp.float32).reshape(-1, block_rows)

        def forward_one_block(block_index, carried):
            key_docs = key_doc_blocks[block_index]
            results = []
            for query_index in range(query_blocks.shape[0]):
                current = tuple((member[query_index] for member in carried))
                update = partial(
                    forward_update,
                    query_block=query_blocks[query_index],
                    query_docs=doc_blocks[query_index],
                    key_block=key_blocks[block_index],
                    value_block=value_blocks[block_index],
                    key_docs=key_docs,
                )
                results.append(
                    lax.cond(
                        intersecting(doc_blocks[query_index], key_docs), update, keep_state, current
                    )
                )
            return tuple((jnp.stack([entry[member] for entry in results]) for member in range(3)))

        return lax.fori_loop(0, key_blocks.shape[0], forward_one_block, carried_in)

    return forward_fold_step


def query_grad_update(
    grad_query,
    query_block,
    query_docs,
    grad_block,
    log_total,
    delta_rows,
    key_block,
    value_block,
    key_docs,
):
    scores, allowed = block_scores(query_block, key_block, query_docs, key_docs)
    probs = jnp.where(allowed, jnp.exp(scores - log_total[:, :, None]), 0.0)
    grad_probs = jnp.einsum(
        "qhd,khd->hqk", grad_block, value_block, preferred_element_type=jnp.float32
    )
    grad_scores = (probs * (grad_probs - delta_rows[:, :, None])).astype(jnp.bfloat16)
    return grad_query + jnp.einsum(
        "hqk,khd->hqd", grad_scores, key_block, preferred_element_type=jnp.float32
    ) * HEAD_DIM ** (-0.5)


def query_grad_folder(query_blocks, doc_blocks, grad_blocks, log_blocks, delta_blocks):
    block_rows = query_blocks.shape[1]

    def query_fold_step(carried_in, pieces, start_row):
        key_piece, value_piece, key_doc_piece = pieces
        key_blocks = split_blocks(key_piece, block_rows)
        value_blocks = split_blocks(value_piece, block_rows)
        key_doc_blocks = key_doc_piece.astype(jnp.float32).reshape(-1, block_rows)

        def query_one_block(block_index, carried):
            key_docs = key_doc_blocks[block_index]
            results = []
            for query_index in range(query_blocks.shape[0]):
                update = partial(
                    query_grad_update,
                    query_block=query_blocks[query_index],
                    query_docs=doc_blocks[query_index],
                    grad_block=grad_blocks[query_index],
                    log_total=log_blocks[query_index],
                    delta_rows=delta_blocks[query_index],
                    key_block=key_blocks[block_index],
                    value_block=value_blocks[block_index],
                    key_docs=key_docs,
                )
                results.append(
                    lax.cond(
                        intersecting(doc_blocks[query_index], key_docs),
                        update,
                        keep_state,
                        carried[query_index],
                    )
                )
            return jnp.stack(results)

        return lax.fori_loop(0, key_blocks.shape[0], query_one_block, carried_in)

    return query_fold_step


def key_grad_update(
    carried,
    key_block,
    value_block,
    key_docs,
    query_block,
    grad_block,
    log_total,
    delta_rows,
    query_docs,
):
    grad_key, grad_value = carried
    scores, allowed = block_scores(query_block, key_block, query_docs, key_docs)
    probs = jnp.where(allowed, jnp.exp(scores - log_total[:, :, None]), 0.0)
    grad_value = grad_value + jnp.einsum(
        "hqk,qhd->hkd", probs.astype(jnp.bfloat16), grad_block, preferred_element_type=jnp.float32
    )
    grad_probs = jnp.einsum(
        "qhd,khd->hqk", grad_block, value_block, preferred_element_type=jnp.float32
    )
    grad_scores = (probs * (grad_probs - delta_rows[:, :, None])).astype(jnp.bfloat16)
    grad_key = grad_key + jnp.einsum(
        "hqk,qhd->hkd", grad_scores, query_block, preferred_element_type=jnp.float32
    ) * HEAD_DIM ** (-0.5)
    return (grad_key, grad_value)


def key_grad_folder(key_blocks, value_blocks, doc_blocks):
    block_rows = key_blocks.shape[1]

    def key_fold_step(carried_in, pieces, start_row):
        query_piece, grad_piece, log_piece, delta_piece, doc_piece = pieces
        query_blocks = split_blocks(query_piece.astype(jnp.bfloat16), block_rows)
        grad_blocks = split_blocks(grad_piece.astype(jnp.bfloat16), block_rows)
        log_blocks = jnp.transpose(log_piece.reshape(-1, block_rows, log_piece.shape[1]), (0, 2, 1))
        delta_blocks = jnp.transpose(
            delta_piece.reshape(-1, block_rows, delta_piece.shape[1]), (0, 2, 1)
        )
        query_doc_blocks = doc_piece.reshape(-1, block_rows)

        def key_one_block(block_index, carried):
            query_docs = query_doc_blocks[block_index]
            results = []
            for key_index in range(key_blocks.shape[0]):
                current = (carried[0][key_index], carried[1][key_index])
                update = partial(
                    key_grad_update,
                    key_block=key_blocks[key_index],
                    value_block=value_blocks[key_index],
                    key_docs=doc_blocks[key_index],
                    query_block=query_blocks[block_index],
                    grad_block=grad_blocks[block_index],
                    log_total=log_blocks[block_index],
                    delta_rows=delta_blocks[block_index],
                    query_docs=query_docs,
                )
                results.append(
                    lax.cond(
                        intersecting(query_docs, doc_blocks[key_index]), update, keep_state, current
                    )
                )
            return (
                jnp.stack([entry[0] for entry in results]),
                jnp.stack([entry[1] for entry in results]),
            )

        return lax.fori_loop(0, query_blocks.shape[0], key_one_block, carried_in)

    return key_fold_step


def attention_forward(query_rows, key_rows, value_rows, row_docs, block_rows):
    query_blocks = split_blocks(query_rows, block_rows)
    doc_blocks = row_docs.reshape(-1, block_rows)
    block_count = query_blocks.shape[0]
    head_count = query_blocks.shape[2]
    send_docs = row_docs.astype(jnp.bfloat16)
    start_state = (
        jnp.full((block_count, head_count, block_rows), MASKED_SCORE, jnp.float32),
        jnp.zeros((block_count, head_count, block_rows), jnp.float32),
        jnp.zeros((block_count, head_count, block_rows, HEAD_DIM), jnp.float32),
    )
    fold_forward = forward_folder(query_blocks, doc_blocks)
    running_max, row_total, accumulated = fold_forward(
        start_state,
        (
            lax.all_gather(key_rows, "blk", axis=0, tiled=True),
            lax.all_gather(value_rows, "blk", axis=0, tiled=True),
            lax.all_gather(send_docs, "blk", axis=0, tiled=True),
        ),
        jnp.int32(0),
    )
    head_outputs = blocks_to_rows(accumulated / row_total[:, :, :, None]).astype(jnp.bfloat16)
    log_total = running_max + jnp.log(row_total)
    return (head_outputs, log_total)


def attention_backward(
    grad_rows, head_outputs, log_total, query_rows, key_rows, value_rows, row_docs, block_rows
):
    query_blocks = split_blocks(query_rows, block_rows)
    key_blocks = split_blocks(key_rows, block_rows)
    value_blocks = split_blocks(value_rows, block_rows)
    doc_blocks = row_docs.reshape(-1, block_rows)
    block_count = query_blocks.shape[0]
    head_count = query_blocks.shape[2]
    send_docs = row_docs.astype(jnp.bfloat16)
    grad_blocks = split_blocks(grad_rows, block_rows)
    output_blocks = split_blocks(head_outputs, block_rows)
    delta_blocks = jnp.einsum(
        "nqhd,nqhd->nhq", grad_blocks.astype(jnp.float32), output_blocks.astype(jnp.float32)
    )
    log_rows = jnp.transpose(log_total, (0, 2, 1)).reshape(-1, head_count)
    delta_rows = jnp.transpose(delta_blocks, (0, 2, 1)).reshape(-1, head_count)
    fold_queries = query_grad_folder(query_blocks, doc_blocks, grad_blocks, log_total, delta_blocks)
    fold_keys = key_grad_folder(key_blocks, value_blocks, doc_blocks)
    query_start = jnp.zeros((block_count, head_count, block_rows, HEAD_DIM), jnp.float32)
    key_start = (query_start, query_start)
    query_send = (
        query_rows.astype(jnp.float32),
        grad_rows.astype(jnp.float32),
        log_rows,
        delta_rows,
        row_docs,
    )
    grad_query_state = fold_queries(
        query_start,
        (
            lax.all_gather(key_rows, "blk", axis=0, tiled=True),
            lax.all_gather(value_rows, "blk", axis=0, tiled=True),
            lax.all_gather(send_docs, "blk", axis=0, tiled=True),
        ),
        jnp.int32(0),
    )
    grad_key_state, grad_value_state = fold_keys(
        key_start,
        (
            lax.all_gather(query_send[0], "blk", axis=0, tiled=True),
            lax.all_gather(query_send[1], "blk", axis=0, tiled=True),
            lax.all_gather(query_send[2], "blk", axis=0, tiled=True),
            lax.all_gather(query_send[3], "blk", axis=0, tiled=True),
            lax.all_gather(query_send[4], "blk", axis=0, tiled=True),
        ),
        jnp.int32(0),
    )
    return (
        blocks_to_rows(grad_query_state).astype(jnp.bfloat16),
        blocks_to_rows(grad_key_state).astype(jnp.bfloat16),
        blocks_to_rows(grad_value_state).astype(jnp.bfloat16),
    )


def data_layer(tokens, full, row_docs, out_grad, block_rows):
    (
        full_query,
        full_query_bias,
        full_key,
        full_value,
        full_value_bias,
        full_output,
        full_output_bias,
        full_first_gain,
        full_first_shift,
        full_inner,
        full_inner_bias,
        full_outer,
        full_outer_bias,
        full_second_gain,
        full_second_shift,
    ) = full
    queries = (dense_product(tokens, full_query) + full_query_bias.astype(jnp.float32)).astype(
        jnp.bfloat16
    )
    keys_local = dense_product(tokens, full_key).astype(jnp.bfloat16)
    values_local = (dense_product(tokens, full_value) + full_value_bias.astype(jnp.float32)).astype(
        jnp.bfloat16
    )
    query_rows, key_rows, value_rows = (
        lax.all_to_all(queries, "head", split_axis=1, concat_axis=0, tiled=True),
        lax.all_to_all(keys_local, "head", split_axis=1, concat_axis=0, tiled=True),
        lax.all_to_all(values_local, "head", split_axis=1, concat_axis=0, tiled=True),
    )
    head_outputs, log_total = attention_forward(
        query_rows, key_rows, value_rows, row_docs, block_rows
    )
    attended = lax.all_to_all(head_outputs, "head", split_axis=0, concat_axis=1, tiled=True)
    branch = dense_product(attended, full_output) + full_output_bias.astype(jnp.float32)
    hidden, first_normed, first_inverse = norm_forward(
        tokens.astype(jnp.float32) + branch,
        full_first_gain.astype(jnp.float32),
        full_first_shift.astype(jnp.float32),
    )
    hidden_low = hidden.astype(jnp.bfloat16)
    inner_value = dense_product(hidden_low, full_inner) + full_inner_bias.astype(jnp.float32)
    activated_full, gelu_pullback = jax.vjp(partial(jax.nn.gelu, approximate=False), inner_value)
    activated = activated_full.astype(jnp.bfloat16)
    outer_value = dense_product(activated, full_outer) + full_outer_bias.astype(jnp.float32)
    layer_full, second_normed, second_inverse = norm_forward(
        hidden + outer_value,
        full_second_gain.astype(jnp.float32),
        full_second_shift.astype(jnp.float32),
    )
    layer_out = layer_full.astype(jnp.bfloat16)
    grad_output = out_grad.astype(jnp.float32)
    grad_resid2, second_gain_term, second_shift_term = norm_backward(
        grad_output, second_normed, second_inverse, full_second_gain.astype(jnp.float32)
    )
    grad_outer = grad_resid2.astype(jnp.bfloat16)
    outer_weight_term = product_left(activated, grad_outer)
    outer_bias_term = jnp.sum(grad_outer.astype(jnp.float32), axis=0)
    grad_inner = gelu_pullback(product_back(grad_outer, full_outer))[0].astype(jnp.bfloat16)
    inner_weight_term = product_left(hidden_low, grad_inner)
    inner_bias_term = jnp.sum(grad_inner.astype(jnp.float32), axis=0)
    grad_hidden = grad_resid2 + product_back(grad_inner, full_inner)
    grad_resid1, first_gain_term, first_shift_term = norm_backward(
        grad_hidden, first_normed, first_inverse, full_first_gain.astype(jnp.float32)
    )
    grad_branch = grad_resid1.astype(jnp.bfloat16)
    output_weight_term = product_left(attended, grad_branch)
    output_bias_term = jnp.sum(grad_branch.astype(jnp.float32), axis=0)
    grad_attended = product_back(grad_branch, full_output).astype(jnp.bfloat16)
    grad_rows = lax.all_to_all(grad_attended, "head", split_axis=1, concat_axis=0, tiled=True)
    grad_query_rows, grad_key_rows, grad_value_rows = attention_backward(
        grad_rows, head_outputs, log_total, query_rows, key_rows, value_rows, row_docs, block_rows
    )
    grad_queries, grad_keys, grad_values = (
        lax.all_to_all(grad_query_rows, "head", split_axis=0, concat_axis=1, tiled=True),
        lax.all_to_all(grad_key_rows, "head", split_axis=0, concat_axis=1, tiled=True),
        lax.all_to_all(grad_value_rows, "head", split_axis=0, concat_axis=1, tiled=True),
    )
    query_weight_term = product_left(tokens, grad_queries)
    query_bias_term = jnp.sum(grad_queries.astype(jnp.float32), axis=0)
    key_weight_term = product_left(tokens, grad_keys)
    value_weight_term = product_left(tokens, grad_values)
    value_bias_term = jnp.sum(grad_values.astype(jnp.float32), axis=0)
    tokens_grad = (
        grad_resid1
        + product_back(grad_queries, full_query)
        + product_back(grad_keys, full_key)
        + product_back(grad_values, full_value)
    ).astype(jnp.bfloat16)
    summed = (
        lax.psum_scatter(query_weight_term, ("head", "blk"), scatter_dimension=0, tiled=True),
        lax.psum_scatter(query_bias_term, ("head", "blk"), scatter_dimension=0, tiled=True),
        lax.psum_scatter(key_weight_term, ("head", "blk"), scatter_dimension=0, tiled=True),
        lax.psum_scatter(value_weight_term, ("head", "blk"), scatter_dimension=0, tiled=True),
        lax.psum_scatter(value_bias_term, ("head", "blk"), scatter_dimension=0, tiled=True),
        lax.psum_scatter(output_weight_term, ("head", "blk"), scatter_dimension=0, tiled=True),
        lax.psum_scatter(output_bias_term, ("head", "blk"), scatter_dimension=0, tiled=True),
        lax.psum_scatter(first_gain_term, ("head", "blk"), scatter_dimension=0, tiled=True),
        lax.psum_scatter(first_shift_term, ("head", "blk"), scatter_dimension=0, tiled=True),
        lax.psum_scatter(inner_weight_term, ("head", "blk"), scatter_dimension=0, tiled=True),
        lax.psum_scatter(inner_bias_term, ("head", "blk"), scatter_dimension=0, tiled=True),
        lax.psum_scatter(outer_weight_term, ("head", "blk"), scatter_dimension=0, tiled=True),
        lax.psum_scatter(outer_bias_term, ("head", "blk"), scatter_dimension=0, tiled=True),
        lax.psum_scatter(second_gain_term, ("head", "blk"), scatter_dimension=0, tiled=True),
        lax.psum_scatter(second_shift_term, ("head", "blk"), scatter_dimension=0, tiled=True),
    )
    return (layer_out, tokens_grad) + tuple(summed)


def body(
    tokens,
    query_weight,
    query_bias,
    key_weight,
    value_weight,
    value_bias,
    output_weight,
    output_bias,
    first_gain,
    first_shift,
    inner_weight,
    inner_bias,
    outer_weight,
    outer_bias,
    second_gain,
    second_shift,
    doc_starts,
    out_grad,
):
    shards = (
        query_weight,
        query_bias,
        key_weight,
        value_weight,
        value_bias,
        output_weight,
        output_bias,
        first_gain,
        first_shift,
        inner_weight,
        inner_bias,
        outer_weight,
        outer_bias,
        second_gain,
        second_shift,
    )
    full = (
        lax.all_gather(shards[0], ("head", "blk"), axis=0, tiled=True),
        lax.all_gather(shards[1], ("head", "blk"), axis=0, tiled=True),
        lax.all_gather(shards[2], ("head", "blk"), axis=0, tiled=True),
        lax.all_gather(shards[3], ("head", "blk"), axis=0, tiled=True),
        lax.all_gather(shards[4], ("head", "blk"), axis=0, tiled=True),
        lax.all_gather(shards[5], ("head", "blk"), axis=0, tiled=True),
        lax.all_gather(shards[6], ("head", "blk"), axis=0, tiled=True),
        lax.all_gather(shards[7], ("head", "blk"), axis=0, tiled=True),
        lax.all_gather(shards[8], ("head", "blk"), axis=0, tiled=True),
        lax.all_gather(shards[9], ("head", "blk"), axis=0, tiled=True),
        lax.all_gather(shards[10], ("head", "blk"), axis=0, tiled=True),
        lax.all_gather(shards[11], ("head", "blk"), axis=0, tiled=True),
        lax.all_gather(shards[12], ("head", "blk"), axis=0, tiled=True),
        lax.all_gather(shards[13], ("head", "blk"), axis=0, tiled=True),
        lax.all_gather(shards[14], ("head", "blk"), axis=0, tiled=True),
    )
    tok_rows = tokens.shape[0]
    half_length = tok_rows * lax.axis_size("blk")
    blk_place = lax.axis_index("blk")
    offsets = jnp.arange(tok_rows, dtype=jnp.int32)
    row_positions = jnp.concatenate(
        [blk_place * tok_rows + offsets, half_length + blk_place * tok_rows + offsets]
    )
    row_docs = doc_numbers(doc_starts, row_positions)
    return data_layer(tokens, full, row_docs, out_grad, tok_rows)


MESH = pl.DeviceIdType.MESH
F32 = jnp.float32
BF16 = jnp.bfloat16
D = 768
QUARTER = 384
FF_CORE = 1536
HALF_ROWS = 2048
CHIP_ROWS = 256
CORE_HEADS = 6
PENALTY = -1e30


def nn(a, b):
    return lax.dot_general(a, b, (((1,), (0,)), ((), ())), preferred_element_type=F32)


def nt(a, b):
    return lax.dot_general(a, b, (((1,), (1,)), ((), ())), preferred_element_type=F32)


def tn(a, b):
    return lax.dot_general(a, b, (((0,), (0,)), ((), ())), preferred_element_type=F32)


def at_128(index):
    return pl.multiple_of(index, 128)


def at_16(index):
    return pl.multiple_of(index, 16)


def at_8(index):
    return pl.multiple_of(index, 8)


class Place:
    def __init__(self):
        self.x = lax.axis_index("head")
        b = lax.axis_index("blk")
        self.z = lax.div(b, 4)
        self.y = lax.rem(lax.div(b, 2), 2)
        self.c = lax.rem(b, 2)
        self.chip = self.x * 8 + self.z * 2 + self.y
        self.slot = self.y * 4 + self.z
        self.ups = [self.z] + [lax.rem(self.z + k, 4) for k in (1, 2, 3)]
        self.downs = [self.ups[0], self.ups[3], self.ups[2], self.ups[1]]
        self.above = self.device(z=jnp.minimum(self.z + 1, 3))
        self.below = self.device(z=jnp.maximum(self.z - 1, 0))
        self.can_up, self.can_down = self.z < 3, self.z > 0
        self.has_below = [None] + [self.z >= step for step in (1, 2, 3)]
        self.has_above = [None] + [self.z <= 3 - step for step in (1, 2, 3)]
        self.sibling = self.device(c=1 - self.c)
        self.side = {"x": self.device(x=1 - self.x), "y": self.device(y=1 - self.y)}

    def device(self, x=None, z=None, y=None, c=None):
        x = self.x if x is None else x
        z = self.z if z is None else z
        y = self.y if y is None else y
        c = self.c if c is None else c
        return (x, z * 4 + y * 2 + c)

    def up(self, k):
        return self.ups[k]

    def down(self, k):
        return self.downs[k]


class Sems:
    def __init__(self, send, recv):
        self.send, self.recv, self.used = send, recv, 0

    def take(self, count):
        first = self.used
        self.used += count
        assert self.used <= self.send.shape[0]
        return first


class Mover:
    def __init__(self, sems, count):
        self.sems, self.first, self.parts = sems, sems.take(count), {}

    def copy(self, index):
        place = self.first + index
        src, dst, device = self.parts[index]()
        return pltpu.make_async_remote_copy(
            src,
            dst,
            self.sems.send.at[place],
            self.sems.recv.at[place],
            device_id=device,
            device_id_type=MESH,
        )

    def start(self, index, part):
        self.parts[index] = part
        self.copy(index).start()

    def arrived(self, index):
        self.copy(index).wait_recv()

    def sent(self):
        for index in sorted(self.parts):
            self.copy(index).wait_send()


class Gather:
    def __init__(self, place, sems, piece, first, second=None):
        self.place, self.sems, self.piece = place, sems, piece
        self.device = {"up": place.above, "down": place.below, "first": first}
        if second is not None:
            self.device.update(second=second, across=second)
        self.slot = {kind: sems.take(4) for kind in self.device}

    def copy(self, kind, z):
        place = self.slot[kind] + z
        piece = self.piece(z, kind == "across")
        return pltpu.make_async_remote_copy(
            piece,
            piece,
            self.sems.send.at[place],
            self.sems.recv.at[place],
            device_id=self.device[kind],
            device_id_type=MESH,
        )

    def sideways(self, z):
        self.copy("first", z).start()
        if "second" in self.device:
            self.copy("second", z).start()

    def begin_z(self):
        p = self.place

        @pl.when(p.can_up)
        def _():
            self.copy("up", p.z).start()

        @pl.when(p.can_down)
        def _():
            self.copy("down", p.z).start()

    def begin(self):
        self.begin_z()
        self.sideways(self.place.z)

    def hop(self, step):
        p = self.place

        @pl.when(p.has_below[step])
        def _():
            z = p.z - step
            self.copy("up", z).wait_recv()

            @pl.when(p.can_up)
            def _():
                self.copy("up", z).start()

            self.sideways(z)

        @pl.when(p.has_above[step])
        def _():
            z = p.z + step
            self.copy("down", z).wait_recv()

            @pl.when(p.can_down)
            def _():
                self.copy("down", z).start()

            self.sideways(z)

    def across_one(self, z):
        self.copy("first", z).wait_recv()
        if "second" in self.device:
            self.copy("across", z).start()

    def across(self, step):
        p = self.place
        if step == 0:
            self.across_one(p.z)
            return

        @pl.when(p.has_below[step])
        def _():
            self.across_one(p.z - step)

        @pl.when(p.has_above[step])
        def _():
            self.across_one(p.z + step)

    def complete(self):
        for z in range(4):
            self.copy("second", z).wait_recv()
            self.copy("across", z).wait_recv()

    def sent(self):
        p = self.place
        for z in range(4):
            for kind in self.device:
                wait = self.copy(kind, z).wait_send
                if kind == "up":
                    pl.when(jnp.logical_and(p.can_up, p.z >= z))(wait)
                elif kind == "down":
                    pl.when(jnp.logical_and(p.can_down, p.z <= z))(wait)
                else:
                    wait()


class Reduce(Mover):
    def __init__(self, place, sems, ref, rows, first, slots):
        super().__init__(sems, 15)
        self.place, self.ref, self.rows, self.axis = place, ref, rows, first
        self.one, self.two, self.three = slots

    def rows_of(self, x, z, y, count=1):
        return pl.ds(at_8((x * 8 + z * 2 + y) * self.rows), count * self.rows)

    def send_one(self, k):
        p, R = self.place, self.rows
        if self.axis == "x":

            def part():
                where = self.rows_of(1 - p.x, p.up(k), 0, 2)
                return self.ref.at[where], self.one.at[k], p.side["x"]

            self.start(2 * k, part)
        else:
            for xx in (0, 1):

                def part(xx=xx):
                    where = self.rows_of(xx, p.up(k), 1 - p.y)
                    return self.ref.at[where], self.one.at[k, pl.ds(xx * R, R)], p.side["y"]

                self.start(2 * k + xx, part)

    def add(self, where, term):
        self.ref[where] = (self.ref[where].astype(F32) + term.astype(F32)).astype(self.ref.dtype)

    def send_two(self, k):
        p, R = self.place, self.rows
        if self.axis == "x":
            self.arrived(2 * k)
            self.add(self.rows_of(p.x, p.up(k), 0, 2), self.one[k])

            def part():
                where = self.rows_of(p.x, p.up(k), 1 - p.y)
                return self.ref.at[where], self.two.at[k], p.side["y"]

        else:
            for xx in (0, 1):
                self.arrived(2 * k + xx)
                self.add(self.rows_of(xx, p.up(k), p.y), self.one[k, xx * R : (xx + 1) * R])

            def part():
                where = self.rows_of(1 - p.x, p.up(k), p.y)
                return self.ref.at[where], self.two.at[k], p.side["x"]

        self.start(8 + k, part)

    def send_three(self, k):
        p = self.place
        self.arrived(8 + k)
        if k:
            self.add(self.rows_of(p.x, p.up(k), p.y), self.two[k])

            def part():
                where = self.rows_of(p.x, p.up(k), p.y)
                return self.ref.at[where], self.three.at[k - 1], p.device(z=p.up(k))

            self.start(12 + k - 1, part)

    def result(self):
        p = self.place
        total = self.ref[self.rows_of(p.x, p.z, p.y)].astype(F32) + self.two[0].astype(F32)
        for k in (1, 2, 3):
            self.arrived(12 + k - 1)
            total = total + self.three[k - 1].astype(F32)
        return total


def during(index, events):
    for step, event in events.items():
        pl.when(index == step)(event)


def row_mean(value):
    return jnp.sum(value, axis=1, keepdims=True) * (1.0 / D)


def normed_of(residual):
    centred = residual - row_mean(residual)
    inverse = lax.rsqrt(row_mean(centred * centred) + LN_EPS)
    return centred * inverse, inverse


def normed_back(grad_normed, normed, inverse):
    return inverse * (grad_normed - row_mean(grad_normed) - normed * row_mean(grad_normed * normed))


def lane_iota(shape):
    return lax.broadcasted_iota(jnp.int32, shape, len(shape) - 1)


def row_iota(shape):
    return lax.broadcasted_iota(jnp.int32, shape, 0)


SCRATCH = dict(
    X=((HALF_ROWS, D), BF16),
    WS=((512, 128), BF16),
    WA=((D, 1536), BF16),
    WI=((D, FF_CORE), BF16),
    WT=((2 * FF_CORE, QUARTER), BF16),
    WO=((QUARTER, D), BF16),
    WTR=((FF_CORE, D), BF16),
    OG=((CHIP_ROWS, D), BF16),
    SWAP_S=((24, 3072), F32),
    SWAP_R=((24, 3072), F32),
    QKV=((HALF_ROWS, 1152), BF16),
    QE=((HALF_ROWS, 128), BF16),
    KE=((HALF_ROWS, 128), BF16),
    ATT=((CHIP_ROWS, QUARTER), BF16),
    LSE=((CHIP_ROWS, 128), F32),
    DELTA=((CHIP_ROWS, 128), F32),
    VEC=((16, D), F32),
    BIN=((8, FF_CORE), F32),
    DO=((HALF_ROWS, QUARTER), BF16),
    STAT=((16, HALF_ROWS), F32),
    PX_S=((4, CHIP_ROWS, D), BF16),
    PX_R=((4, CHIP_ROWS, D), BF16),
    PART=((CHIP_ROWS, D), F32),
    HID=((CHIP_ROWS, D), F32),
    N1=((CHIP_ROWS, D), F32),
    HL=((CHIP_ROWS, D), BF16),
    ACT=((CHIP_ROWS, FF_CORE), BF16),
    GP=((CHIP_ROWS, FF_CORE), F32),
    GIN=((CHIP_ROWS, FF_CORE), BF16),
    GO=((CHIP_ROWS, D), BF16),
    GB=((CHIP_ROWS, D), BF16),
    DQKV=((CHIP_ROWS, 1152), BF16),
    SV=((16, D), F32),
    GI=((D, FF_CORE), BF16),
    GT=((2 * FF_CORE, QUARTER), BF16),
    GT_S=((FF_CORE, QUARTER), BF16),
    GW=((D, QUARTER), BF16),
    GW_S=((QUARTER, QUARTER), BF16),
    GQ=((D, QUARTER), BF16),
    GK=((D, D), BF16),
    SG=((512, 128), F32),
    GI1=((4, 96, FF_CORE), BF16),
    GI2=((4, 48, FF_CORE), BF16),
    GI3=((3, 48, FF_CORE), BF16),
    GT1=((4, 384, QUARTER), BF16),
    GT2=((4, 192, QUARTER), BF16),
    GT3=((3, 192, QUARTER), BF16),
    GW1=((4, 96, QUARTER), BF16),
    GW2=((4, 48, QUARTER), BF16),
    GW3=((3, 48, QUARTER), BF16),
    GQ1=((4, 96, QUARTER), BF16),
    GQ2=((4, 48, QUARTER), BF16),
    GQ3=((3, 48, QUARTER), BF16),
    GK1=((4, 96, D), BF16),
    GK2=((4, 48, D), BF16),
    GK3=((3, 48, D), BF16),
    SG1=((4, 64, 128), F32),
    SG2=((4, 32, 128), F32),
    SG3=((3, 32, 128), F32),
    FI=((48, FF_CORE), F32),
    FT=((192, QUARTER), F32),
    FW=((48, QUARTER), F32),
    FQ=((48, QUARTER), F32),
    FK=((48, D), F32),
    FS=((32, 128), F32),
    FI_R=((24, FF_CORE), F32),
    FT_R=((96, QUARTER), F32),
    FW_R=((24, QUARTER), F32),
    FQ_R=((24, QUARTER), F32),
    FK_R=((24, D), F32),
    FS_R=((16, 128), F32),
)
SEM_COUNT = 250


class Refs:
    pass


def layer_kernel(*refs):
    r = Refs()
    (
        r.tok, r.og, r.wq, r.wk, r.wv, r.wo, r.wi, r.wt, r.small, r.docs,
        r.out, r.tgrad, r.gq, r.gk, r.gv, r.go, r.gi, r.gt, r.gs,
    ) = refs[:19]
    for name, ref in zip(SCRATCH, refs[19:]):
        setattr(r, name, ref)
    sems = Sems(refs[-2], refs[-1])
    p = Place()
    c, other = p.c, 1 - p.c

    barrier = pltpu.get_barrier_semaphore()
    partners = [p.sibling, p.side["x"], p.side["y"]] + [p.device(z=p.up(k)) for k in (1, 2, 3)]
    for partner in partners:
        pl.semaphore_signal(barrier, inc=1, device_id=partner, device_id_type=MESH)
    pl.semaphore_wait(barrier, len(partners))

    swap = Mover(sems, 16)
    chip_base = p.slot * CHIP_ROWS
    own_base = chip_base + 128 * c
    chip = pl.ds(at_128(chip_base), CHIP_ROWS)
    own_half = pl.ds(at_128(128 * c), 128)

    cols = [pl.ds(at_128(QUARTER * side), QUARTER) for side in (0, 1)]
    mine_cols = pl.ds(at_128(QUARTER * c), QUARTER)
    other_cols = pl.ds(at_128(QUARTER * other), QUARTER)
    for index, ref in enumerate((r.wq, r.wk, r.wv, r.wo)):
        r.SWAP_S[:, QUARTER * index : QUARTER * (index + 1)] = ref[:, other_cols].astype(F32)
    r.SWAP_S[:, 1536:3072] = r.wi[:, pl.ds(at_128(FF_CORE * other), FF_CORE)].astype(F32)
    swap.start(0, lambda: (r.SWAP_S, r.SWAP_R, p.sibling))
    r.X[pl.ds(at_128(own_base), 128), :] = r.tok[...]

    def tok_piece(z, across):
        y = 1 - p.y if across else p.y
        return r.X.at[pl.ds(at_128((y * 4 + z) * CHIP_ROWS + 128 * c), 128)]

    tok = Gather(p, sems, tok_piece, p.side["y"], p.sibling)
    tok.sideways(p.z)

    small_rows = r.WS.at[pl.ds(at_16(32 * p.chip + 16 * c), 16)]
    r.WS[pl.ds(at_16(32 * p.chip + 16 * c), 16), :] = r.small[...]
    swap.start(1, lambda: (small_rows, small_rows, p.sibling))
    outer_rows = pl.ds(at_16(192 * p.chip + 96 * c), 96)
    r.WT[outer_rows, :] = r.wt[:, mine_cols]
    swap.start(2, lambda: (r.wt.at[:, other_cols], r.WT.at[outer_rows], p.sibling))
    og_rows = r.OG.at[own_half]
    r.OG[own_half, :] = r.og[...]
    swap.start(3, lambda: (og_rows, og_rows, p.sibling))

    def weights(ref, rows, first):
        def piece(z, across):
            x, y = p.x, p.y
            if across:
                x, y = (x, 1 - y) if first == "y" else (1 - x, y)
            return ref.at[pl.ds(at_16((x * 8 + z * 2 + y) * rows), rows)]

        return Gather(p, sems, piece, p.side[first], p.side["y" if first == "x" else "x"])

    gs = weights(r.WS, 32, "y")
    ga = weights(r.WA, 48, "y")
    gi = weights(r.WI, 48, "y")
    gt = weights(r.WT, 192, "x")

    swap.arrived(0)
    own_is_first = c == 0
    chip_weights = pl.ds(at_16(48 * p.chip), 48)
    for index, ref in enumerate((r.wq, r.wk, r.wv, r.wo)):
        where = slice(QUARTER * index, QUARTER * (index + 1))
        kept = ref[:, mine_cols].astype(F32)
        came = r.SWAP_R[:, where]
        both = jnp.concatenate(
            [jnp.where(own_is_first, kept, came), jnp.where(own_is_first, came, kept)], axis=0
        )
        r.WA[chip_weights, where] = both.astype(BF16)
    swap.arrived(1)
    ga.begin()
    gs.begin()
    tok.begin_z()
    kept = r.wi[:, pl.ds(at_128(FF_CORE * c), FF_CORE)].astype(F32)
    came = r.SWAP_R[:, 1536:3072]
    both = jnp.concatenate(
        [jnp.where(own_is_first, kept, came), jnp.where(own_is_first, came, kept)], axis=0
    )
    r.WI[chip_weights, :] = both.astype(BF16)
    gi.sideways(p.z)
    swap.arrived(2)
    gt.sideways(p.z)

    starts, nexts = r.docs[0:1, :], r.docs[1:2, :]
    lanes = lane_iota((CHIP_ROWS, 128))
    for j in range(8):
        place = row_iota((CHIP_ROWS, 128)) + (p.x * HALF_ROWS + (j % 4) * 512 + (j // 4) * 256)
        inside = jnp.logical_and(place >= starts, place < nexts)
        rows = slice(j * CHIP_ROWS, (j + 1) * CHIP_ROWS)
        r.QE[rows, :] = jnp.where(inside, 1.0, 0.0).astype(BF16)
        r.KE[rows, :] = jnp.where(jnp.logical_or(inside, lanes >= 16), 0.0, PENALTY).astype(BF16)

    ga.hop(1)
    gs.hop(1)
    tok.hop(1)
    ga.hop(2)
    gs.hop(2)
    gi.begin_z()
    tok.hop(2)
    for gather in (ga, gs, tok):
        gather.across(0)
    ga.hop(3)
    gs.hop(3)
    gt.begin_z()
    tok.hop(3)
    gi.hop(1)
    for gather in (ga, gs, tok):
        gather.across(1)
    gt.hop(1)
    for gather in (ga, gs, tok):
        gather.across(2)
    gi.hop(2)
    for gather in (ga, gs, tok):
        gather.across(3)
    gs.complete()
    ga.complete()

    column = lane_iota((1, D))
    by_24, in_24 = lax.div(column, 24), lax.rem(column, 24)
    spread = jnp.where(row_iota((128, D)) == in_24, 1.0, 0.0).astype(BF16)
    spread_rows = nn(r.WS[...], spread)
    row = row_iota((512, 1))
    owner, kind = lax.shift_right_logical(row, 4), jnp.bitwise_and(row, 15)
    chosen = jnp.where(owner == by_24, spread_rows, 0.0)
    r.VEC[...] = jnp.sum(chosen.reshape(32, 16, D), axis=0)
    part_of = jnp.where(
        jnp.logical_and(kind >= 8, kind < 12), 4 * (owner - 16 * c) + kind - 8, -1000
    )
    for u in (0, 1):
        chosen = jnp.where(part_of - 32 * u == by_24, spread_rows, 0.0)
        r.BIN[0:1, D * u : D * (u + 1)] = jnp.sum(chosen, axis=0, keepdims=True)
    query_bias, value_bias = r.VEC[0:1, mine_cols], r.VEC[1:2, mine_cols]
    output_bias, first_gain, first_shift = r.VEC[2:3, :], r.VEC[3:4, :], r.VEC[4:5, :]
    outer_bias, second_gain, second_shift = r.VEC[5:6, :], r.VEC[6:7, :], r.VEC[7:8, :]

    row_set = pl.ds(at_128(QUARTER * c), QUARTER)
    other_set = pl.ds(at_128(QUARTER * other), QUARTER)
    o_cols = slice(1152, 1536)
    r.WO[:, mine_cols] = r.WA[row_set, o_cols]
    swap.start(4, lambda: (r.WA.at[other_set, pl.ds(1152, QUARTER)], r.WO.at[:, mine_cols], p.sibling))

    tok.complete()
    bias = jnp.concatenate([query_bias, jnp.zeros_like(query_bias), value_bias], axis=1)

    def project(j, carry):
        during(
            j,
            {
                1: lambda: gt.hop(2),
                3: lambda: gi.hop(3),
                5: lambda: gt.hop(3),
                6: lambda: gi.across(0),
                7: lambda: gt.across(0),
            },
        )
        rows = pl.ds(at_128(j * CHIP_ROWS), CHIP_ROWS)
        r.QKV[rows, :] = (nn(r.X[rows, :], r.WA[:, 0:1152]) + bias).astype(BF16)
        return carry

    lax.fori_loop(0, 8, project, 0)

    lanes128 = lane_iota((1, 128))
    in_head = [jnp.logical_and(lanes128 >= 64 * e, lanes128 < 64 * e + 64) for e in (0, 1)]

    def masked(value, e, scale=1.0):
        return jnp.where(in_head[e], value.astype(F32) * scale, 0.0).astype(BF16)

    def pair_cols(base, pair):
        return pl.ds(at_128(base + 128 * pair), 128)

    r.LSE[...] = jnp.zeros_like(r.LSE)
    r.DELTA[...] = jnp.zeros_like(r.DELTA)
    query_doc = r.QE[chip, :]

    def attend(pair, carry):
        def forward(step):
            gi.across(step)
            gt.across(step)

        during(pair, {0: lambda: forward(1), 1: lambda: forward(2)})
        queries = r.QKV[chip, pair_cols(0, pair)]
        keys = jnp.concatenate([r.QKV[:, pair_cols(QUARTER, pair)], r.KE[...]], axis=1)
        values = r.QKV[:, pair_cols(2 * QUARTER, pair)]
        outputs = []
        for e in (0, 1):
            query = jnp.concatenate([masked(queries, e, 0.125), query_doc], axis=1)
            scores = nt(query, keys)
            top = jnp.max(scores, axis=1, keepdims=True)
            weights = jnp.exp(scores - top)
            total = jnp.sum(weights, axis=1, keepdims=True)
            outputs.append(nn(weights.astype(BF16), values) / total)
            log_total = top + jnp.log(total)
            r.LSE[...] = jnp.where(lanes128 == 2 * pair + e, log_total, r.LSE[...])
        r.ATT[:, pair_cols(0, pair)] = jnp.where(in_head[0], outputs[0], outputs[1]).astype(BF16)
        return carry

    lax.fori_loop(0, 3, attend, 0)

    gi.across(3)
    gt.across(3)
    outer_set = pl.ds(at_128(FF_CORE * c), FF_CORE)
    other_outer = pl.ds(at_128(FF_CORE * other), FF_CORE)

    swap.arrived(4)
    swap.arrived(3)

    def exchange(index, partial):
        r.PX_S[index] = partial.astype(BF16)
        swap.start(6 + index, lambda: (r.PX_S.at[index], r.PX_R.at[index], p.sibling))

    branch = nn(r.ATT[...], r.WO[...])
    exchange(0, branch)
    swap.arrived(6)
    branch = branch + r.PX_R[0].astype(F32) + output_bias
    normed, first_inverse = normed_of(r.X[chip, :].astype(F32) + branch)
    r.N1[...] = normed
    hidden = normed * first_gain + first_shift
    r.HID[...] = hidden
    r.HL[...] = hidden.astype(BF16)

    gi.complete()

    def inner_block(j, carry):
        where = pl.ds(at_128(j * QUARTER), QUARTER)
        value = nn(r.HL[...], r.WI[:, where]) + r.BIN[0:1, where]
        phi = 0.5 + 0.5 * lax.erf(value * (0.5**0.5))
        r.ACT[:, where] = (value * phi).astype(BF16)
        density = jnp.exp(value * value * -0.5) * 0.3989422804014327
        r.GP[:, where] = phi + value * density
        return carry

    lax.fori_loop(0, 4, inner_block, 0)

    gt.complete()
    swap.start(5, lambda: (r.WT.at[other_outer], r.WTR.at[:, mine_cols], p.sibling))
    r.WTR[:, mine_cols] = r.WT[outer_set, :]
    swap.arrived(5)

    def outer_block(j, carry):
        where = pl.ds(at_128(j * 256), 256)
        r.PART[:, where] = nn(r.ACT[...], r.WTR[:, where])
        return carry

    lax.fori_loop(0, 3, outer_block, 0)
    exchange(1, r.PART[...])
    swap.arrived(7)
    outer = r.PART[...] + r.PX_R[1].astype(F32) + outer_bias
    normed2, inverse2 = normed_of(r.HID[...] + outer)
    r.HID[...] = normed2 * second_gain + second_shift
    r.out[...] = r.HID[own_half, :].astype(BF16)
    grad_out = r.OG[...].astype(F32)
    grad_resid2 = normed_back(grad_out * second_gain, normed2, inverse2)
    r.HID[...] = grad_resid2
    grad_outer = grad_resid2.astype(BF16)
    r.GO[...] = grad_outer
    own_row = lax.shift_right_logical(row_iota((CHIP_ROWS, 1)), 7) == c

    def column_sum(value):
        return jnp.sum(jnp.where(own_row, value, 0.0), axis=0, keepdims=True)

    r.SV[...] = jnp.zeros_like(r.SV)
    r.SV[6:7, :] = column_sum(grad_out * normed2)
    r.SV[7:8, :] = column_sum(grad_out)
    r.SV[5:6, :] = column_sum(grad_outer.astype(F32))

    ri = Reduce(p, sems, r.GI, 48, "x", (r.GI1, r.GI2, r.GI3))
    rt = Reduce(p, sems, r.GT, 192, "x", (r.GT1, r.GT2, r.GT3))
    rw = Reduce(p, sems, r.GW, 48, "y", (r.GW1, r.GW2, r.GW3))
    rq = Reduce(p, sems, r.GQ, 48, "y", (r.GQ1, r.GQ2, r.GQ3))
    rk = Reduce(p, sems, r.GK, 48, "y", (r.GK1, r.GK2, r.GK3))
    rs = Reduce(p, sems, r.SG, 32, "y", (r.SG1, r.SG2, r.SG3))
    ORDER = (1, 2, 3, 0)

    def outer_grads(j, carry):
        where = pl.ds(at_128(j * QUARTER), QUARTER)
        mine_rows = pl.ds(at_128(FF_CORE * c + j * QUARTER), QUARTER)
        r.GT_S[where, :] = tn(r.ACT[:, where], r.GO[:, other_cols]).astype(BF16)
        r.GT[mine_rows, :] = tn(r.ACT[:, where], r.GO[:, mine_cols]).astype(BF16)
        return carry

    lax.fori_loop(0, 4, outer_grads, 0)
    swap.start(10, lambda: (r.GT_S, r.GT.at[outer_set], p.sibling))

    def inner_back(j, carry):
        where = pl.ds(at_128(j * QUARTER), QUARTER)
        grad = (nt(r.GO[...], r.WTR[where, :]) * r.GP[:, where]).astype(BF16)
        r.GIN[:, where] = grad
        r.BIN[1:2, where] = jnp.sum(grad.astype(F32), axis=0, keepdims=True)
        r.GI[:, where] = tn(r.HL[...], grad).astype(BF16)
        return carry

    lax.fori_loop(0, 4, inner_back, 0)
    for k in ORDER:
        ri.send_one(k)
    for u in (0, 1):
        r.SV[pl.ds(8 + 2 * c + u, 1), :] = r.BIN[1:2, D * u : D * (u + 1)]

    def hidden_back(j, carry):
        where = pl.ds(at_128(j * 256), 256)
        r.PART[:, where] = nt(r.GIN[...], r.WI[where, :])
        return carry

    lax.fori_loop(0, 3, hidden_back, 0)
    exchange(2, r.PART[...])
    swap.arrived(10)
    for k in ORDER:
        rt.send_one(k)

    swap.arrived(8)
    grad_hidden = r.HID[...] + r.PART[...] + r.PX_R[2].astype(F32)
    normed = r.N1[...]
    grad_resid1 = normed_back(grad_hidden * first_gain, normed, first_inverse)
    r.SV[3:4, :] = column_sum(grad_hidden * normed)
    r.SV[4:5, :] = column_sum(grad_hidden)
    r.HID[...] = grad_resid1
    grad_branch = grad_resid1.astype(BF16)
    r.GB[...] = grad_branch
    r.SV[2:3, :] = column_sum(grad_branch.astype(F32))
    grad_attended = nt(grad_branch, r.WO[...]).astype(BF16)
    r.DO[chip, :] = grad_attended
    attended = r.ATT[...].astype(F32)
    product = grad_attended.astype(F32) * attended
    for head in range(CORE_HEADS):
        pair = slice(128 * (head // 2), 128 * (head // 2) + 128)
        delta = jnp.sum(jnp.where(in_head[head % 2], product[:, pair], 0.0), axis=1, keepdims=True)
        r.DELTA[...] = jnp.where(lanes128 == head, delta, r.DELTA[...])
    chip_lanes = pl.ds(at_128(chip_base), CHIP_ROWS)
    r.STAT[0:8, chip_lanes] = jnp.transpose(r.LSE[...])[0:8, :]
    r.STAT[8:16, chip_lanes] = jnp.transpose(r.DELTA[...])[0:8, :]

    def back_piece(z, across):
        y = 1 - p.y if across else p.y
        return r.DO.at[pl.ds(at_128((y * 4 + z) * CHIP_ROWS), CHIP_ROWS)]

    def stat_piece(z, across):
        y = 1 - p.y if across else p.y
        return r.STAT.at[:, pl.ds(at_128((y * 4 + z) * CHIP_ROWS), CHIP_ROWS)]

    back = Gather(p, sems, back_piece, p.side["y"])
    stat = Gather(p, sems, stat_piece, p.side["y"])
    back.begin()
    stat.begin()
    r.GW_S[...] = tn(r.ATT[...], r.GB[:, other_cols]).astype(BF16)
    r.GW[row_set, :] = tn(r.ATT[...], r.GB[:, mine_cols]).astype(BF16)
    swap.start(11, lambda: (r.GW_S, r.GW.at[row_set], p.sibling))

    def query_back(pair, carry):
        def second():
            back.hop(1)
            stat.hop(1)
            ri.send_two(1)

        def third():
            back.hop(2)
            stat.hop(2)

        during(pair, {1: second, 2: third})
        queries = r.QKV[chip, pair_cols(0, pair)]
        keys = r.QKV[:, pair_cols(QUARTER, pair)]
        keys_doc = jnp.concatenate([keys, r.KE[...]], axis=1)
        values = r.QKV[:, pair_cols(2 * QUARTER, pair)]
        grads = r.DO[chip, pair_cols(0, pair)]
        outputs = []
        for e in (0, 1):
            pick = lanes128 == 2 * pair + e
            log_total = jnp.sum(jnp.where(pick, r.LSE[...], 0.0), axis=1, keepdims=True)
            delta = jnp.sum(jnp.where(pick, r.DELTA[...], 0.0), axis=1, keepdims=True)
            query = jnp.concatenate([masked(queries, e, 0.125), query_doc], axis=1)
            probs = jnp.exp(nt(query, keys_doc) - log_total)
            grad_probs = nt(masked(grads, e), values)
            grad_scores = (probs * (grad_probs - delta)).astype(BF16)
            outputs.append(nn(grad_scores, keys) * 0.125)
        r.DQKV[:, pair_cols(0, pair)] = jnp.where(in_head[0], outputs[0], outputs[1]).astype(BF16)
        return carry

    lax.fori_loop(0, 3, query_back, 0)
    r.GQ[...] = tn(r.X[chip, :], r.DQKV[:, 0:QUARTER]).astype(BF16)
    swap.arrived(11)
    back.hop(3)
    stat.hop(3)
    ri.send_two(2)
    ri.send_three(1)
    for k in ORDER:
        rw.send_one(k)
        rq.send_one(k)
    ri.send_two(3)
    ri.send_three(2)
    for step in range(4):
        back.across(step)
        stat.across(step)
    ri.send_two(0)
    ri.send_three(3)

    key_doc = r.KE[chip, :]

    def key_back(pair, carry):
        def first():
            rw.send_two(1)
            rq.send_two(1)
            rw.send_two(2)
            rq.send_two(2)

        def second():
            rt.send_two(1)
            rw.send_two(3)
            rq.send_two(3)

        def third():
            ri.send_three(0)
            rw.send_two(0)
            rq.send_two(0)

        during(pair, {0: first, 1: second, 2: third})
        keys = r.QKV[chip, pair_cols(QUARTER, pair)]
        values = r.QKV[chip, pair_cols(2 * QUARTER, pair)]
        queries = r.QKV[:, pair_cols(0, pair)]
        queries_doc = jnp.concatenate([queries, r.QE[...]], axis=1)
        grads = r.DO[:, pair_cols(0, pair)]
        key_grads, value_grads = [], []
        for e in (0, 1):
            log_total = r.STAT[pl.ds(2 * pair + e, 1), :]
            delta = r.STAT[pl.ds(8 + 2 * pair + e, 1), :]
            key = jnp.concatenate([masked(keys, e, 0.125), key_doc], axis=1)
            probs = jnp.exp(nt(key, queries_doc) - log_total)
            value_grads.append(nn(probs.astype(BF16), grads))
            grad_probs = nt(masked(values, e), grads)
            grad_scores = (probs * (grad_probs - delta)).astype(BF16)
            key_grads.append(nn(grad_scores, queries) * 0.125)
        r.DQKV[:, pair_cols(QUARTER, pair)] = jnp.where(
            in_head[0], key_grads[0], key_grads[1]
        ).astype(BF16)
        r.DQKV[:, pair_cols(2 * QUARTER, pair)] = jnp.where(
            in_head[0], value_grads[0], value_grads[1]
        ).astype(BF16)
        return carry

    lax.fori_loop(0, 3, key_back, 0)

    def project_grads(j, carry):
        where = pl.ds(at_128(j * QUARTER), QUARTER)
        source = pl.ds(at_128((j + 1) * QUARTER), QUARTER)
        r.GK[:, where] = tn(r.X[chip, :], r.DQKV[:, source]).astype(BF16)
        return carry

    lax.fori_loop(0, 2, project_grads, 0)
    for k in ORDER:
        rk.send_one(k)
    rt.send_two(2)
    rt.send_three(1)

    def tokens_back(j, carry):
        where = pl.ds(at_128(j * 256), 256)
        r.PART[:, where] = nt(r.DQKV[...], r.WA[where, 0:1152])
        return carry

    lax.fori_loop(0, 3, tokens_back, 0)
    sibling_half = pl.ds(at_128(128 * other), 128)
    r.PX_S[3, 0:128, :] = r.PART[sibling_half, :].astype(BF16)
    swap.start(9, lambda: (r.PX_S.at[3, pl.ds(0, 128)], r.PX_R.at[3, pl.ds(0, 128)], p.sibling))

    r.SV[0:1, mine_cols] = jnp.sum(r.DQKV[:, 0:QUARTER].astype(F32), axis=0, keepdims=True)
    r.SV[1:2, mine_cols] = jnp.sum(r.DQKV[:, 2 * QUARTER :].astype(F32), axis=0, keepdims=True)
    by_96, in_96 = lax.div(column, 96), lax.rem(column, 96)
    gather_96 = jnp.where(row_iota((128, D)) == in_96, 1.0, 0.0).astype(BF16)
    sums = jnp.broadcast_to(r.SV[...].reshape(1, 16, D), (32, 16, D)).reshape(512, D)
    late = kind >= 8
    wanted = jnp.where(late, 8 * (kind - 8) + by_96, by_24) == owner
    sums = jnp.where(wanted, sums, 0.0)
    high = sums.astype(BF16)
    low_part = (sums - high.astype(F32)).astype(BF16)
    r.SG[...] = jnp.where(
        late,
        nt(high, gather_96) + nt(low_part, gather_96),
        nt(high, spread) + nt(low_part, spread),
    )
    for k in ORDER:
        rs.send_one(k)

    rt.send_two(3)
    rt.send_three(2)
    rt.send_two(0)
    for k in ORDER:
        rk.send_two(k)
        rs.send_two(k)
    for k in ORDER:
        rw.send_three(k)
        rq.send_three(k)
    rt.send_three(3)
    rt.send_three(0)
    for k in ORDER:
        rk.send_three(k)
        rs.send_three(k)

    last = Mover(sems, 6)
    finals = (
        (ri, r.FI, r.FI_R, 24),
        (rt, r.FT, r.FT_R, 96),
        (rw, r.FW, r.FW_R, 24),
        (rq, r.FQ, r.FQ_R, 24),
        (rk, r.FK, r.FK_R, 24),
        (rs, r.FS, r.FS_R, 16),
    )
    for index, (reduce, total, came, rows) in enumerate(finals):
        total[...] = reduce.result()

        def part(total=total, came=came, rows=rows):
            return total.at[pl.ds(at_8(rows * other), rows)], came, p.sibling

        last.start(index, part)

    swap.arrived(9)
    r.tgrad[...] = (
        r.HID[own_half, :] + r.PART[own_half, :] + r.PX_R[3, 0:128, :].astype(F32)
    ).astype(BF16)

    kept24 = pl.ds(at_8(24 * c), 24)
    last.arrived(0)
    r.gi[:, pl.ds(at_128(FF_CORE * c), FF_CORE)] = r.FI[kept24, :]
    r.gi[:, pl.ds(at_128(FF_CORE * other), FF_CORE)] = r.FI_R[...]
    last.arrived(1)
    r.gt[:, mine_cols] = r.FT[pl.ds(at_8(96 * c), 96), :]
    r.gt[:, other_cols] = r.FT_R[...]
    last.arrived(2)
    r.go[:, mine_cols] = r.FW[kept24, :]
    r.go[:, other_cols] = r.FW_R[...]
    last.arrived(3)
    r.gq[:, mine_cols] = r.FQ[kept24, :]
    r.gq[:, other_cols] = r.FQ_R[...]
    last.arrived(4)
    for index, ref in enumerate((r.gk, r.gv)):
        where = slice(QUARTER * index, QUARTER * (index + 1))
        ref[:, mine_cols] = r.FK[kept24, where]
        ref[:, other_cols] = r.FK_R[:, where]
    last.arrived(5)
    totals = r.FS[pl.ds(at_8(16 * c), 16), :] + r.FS_R[...]
    inner_total = totals[8:9] + totals[9:10] + totals[10:11] + totals[11:12]
    r.gs[0:8, :] = totals[0:8]
    r.gs[8:16, :] = jnp.broadcast_to(inner_total, (8, 128))

    for mover in (swap, tok, gs, ga, gi, gt, back, stat, ri, rt, rw, rq, rk, rs, last):
        mover.sent()


def slice_body(
    tokens, query_weight, query_bias, key_weight, value_weight, value_bias, output_weight, output_bias,
    first_gain, first_shift, inner_weight, inner_bias, outer_weight, outer_bias, second_gain,
    second_shift, doc_starts, out_grad,
):
    vectors = jnp.stack(
        [
            query_bias, value_bias, output_bias, first_gain, first_shift, outer_bias,
            second_gain, second_shift,
        ]
        + [inner_bias[24 * part : 24 * part + 24] for part in range(4)]
    )
    small = jnp.pad(vectors, ((0, 4), (0, 104)))
    far = jnp.int32(2**30)
    pad = jnp.full((128 - doc_starts.shape[0],), far)
    starts = jnp.concatenate([doc_starts, pad])
    nexts = jnp.concatenate([doc_starts[1:], far[None], pad])
    docs = jnp.concatenate([starts[None], nexts[None], jnp.zeros((6, 128), jnp.int32)])
    shape = jax.ShapeDtypeStruct
    vmem = pl.BlockSpec(memory_space=pltpu.VMEM)
    out_shapes = (
        shape((128, D), BF16), shape((128, D), BF16), shape((24, D), F32), shape((24, D), F32),
        shape((24, D), F32), shape((24, D), F32), shape((24, 3072), F32), shape((96, D), F32),
        shape((16, 128), F32),
    )
    out, tgrad, gq, gk, gv, go, gi, gt, gs = pl.pallas_call(
        layer_kernel,
        out_shape=out_shapes,
        in_specs=[vmem] * 10,
        out_specs=[vmem] * 9,
        scratch_shapes=[pltpu.VMEM(*entry) for entry in SCRATCH.values()]
        + [pltpu.SemaphoreType.DMA((SEM_COUNT,)), pltpu.SemaphoreType.DMA((SEM_COUNT,))],
        compiler_params=pltpu.CompilerParams(
            collective_id=0, has_side_effects=True, vmem_limit_bytes=62 * 2**20
        ),
        name="layer",
    )(
        tokens, out_grad, query_weight, key_weight, value_weight, output_weight, inner_weight,
        outer_weight, small, docs,
    )
    v = lambda row: gs[row, :24]
    return (
        out, tgrad, gq, v(0), gk, gv, v(1), go, v(2), v(3), v(4), gi, gs[8, :96], gt, v(5), v(6), v(7)
    )


def solution(mesh):
    rows, flat = P(("head", "blk"), None), P(("head", "blk"))
    in_specs = (
        rows, rows, flat, rows, rows, flat, rows, flat, flat, flat, rows, flat, rows, flat, flat, flat,
        P(), rows,
    )
    out_specs = (
        rows, rows, rows, flat, rows, rows, flat, rows, flat, flat, flat, rows, flat, rows, flat, flat,
        flat,
    )
    small_slice = mesh.shape["head"] == 2 and mesh.shape["blk"] == 16
    return jax.shard_map(
        slice_body if small_slice else body,
        mesh=mesh,
        in_specs=in_specs,
        out_specs=out_specs,
        check_vma=False,
    )
```

```python
from functools import partial

import jax
import jax.numpy as jnp
from jax import lax
from jax.experimental import pallas as pl
from jax.experimental.pallas import tpu as pltpu
from jax.sharding import PartitionSpec as P

HEAD_DIM = 64


LN_EPS = 1e-12
MASKED_SCORE = -1e30


def doc_numbers(doc_starts, positions):
    covered = (doc_starts[None, :] <= positions[:, None]).astype(jnp.int32)
    return (jnp.sum(covered, axis=1) - 1).astype(jnp.float32)


def dense_product(left_side, right_side):
    return jnp.dot(left_side, right_side, preferred_element_type=jnp.float32)


def product_back(left_side, right_side):
    return lax.dot_general(
        left_side, right_side, (((1,), (1,)), ((), ())), preferred_element_type=jnp.float32
    )


def product_left(left_side, right_side):
    return lax.dot_general(
        left_side, right_side, (((0,), (0,)), ((), ())), preferred_element_type=jnp.float32
    )


def norm_forward(residual, scale_gain, shift_bias):
    row_mean = jnp.mean(residual, axis=-1, keepdims=True)
    centred = residual - row_mean
    variance = jnp.mean(centred * centred, axis=-1, keepdims=True)
    inverse = lax.rsqrt(variance + LN_EPS)
    normed = centred * inverse
    return (normed * scale_gain + shift_bias, normed, inverse)


def norm_backward(grad_output, normed, inverse, scale_gain):
    grad_normed = grad_output * scale_gain
    first_term = jnp.mean(grad_normed, axis=-1, keepdims=True)
    second_term = jnp.mean(grad_normed * normed, axis=-1, keepdims=True)
    grad_input = inverse * (grad_normed - first_term - normed * second_term)
    return (grad_input, jnp.sum(grad_output * normed, axis=0), jnp.sum(grad_output, axis=0))


def split_blocks(rows_array, block_rows):
    return rows_array.reshape(-1, block_rows, rows_array.shape[1] // HEAD_DIM, HEAD_DIM)


def blocks_to_rows(blocked):
    reordered = jnp.transpose(blocked, (0, 2, 1, 3))
    return reordered.reshape(-1, blocked.shape[1] * blocked.shape[3])


def block_scores(query_block, key_block, query_docs, key_docs):
    scores = jnp.einsum(
        "qhd,khd->hqk", query_block, key_block, preferred_element_type=jnp.float32
    ) * HEAD_DIM ** (-0.5)
    allowed = (query_docs[:, None] == key_docs[None, :])[None, :, :]
    return (scores, allowed)


def intersecting(first_docs, second_docs):
    return jnp.logical_and(
        jnp.max(first_docs) >= jnp.min(second_docs), jnp.min(first_docs) <= jnp.max(second_docs)
    )


def keep_state(carried):
    return carried


def forward_update(carried, query_block, query_docs, key_block, value_block, key_docs):
    running_max, row_total, accumulated = carried
    scores, allowed = block_scores(query_block, key_block, query_docs, key_docs)
    scores = jnp.where(allowed, scores, MASKED_SCORE)
    new_max = jnp.maximum(running_max, jnp.max(scores, axis=2))
    decay_factor = jnp.exp(running_max - new_max)
    weights = jnp.where(allowed, jnp.exp(scores - new_max[:, :, None]), 0.0)
    row_total = row_total * decay_factor + jnp.sum(weights, axis=2)
    update = jnp.einsum(
        "hqk,khd->hqd",
        weights.astype(jnp.bfloat16),
        value_block,
        preferred_element_type=jnp.float32,
    )
    return (new_max, row_total, accumulated * decay_factor[:, :, None] + update)


def forward_folder(query_blocks, doc_blocks):
    block_rows = query_blocks.shape[1]

    def forward_fold_step(carried_in, pieces, start_row):
        key_piece, value_piece, key_doc_piece = pieces
        key_blocks = split_blocks(key_piece, block_rows)
        value_blocks = split_blocks(value_piece, block_rows)
        key_doc_blocks = key_doc_piece.astype(jnp.float32).reshape(-1, block_rows)

        def forward_one_block(block_index, carried):
            key_docs = key_doc_blocks[block_index]
            results = []
            for query_index in range(query_blocks.shape[0]):
                current = tuple((member[query_index] for member in carried))
                update = partial(
                    forward_update,
                    query_block=query_blocks[query_index],
                    query_docs=doc_blocks[query_index],
                    key_block=key_blocks[block_index],
                    value_block=value_blocks[block_index],
                    key_docs=key_docs,
                )
                results.append(
                    lax.cond(
                        intersecting(doc_blocks[query_index], key_docs), update, keep_state, current
                    )
                )
            return tuple((jnp.stack([entry[member] for entry in results]) for member in range(3)))

        return lax.fori_loop(0, key_blocks.shape[0], forward_one_block, carried_in)

    return forward_fold_step


def query_grad_update(
    grad_query,
    query_block,
    query_docs,
    grad_block,
    log_total,
    delta_rows,
    key_block,
    value_block,
    key_docs,
):
    scores, allowed = block_scores(query_block, key_block, query_docs, key_docs)
    probs = jnp.where(allowed, jnp.exp(scores - log_total[:, :, None]), 0.0)
    grad_probs = jnp.einsum(
        "qhd,khd->hqk", grad_block, value_block, preferred_element_type=jnp.float32
    )
    grad_scores = (probs * (grad_probs - delta_rows[:, :, None])).astype(jnp.bfloat16)
    return grad_query + jnp.einsum(
        "hqk,khd->hqd", grad_scores, key_block, preferred_element_type=jnp.float32
    ) * HEAD_DIM ** (-0.5)


def query_grad_folder(query_blocks, doc_blocks, grad_blocks, log_blocks, delta_blocks):
    block_rows = query_blocks.shape[1]

    def query_fold_step(carried_in, pieces, start_row):
        key_piece, value_piece, key_doc_piece = pieces
        key_blocks = split_blocks(key_piece, block_rows)
        value_blocks = split_blocks(value_piece, block_rows)
        key_doc_blocks = key_doc_piece.astype(jnp.float32).reshape(-1, block_rows)

        def query_one_block(block_index, carried):
            key_docs = key_doc_blocks[block_index]
            results = []
            for query_index in range(query_blocks.shape[0]):
                update = partial(
                    query_grad_update,
                    query_block=query_blocks[query_index],
                    query_docs=doc_blocks[query_index],
                    grad_block=grad_blocks[query_index],
                    log_total=log_blocks[query_index],
                    delta_rows=delta_blocks[query_index],
                    key_block=key_blocks[block_index],
                    value_block=value_blocks[block_index],
                    key_docs=key_docs,
                )
                results.append(
                    lax.cond(
                        intersecting(doc_blocks[query_index], key_docs),
                        update,
                        keep_state,
                        carried[query_index],
                    )
                )
            return jnp.stack(results)

        return lax.fori_loop(0, key_blocks.shape[0], query_one_block, carried_in)

    return query_fold_step


def key_grad_update(
    carried,
    key_block,
    value_block,
    key_docs,
    query_block,
    grad_block,
    log_total,
    delta_rows,
    query_docs,
):
    grad_key, grad_value = carried
    scores, allowed = block_scores(query_block, key_block, query_docs, key_docs)
    probs = jnp.where(allowed, jnp.exp(scores - log_total[:, :, None]), 0.0)
    grad_value = grad_value + jnp.einsum(
        "hqk,qhd->hkd", probs.astype(jnp.bfloat16), grad_block, preferred_element_type=jnp.float32
    )
    grad_probs = jnp.einsum(
        "qhd,khd->hqk", grad_block, value_block, preferred_element_type=jnp.float32
    )
    grad_scores = (probs * (grad_probs - delta_rows[:, :, None])).astype(jnp.bfloat16)
    grad_key = grad_key + jnp.einsum(
        "hqk,qhd->hkd", grad_scores, query_block, preferred_element_type=jnp.float32
    ) * HEAD_DIM ** (-0.5)
    return (grad_key, grad_value)


def key_grad_folder(key_blocks, value_blocks, doc_blocks):
    block_rows = key_blocks.shape[1]

    def key_fold_step(carried_in, pieces, start_row):
        query_piece, grad_piece, log_piece, delta_piece, doc_piece = pieces
        query_blocks = split_blocks(query_piece.astype(jnp.bfloat16), block_rows)
        grad_blocks = split_blocks(grad_piece.astype(jnp.bfloat16), block_rows)
        log_blocks = jnp.transpose(log_piece.reshape(-1, block_rows, log_piece.shape[1]), (0, 2, 1))
        delta_blocks = jnp.transpose(
            delta_piece.reshape(-1, block_rows, delta_piece.shape[1]), (0, 2, 1)
        )
        query_doc_blocks = doc_piece.reshape(-1, block_rows)

        def key_one_block(block_index, carried):
            query_docs = query_doc_blocks[block_index]
            results = []
            for key_index in range(key_blocks.shape[0]):
                current = (carried[0][key_index], carried[1][key_index])
                update = partial(
                    key_grad_update,
                    key_block=key_blocks[key_index],
                    value_block=value_blocks[key_index],
                    key_docs=doc_blocks[key_index],
                    query_block=query_blocks[block_index],
                    grad_block=grad_blocks[block_index],
                    log_total=log_blocks[block_index],
                    delta_rows=delta_blocks[block_index],
                    query_docs=query_docs,
                )
                results.append(
                    lax.cond(
                        intersecting(query_docs, doc_blocks[key_index]), update, keep_state, current
                    )
                )
            return (
                jnp.stack([entry[0] for entry in results]),
                jnp.stack([entry[1] for entry in results]),
            )

        return lax.fori_loop(0, query_blocks.shape[0], key_one_block, carried_in)

    return key_fold_step


def attention_forward(query_rows, key_rows, value_rows, row_docs, block_rows):
    query_blocks = split_blocks(query_rows, block_rows)
    doc_blocks = row_docs.reshape(-1, block_rows)
    block_count = query_blocks.shape[0]
    head_count = query_blocks.shape[2]
    send_docs = row_docs.astype(jnp.bfloat16)
    start_state = (
        jnp.full((block_count, head_count, block_rows), MASKED_SCORE, jnp.float32),
        jnp.zeros((block_count, head_count, block_rows), jnp.float32),
        jnp.zeros((block_count, head_count, block_rows, HEAD_DIM), jnp.float32),
    )
    fold_forward = forward_folder(query_blocks, doc_blocks)
    running_max, row_total, accumulated = fold_forward(
        start_state,
        (
            lax.all_gather(key_rows, "blk", axis=0, tiled=True),
            lax.all_gather(value_rows, "blk", axis=0, tiled=True),
            lax.all_gather(send_docs, "blk", axis=0, tiled=True),
        ),
        jnp.int32(0),
    )
    head_outputs = blocks_to_rows(accumulated / row_total[:, :, :, None]).astype(jnp.bfloat16)
    log_total = running_max + jnp.log(row_total)
    return (head_outputs, log_total)


def attention_backward(
    grad_rows, head_outputs, log_total, query_rows, key_rows, value_rows, row_docs, block_rows
):
    query_blocks = split_blocks(query_rows, block_rows)
    key_blocks = split_blocks(key_rows, block_rows)
    value_blocks = split_blocks(value_rows, block_rows)
    doc_blocks = row_docs.reshape(-1, block_rows)
    block_count = query_blocks.shape[0]
    head_count = query_blocks.shape[2]
    send_docs = row_docs.astype(jnp.bfloat16)
    grad_blocks = split_blocks(grad_rows, block_rows)
    output_blocks = split_blocks(head_outputs, block_rows)
    delta_blocks = jnp.einsum(
        "nqhd,nqhd->nhq", grad_blocks.astype(jnp.float32), output_blocks.astype(jnp.float32)
    )
    log_rows = jnp.transpose(log_total, (0, 2, 1)).reshape(-1, head_count)
    delta_rows = jnp.transpose(delta_blocks, (0, 2, 1)).reshape(-1, head_count)
    fold_queries = query_grad_folder(query_blocks, doc_blocks, grad_blocks, log_total, delta_blocks)
    fold_keys = key_grad_folder(key_blocks, value_blocks, doc_blocks)
    query_start = jnp.zeros((block_count, head_count, block_rows, HEAD_DIM), jnp.float32)
    key_start = (query_start, query_start)
    query_send = (
        query_rows.astype(jnp.float32),
        grad_rows.astype(jnp.float32),
        log_rows,
        delta_rows,
        row_docs,
    )
    grad_query_state = fold_queries(
        query_start,
        (
            lax.all_gather(key_rows, "blk", axis=0, tiled=True),
            lax.all_gather(value_rows, "blk", axis=0, tiled=True),
            lax.all_gather(send_docs, "blk", axis=0, tiled=True),
        ),
        jnp.int32(0),
    )
    grad_key_state, grad_value_state = fold_keys(
        key_start,
        (
            lax.all_gather(query_send[0], "blk", axis=0, tiled=True),
            lax.all_gather(query_send[1], "blk", axis=0, tiled=True),
            lax.all_gather(query_send[2], "blk", axis=0, tiled=True),
            lax.all_gather(query_send[3], "blk", axis=0, tiled=True),
            lax.all_gather(query_send[4], "blk", axis=0, tiled=True),
        ),
        jnp.int32(0),
    )
    return (
        blocks_to_rows(grad_query_state).astype(jnp.bfloat16),
        blocks_to_rows(grad_key_state).astype(jnp.bfloat16),
        blocks_to_rows(grad_value_state).astype(jnp.bfloat16),
    )


def data_layer(tokens, full, row_docs, out_grad, block_rows):
    (
        full_query,
        full_query_bias,
        full_key,
        full_value,
        full_value_bias,
        full_output,
        full_output_bias,
        full_first_gain,
        full_first_shift,
        full_inner,
        full_inner_bias,
        full_outer,
        full_outer_bias,
        full_second_gain,
        full_second_shift,
    ) = full
    queries = (dense_product(tokens, full_query) + full_query_bias.astype(jnp.float32)).astype(
        jnp.bfloat16
    )
    keys_local = dense_product(tokens, full_key).astype(jnp.bfloat16)
    values_local = (dense_product(tokens, full_value) + full_value_bias.astype(jnp.float32)).astype(
        jnp.bfloat16
    )
    query_rows, key_rows, value_rows = (
        lax.all_to_all(queries, "head", split_axis=1, concat_axis=0, tiled=True),
        lax.all_to_all(keys_local, "head", split_axis=1, concat_axis=0, tiled=True),
        lax.all_to_all(values_local, "head", split_axis=1, concat_axis=0, tiled=True),
    )
    head_outputs, log_total = attention_forward(
        query_rows, key_rows, value_rows, row_docs, block_rows
    )
    attended = lax.all_to_all(head_outputs, "head", split_axis=0, concat_axis=1, tiled=True)
    branch = dense_product(attended, full_output) + full_output_bias.astype(jnp.float32)
    hidden, first_normed, first_inverse = norm_forward(
        tokens.astype(jnp.float32) + branch,
        full_first_gain.astype(jnp.float32),
        full_first_shift.astype(jnp.float32),
    )
    hidden_low = hidden.astype(jnp.bfloat16)
    inner_value = dense_product(hidden_low, full_inner) + full_inner_bias.astype(jnp.float32)
    activated_full, gelu_pullback = jax.vjp(partial(jax.nn.gelu, approximate=False), inner_value)
    activated = activated_full.astype(jnp.bfloat16)
    outer_value = dense_product(activated, full_outer) + full_outer_bias.astype(jnp.float32)
    layer_full, second_normed, second_inverse = norm_forward(
        hidden + outer_value,
        full_second_gain.astype(jnp.float32),
        full_second_shift.astype(jnp.float32),
    )
    layer_out = layer_full.astype(jnp.bfloat16)
    grad_output = out_grad.astype(jnp.float32)
    grad_resid2, second_gain_term, second_shift_term = norm_backward(
        grad_output, second_normed, second_inverse, full_second_gain.astype(jnp.float32)
    )
    grad_outer = grad_resid2.astype(jnp.bfloat16)
    outer_weight_term = product_left(activated, grad_outer)
    outer_bias_term = jnp.sum(grad_outer.astype(jnp.float32), axis=0)
    grad_inner = gelu_pullback(product_back(grad_outer, full_outer))[0].astype(jnp.bfloat16)
    inner_weight_term = product_left(hidden_low, grad_inner)
    inner_bias_term = jnp.sum(grad_inner.astype(jnp.float32), axis=0)
    grad_hidden = grad_resid2 + product_back(grad_inner, full_inner)
    grad_resid1, first_gain_term, first_shift_term = norm_backward(
        grad_hidden, first_normed, first_inverse, full_first_gain.astype(jnp.float32)
    )
    grad_branch = grad_resid1.astype(jnp.bfloat16)
    output_weight_term = product_left(attended, grad_branch)
    output_bias_term = jnp.sum(grad_branch.astype(jnp.float32), axis=0)
    grad_attended = product_back(grad_branch, full_output).astype(jnp.bfloat16)
    grad_rows = lax.all_to_all(grad_attended, "head", split_axis=1, concat_axis=0, tiled=True)
    grad_query_rows, grad_key_rows, grad_value_rows = attention_backward(
        grad_rows, head_outputs, log_total, query_rows, key_rows, value_rows, row_docs, block_rows
    )
    grad_queries, grad_keys, grad_values = (
        lax.all_to_all(grad_query_rows, "head", split_axis=0, concat_axis=1, tiled=True),
        lax.all_to_all(grad_key_rows, "head", split_axis=0, concat_axis=1, tiled=True),
        lax.all_to_all(grad_value_rows, "head", split_axis=0, concat_axis=1, tiled=True),
    )
    query_weight_term = product_left(tokens, grad_queries)
    query_bias_term = jnp.sum(grad_queries.astype(jnp.float32), axis=0)
    key_weight_term = product_left(tokens, grad_keys)
    value_weight_term = product_left(tokens, grad_values)
    value_bias_term = jnp.sum(grad_values.astype(jnp.float32), axis=0)
    tokens_grad = (
        grad_resid1
        + product_back(grad_queries, full_query)
        + product_back(grad_keys, full_key)
        + product_back(grad_values, full_value)
    ).astype(jnp.bfloat16)
    summed = (
        lax.psum_scatter(query_weight_term, ("head", "blk"), scatter_dimension=0, tiled=True),
        lax.psum_scatter(query_bias_term, ("head", "blk"), scatter_dimension=0, tiled=True),
        lax.psum_scatter(key_weight_term, ("head", "blk"), scatter_dimension=0, tiled=True),
        lax.psum_scatter(value_weight_term, ("head", "blk"), scatter_dimension=0, tiled=True),
        lax.psum_scatter(value_bias_term, ("head", "blk"), scatter_dimension=0, tiled=True),
        lax.psum_scatter(output_weight_term, ("head", "blk"), scatter_dimension=0, tiled=True),
        lax.psum_scatter(output_bias_term, ("head", "blk"), scatter_dimension=0, tiled=True),
        lax.psum_scatter(first_gain_term, ("head", "blk"), scatter_dimension=0, tiled=True),
        lax.psum_scatter(first_shift_term, ("head", "blk"), scatter_dimension=0, tiled=True),
        lax.psum_scatter(inner_weight_term, ("head", "blk"), scatter_dimension=0, tiled=True),
        lax.psum_scatter(inner_bias_term, ("head", "blk"), scatter_dimension=0, tiled=True),
        lax.psum_scatter(outer_weight_term, ("head", "blk"), scatter_dimension=0, tiled=True),
        lax.psum_scatter(outer_bias_term, ("head", "blk"), scatter_dimension=0, tiled=True),
        lax.psum_scatter(second_gain_term, ("head", "blk"), scatter_dimension=0, tiled=True),
        lax.psum_scatter(second_shift_term, ("head", "blk"), scatter_dimension=0, tiled=True),
    )
    return (layer_out, tokens_grad) + tuple(summed)


def body(
    tokens,
    query_weight,
    query_bias,
    key_weight,
    value_weight,
    value_bias,
    output_weight,
    output_bias,
    first_gain,
    first_shift,
    inner_weight,
    inner_bias,
    outer_weight,
    outer_bias,
    second_gain,
    second_shift,
    doc_starts,
    out_grad,
):
    shards = (
        query_weight,
        query_bias,
        key_weight,
        value_weight,
        value_bias,
        output_weight,
        output_bias,
        first_gain,
        first_shift,
        inner_weight,
        inner_bias,
        outer_weight,
        outer_bias,
        second_gain,
        second_shift,
    )
    full = (
        lax.all_gather(shards[0], ("head", "blk"), axis=0, tiled=True),
        lax.all_gather(shards[1], ("head", "blk"), axis=0, tiled=True),
        lax.all_gather(shards[2], ("head", "blk"), axis=0, tiled=True),
        lax.all_gather(shards[3], ("head", "blk"), axis=0, tiled=True),
        lax.all_gather(shards[4], ("head", "blk"), axis=0, tiled=True),
        lax.all_gather(shards[5], ("head", "blk"), axis=0, tiled=True),
        lax.all_gather(shards[6], ("head", "blk"), axis=0, tiled=True),
        lax.all_gather(shards[7], ("head", "blk"), axis=0, tiled=True),
        lax.all_gather(shards[8], ("head", "blk"), axis=0, tiled=True),
        lax.all_gather(shards[9], ("head", "blk"), axis=0, tiled=True),
        lax.all_gather(shards[10], ("head", "blk"), axis=0, tiled=True),
        lax.all_gather(shards[11], ("head", "blk"), axis=0, tiled=True),
        lax.all_gather(shards[12], ("head", "blk"), axis=0, tiled=True),
        lax.all_gather(shards[13], ("head", "blk"), axis=0, tiled=True),
        lax.all_gather(shards[14], ("head", "blk"), axis=0, tiled=True),
    )
    tok_rows = tokens.shape[0]
    half_length = tok_rows * lax.axis_size("blk")
    blk_place = lax.axis_index("blk")
    offsets = jnp.arange(tok_rows, dtype=jnp.int32)
    row_positions = jnp.concatenate(
        [blk_place * tok_rows + offsets, half_length + blk_place * tok_rows + offsets]
    )
    row_docs = doc_numbers(doc_starts, row_positions)
    return data_layer(tokens, full, row_docs, out_grad, tok_rows)


MESH = pl.DeviceIdType.MESH
F32 = jnp.float32
BF16 = jnp.bfloat16
D = 768
QUARTER = 384
FF_CORE = 1536
HALF_ROWS = 2048
CHIP_ROWS = 256
CORE_HEADS = 6
PENALTY = -1e30
FAR = 2**30


def nn(a, b):
    return lax.dot_general(a, b, (((1,), (0,)), ((), ())), preferred_element_type=F32)


def nt(a, b):
    return lax.dot_general(a, b, (((1,), (1,)), ((), ())), preferred_element_type=F32)


def tn(a, b):
    return lax.dot_general(a, b, (((0,), (0,)), ((), ())), preferred_element_type=F32)


def at_128(index):
    return pl.multiple_of(index, 128)


def at_16(index):
    return pl.multiple_of(index, 16)


def at_8(index):
    return pl.multiple_of(index, 8)


class Place:
    def __init__(self):
        self.x = lax.axis_index("head")
        b = lax.axis_index("blk")
        self.z = lax.div(b, 4)
        self.y = lax.rem(lax.div(b, 2), 2)
        self.c = lax.rem(b, 2)
        self.chip = self.x * 8 + self.z * 2 + self.y
        self.slot = self.y * 4 + self.z
        self.ups = [self.z] + [lax.rem(self.z + k, 4) for k in (1, 2, 3)]
        self.downs = [self.ups[0], self.ups[3], self.ups[2], self.ups[1]]
        self.above = self.device(z=jnp.minimum(self.z + 1, 3))
        self.below = self.device(z=jnp.maximum(self.z - 1, 0))
        self.can_up, self.can_down = self.z < 3, self.z > 0
        self.has_below = [None] + [self.z >= step for step in (1, 2, 3)]
        self.has_above = [None] + [self.z <= 3 - step for step in (1, 2, 3)]
        self.sibling = self.device(c=1 - self.c)
        self.side = {"x": self.device(x=1 - self.x), "y": self.device(y=1 - self.y)}

    def device(self, x=None, z=None, y=None, c=None):
        x = self.x if x is None else x
        z = self.z if z is None else z
        y = self.y if y is None else y
        c = self.c if c is None else c
        return (x, z * 4 + y * 2 + c)

    def up(self, k):
        return self.ups[k]

    def down(self, k):
        return self.downs[k]


class Sems:
    def __init__(self, send, recv):
        self.send, self.recv, self.used = send, recv, 0

    def take(self, count):
        first = self.used
        self.used += count
        assert self.used <= self.send.shape[0]
        return first


class Mover:
    def __init__(self, sems, count):
        self.sems, self.first, self.parts = sems, sems.take(count), {}

    def copy(self, index):
        place = self.first + index
        src, dst, device = self.parts[index]()
        return pltpu.make_async_remote_copy(
            src,
            dst,
            self.sems.send.at[place],
            self.sems.recv.at[place],
            device_id=device,
            device_id_type=MESH,
        )

    def start(self, index, part):
        self.parts[index] = part
        self.copy(index).start()

    def arrived(self, index):
        self.copy(index).wait_recv()

    def sent(self):
        for index in sorted(self.parts):
            self.copy(index).wait_send()


class Gather:
    def __init__(self, place, sems, piece, first, second=None):
        self.place, self.sems, self.piece = place, sems, piece
        self.device = {"up": place.above, "down": place.below, "first": first}
        if second is not None:
            self.device.update(second=second, across=second)
        self.slot = {kind: sems.take(4) for kind in self.device}

    def copy(self, kind, z):
        place = self.slot[kind] + z
        piece = self.piece(z, kind == "across")
        return pltpu.make_async_remote_copy(
            piece,
            piece,
            self.sems.send.at[place],
            self.sems.recv.at[place],
            device_id=self.device[kind],
            device_id_type=MESH,
        )

    def sideways(self, z):
        self.copy("first", z).start()
        if "second" in self.device:
            self.copy("second", z).start()

    def begin_z(self):
        p = self.place

        @pl.when(p.can_up)
        def _():
            self.copy("up", p.z).start()

        @pl.when(p.can_down)
        def _():
            self.copy("down", p.z).start()

    def begin(self):
        self.begin_z()
        self.sideways(self.place.z)

    def hop(self, step):
        p = self.place

        @pl.when(p.has_below[step])
        def _():
            z = p.z - step
            self.copy("up", z).wait_recv()

            @pl.when(p.can_up)
            def _():
                self.copy("up", z).start()

            self.sideways(z)

        @pl.when(p.has_above[step])
        def _():
            z = p.z + step
            self.copy("down", z).wait_recv()

            @pl.when(p.can_down)
            def _():
                self.copy("down", z).start()

            self.sideways(z)

    def across_one(self, z):
        self.copy("first", z).wait_recv()
        if "second" in self.device:
            self.copy("across", z).start()

    def across(self, step):
        p = self.place
        if step == 0:
            self.across_one(p.z)
            return

        @pl.when(p.has_below[step])
        def _():
            self.across_one(p.z - step)

        @pl.when(p.has_above[step])
        def _():
            self.across_one(p.z + step)

    def complete(self):
        for z in range(4):
            self.copy("second", z).wait_recv()
            self.copy("across", z).wait_recv()

    def sent(self):
        p = self.place
        for z in range(4):
            for kind in self.device:
                wait = self.copy(kind, z).wait_send
                if kind == "up":
                    pl.when(jnp.logical_and(p.can_up, p.z >= z))(wait)
                elif kind == "down":
                    pl.when(jnp.logical_and(p.can_down, p.z <= z))(wait)
                else:
                    wait()


class Reduce(Mover):
    def __init__(self, place, sems, ref, rows, first, slots):
        super().__init__(sems, 15)
        self.place, self.ref, self.rows, self.axis = place, ref, rows, first
        self.one, self.two, self.three = slots

    def rows_of(self, x, z, y, count=1):
        return pl.ds(at_8((x * 8 + z * 2 + y) * self.rows), count * self.rows)

    def send_one(self, k):
        p, R = self.place, self.rows
        if self.axis == "x":

            def part():
                where = self.rows_of(1 - p.x, p.up(k), 0, 2)
                return self.ref.at[where], self.one.at[k], p.side["x"]

            self.start(2 * k, part)
        else:
            for xx in (0, 1):

                def part(xx=xx):
                    where = self.rows_of(xx, p.up(k), 1 - p.y)
                    return self.ref.at[where], self.one.at[k, pl.ds(xx * R, R)], p.side["y"]

                self.start(2 * k + xx, part)

    def add(self, where, term):
        self.ref[where] = (self.ref[where].astype(F32) + term.astype(F32)).astype(self.ref.dtype)

    def send_two(self, k):
        p, R = self.place, self.rows
        if self.axis == "x":
            self.arrived(2 * k)
            self.add(self.rows_of(p.x, p.up(k), 0, 2), self.one[k])

            def part():
                where = self.rows_of(p.x, p.up(k), 1 - p.y)
                return self.ref.at[where], self.two.at[k], p.side["y"]

        else:
            for xx in (0, 1):
                self.arrived(2 * k + xx)
                self.add(self.rows_of(xx, p.up(k), p.y), self.one[k, xx * R : (xx + 1) * R])

            def part():
                where = self.rows_of(1 - p.x, p.up(k), p.y)
                return self.ref.at[where], self.two.at[k], p.side["x"]

        self.start(8 + k, part)

    def send_three(self, k):
        p = self.place
        self.arrived(8 + k)
        if k:
            self.add(self.rows_of(p.x, p.up(k), p.y), self.two[k])

            def part():
                where = self.rows_of(p.x, p.up(k), p.y)
                return self.ref.at[where], self.three.at[k - 1], p.device(z=p.up(k))

            self.start(12 + k - 1, part)

    def result(self):
        p = self.place
        total = self.ref[self.rows_of(p.x, p.z, p.y)].astype(F32) + self.two[0].astype(F32)
        for k in (1, 2, 3):
            self.arrived(12 + k - 1)
            total = total + self.three[k - 1].astype(F32)
        return total


def z_start(*gathers):
    return lambda: [gather.begin_z() for gather in gathers]


def first(*gathers):
    return lambda: [gather.copy("first", gather.place.z).start() for gather in gathers]


def second(*gathers):
    return lambda: [gather.copy("second", gather.place.z).start() for gather in gathers]


def hop(step, *gathers):
    return lambda: [gather.hop(step) for gather in gathers]


def across(step, *gathers):
    return lambda: [gather.across(step) for gather in gathers]


def one(reduce):
    return lambda: [reduce.send_one(k) for k in ORDER]


def two(reduce, k):
    return lambda: reduce.send_two(k)


def three(reduce, k):
    return lambda: reduce.send_three(k)


def loop(action, *between):
    def run():
        def step(j, carry):
            for i, steps in enumerate(between):

                @pl.when(j == i + 1)
                def _(steps=steps):
                    for inside in steps:
                        inside()

            action(j)
            return carry

        lax.fori_loop(0, len(between) + 1, step, 0)

    return run


def row_mean(value):
    return jnp.sum(value, axis=1, keepdims=True) * (1.0 / D)


def normed_of(residual):
    centred = residual - row_mean(residual)
    inverse = lax.rsqrt(row_mean(centred * centred) + LN_EPS)
    return centred * inverse, inverse


def normed_back(grad_normed, normed, inverse):
    return inverse * (grad_normed - row_mean(grad_normed) - normed * row_mean(grad_normed * normed))


def lane_iota(shape):
    return lax.broadcasted_iota(jnp.int32, shape, len(shape) - 1)


def row_iota(shape):
    return lax.broadcasted_iota(jnp.int32, shape, 0)


SCRATCH = dict(
    X=((HALF_ROWS, D), BF16),
    WS=((512, 128), BF16),
    WA=((D, 1536), BF16),
    WI=((D, FF_CORE), BF16),
    WT=((2 * FF_CORE, QUARTER), BF16),
    WO=((QUARTER, D), BF16),
    WTR=((FF_CORE, D), BF16),
    OG=((CHIP_ROWS, D), BF16),
    SWAP_S=((24, 3072), F32),
    SWAP_R=((24, 3072), F32),
    QKV=((HALF_ROWS, 1152), BF16),
    QE=((HALF_ROWS, 128), BF16),
    KE=((HALF_ROWS, 128), BF16),
    ATT=((CHIP_ROWS, QUARTER), BF16),
    LSE=((CHIP_ROWS, 128), F32),
    DELTA=((CHIP_ROWS, 128), F32),
    VEC=((16, D), F32),
    BIN=((8, FF_CORE), F32),
    DO=((HALF_ROWS, QUARTER), BF16),
    STAT=((16, HALF_ROWS), F32),
    PX_S=((4, CHIP_ROWS, D), BF16),
    PX_R=((4, CHIP_ROWS, D), BF16),
    PART=((CHIP_ROWS, D), F32),
    HID=((CHIP_ROWS, D), F32),
    N1=((CHIP_ROWS, D), F32),
    HL=((CHIP_ROWS, D), BF16),
    ACT=((CHIP_ROWS, FF_CORE), BF16),
    GP=((CHIP_ROWS, FF_CORE), F32),
    GIN=((CHIP_ROWS, FF_CORE), BF16),
    GO=((CHIP_ROWS, D), BF16),
    GB=((CHIP_ROWS, D), BF16),
    DQKV=((CHIP_ROWS, 1152), BF16),
    SV=((16, D), F32),
    GI=((D, FF_CORE), BF16),
    GT=((2 * FF_CORE, QUARTER), BF16),
    GT_S=((FF_CORE, QUARTER), BF16),
    GW=((D, QUARTER), BF16),
    GW_S=((QUARTER, QUARTER), BF16),
    GQ=((D, QUARTER), BF16),
    GK=((D, D), BF16),
    SG=((512, 128), F32),
    GI1=((4, 96, FF_CORE), BF16),
    GI2=((4, 48, FF_CORE), BF16),
    GI3=((3, 48, FF_CORE), BF16),
    GT1=((4, 384, QUARTER), BF16),
    GT2=((4, 192, QUARTER), BF16),
    GT3=((3, 192, QUARTER), BF16),
    GW1=((4, 96, QUARTER), BF16),
    GW2=((4, 48, QUARTER), BF16),
    GW3=((3, 48, QUARTER), BF16),
    GQ1=((4, 96, QUARTER), BF16),
    GQ2=((4, 48, QUARTER), BF16),
    GQ3=((3, 48, QUARTER), BF16),
    GK1=((4, 96, D), BF16),
    GK2=((4, 48, D), BF16),
    GK3=((3, 48, D), BF16),
    SG1=((4, 64, 128), F32),
    SG2=((4, 32, 128), F32),
    SG3=((3, 32, 128), F32),
    FI=((48, FF_CORE), F32),
    FT=((192, QUARTER), F32),
    FW=((48, QUARTER), F32),
    FQ=((48, QUARTER), F32),
    FK=((48, D), F32),
    FS=((32, 128), F32),
    FI_R=((24, FF_CORE), F32),
    FT_R=((96, QUARTER), F32),
    FW_R=((24, QUARTER), F32),
    FQ_R=((24, QUARTER), F32),
    FK_R=((24, D), F32),
    FS_R=((16, 128), F32),
)
SEM_COUNT = 250
ORDER = (1, 2, 3, 0)


class Refs:
    pass


def layer_kernel(*refs):
    r = Refs()
    (
        r.tok, r.og, r.wq, r.wk, r.wv, r.wo, r.wi, r.wt, r.small, r.docs,
        r.out, r.tgrad, r.gq, r.gk, r.gv, r.go, r.gi, r.gt, r.gs,
    ) = refs[:19]
    for name, ref in zip(SCRATCH, refs[19:]):
        setattr(r, name, ref)
    sems = Sems(refs[-2], refs[-1])
    p = Place()
    c, other = p.c, 1 - p.c

    barrier = pltpu.get_barrier_semaphore()
    partners = [p.sibling, p.side["x"], p.side["y"]] + [p.device(z=p.up(k)) for k in (1, 2, 3)]
    for partner in partners:
        pl.semaphore_signal(barrier, inc=1, device_id=partner, device_id_type=MESH)
    pl.semaphore_wait(barrier, len(partners))

    swap = Mover(sems, 16)
    chip_base = p.slot * CHIP_ROWS
    own_base = chip_base + 128 * c
    chip = pl.ds(at_128(chip_base), CHIP_ROWS)
    own_half = pl.ds(at_128(128 * c), 128)

    cols = [pl.ds(at_128(QUARTER * side), QUARTER) for side in (0, 1)]
    mine_cols = pl.ds(at_128(QUARTER * c), QUARTER)
    other_cols = pl.ds(at_128(QUARTER * other), QUARTER)
    for index, ref in enumerate((r.wq, r.wk, r.wv, r.wo)):
        r.SWAP_S[:, QUARTER * index : QUARTER * (index + 1)] = ref[:, other_cols].astype(F32)
    r.SWAP_S[:, 1536:3072] = r.wi[:, pl.ds(at_128(FF_CORE * other), FF_CORE)].astype(F32)
    swap.start(0, lambda: (r.SWAP_S, r.SWAP_R, p.sibling))
    r.X[pl.ds(at_128(own_base), 128), :] = r.tok[...]

    def tok_piece(z, across):
        y = 1 - p.y if across else p.y
        return r.X.at[pl.ds(at_128((y * 4 + z) * CHIP_ROWS + 128 * c), 128)]

    tok = Gather(p, sems, tok_piece, p.side["y"], p.sibling)

    small_rows = r.WS.at[pl.ds(at_16(32 * p.chip + 16 * c), 16)]
    r.WS[pl.ds(at_16(32 * p.chip + 16 * c), 16), :] = r.small[...]
    swap.start(1, lambda: (small_rows, small_rows, p.sibling))
    outer_rows = pl.ds(at_16(192 * p.chip + 96 * c), 96)
    r.WT[outer_rows, :] = r.wt[:, mine_cols]
    swap.start(2, lambda: (r.wt.at[:, other_cols], r.WT.at[outer_rows], p.sibling))
    og_rows = r.OG.at[own_half]
    r.OG[own_half, :] = r.og[...]
    swap.start(3, lambda: (og_rows, og_rows, p.sibling))

    def weights(ref, rows, first):
        def piece(z, across):
            x, y = p.x, p.y
            if across:
                x, y = (x, 1 - y) if first == "y" else (1 - x, y)
            return ref.at[pl.ds(at_16((x * 8 + z * 2 + y) * rows), rows)]

        return Gather(p, sems, piece, p.side[first], p.side["y" if first == "x" else "x"])

    gs = weights(r.WS, 32, "y")
    ga = weights(r.WA, 48, "y")
    gi = weights(r.WI, 48, "y")
    gt = weights(r.WT, 192, "x")

    column = lane_iota((1, D))
    by_24, in_24 = lax.div(column, 24), lax.rem(column, 24)
    spread = jnp.where(row_iota((128, D)) == in_24, 1.0, 0.0).astype(BF16)
    row = row_iota((512, 1))
    owner, kind = lax.shift_right_logical(row, 4), jnp.bitwise_and(row, 15)
    row_set = pl.ds(at_128(QUARTER * c), QUARTER)
    other_set = pl.ds(at_128(QUARTER * other), QUARTER)
    outer_set = pl.ds(at_128(FF_CORE * c), FF_CORE)
    other_outer = pl.ds(at_128(FF_CORE * other), FF_CORE)
    lanes128 = lane_iota((1, 128))
    in_head = [jnp.logical_and(lanes128 >= 64 * e, lanes128 < 64 * e + 64) for e in (0, 1)]
    own_row = lax.shift_right_logical(row_iota((CHIP_ROWS, 1)), 7) == c
    own_is_first = c == 0
    chip_weights = pl.ds(at_16(48 * p.chip), 48)
    sibling_half = pl.ds(at_128(128 * other), 128)

    def masked(value, e, scale=1.0):
        return jnp.where(in_head[e], value.astype(F32) * scale, 0.0).astype(BF16)

    def pair_cols(base, pair):
        return pl.ds(at_128(base + 128 * pair), 128)

    def exchange(index, partial):
        r.PX_S[index] = partial.astype(BF16)
        swap.start(6 + index, lambda: (r.PX_S.at[index], r.PX_R.at[index], p.sibling))

    def column_sum(value):
        return jnp.sum(jnp.where(own_row, value, 0.0), axis=0, keepdims=True)

    def vector(index):
        return r.VEC[index : index + 1, :]

    kept_values = {}
    def take_weights():
        swap.arrived(0)
        for index, ref in enumerate((r.wq, r.wk, r.wv, r.wo)):
            where = slice(QUARTER * index, QUARTER * (index + 1))
            kept = ref[:, mine_cols].astype(F32)
            came = r.SWAP_R[:, where]
            both = jnp.concatenate(
                [jnp.where(own_is_first, kept, came), jnp.where(own_is_first, came, kept)], axis=0
            )
            r.WA[chip_weights, where] = both.astype(BF16)
        swap.arrived(1)
        kept = r.wi[:, pl.ds(at_128(FF_CORE * c), FF_CORE)].astype(F32)
        came = r.SWAP_R[:, 1536:3072]
        both = jnp.concatenate(
            [jnp.where(own_is_first, kept, came), jnp.where(own_is_first, came, kept)], axis=0
        )
        r.WI[chip_weights, :] = both.astype(BF16)
        swap.arrived(2)

    def mark_documents():
        one_row = lane_iota((1, 128))
        starts = jnp.full((1, 128), FAR, jnp.int32)
        nexts = jnp.full((1, 128), FAR, jnp.int32)
        count = r.docs.shape[0]
        for d in range(count):
            starts = jnp.where(one_row == d, r.docs[d], starts)
            if d:
                nexts = jnp.where(one_row == d - 1, r.docs[d], nexts)
        lanes = lane_iota((CHIP_ROWS, 128))
        for j in range(8):
            place = row_iota((CHIP_ROWS, 128)) + (p.x * HALF_ROWS + (j % 4) * 512 + (j // 4) * 256)
            inside = jnp.logical_and(place >= starts, place < nexts)
            rows = slice(j * CHIP_ROWS, (j + 1) * CHIP_ROWS)
            r.QE[rows, :] = jnp.where(inside, 1.0, 0.0).astype(BF16)
            r.KE[rows, :] = jnp.where(jnp.logical_or(inside, lanes >= 16), 0.0, PENALTY).astype(BF16)

    def spread_vectors():
        gs.complete()
        ga.complete()
        spread_rows = nn(r.WS[...], spread)
        chosen = jnp.where(owner == by_24, spread_rows, 0.0)
        r.VEC[...] = jnp.sum(chosen.reshape(32, 16, D), axis=0)
        part_of = jnp.where(
            jnp.logical_and(kind >= 8, kind < 12), 4 * (owner - 16 * c) + kind - 8, -1000
        )
        for u in (0, 1):
            chosen = jnp.where(part_of - 32 * u == by_24, spread_rows, 0.0)
            r.BIN[0:1, D * u : D * (u + 1)] = jnp.sum(chosen, axis=0, keepdims=True)
        r.WO[:, mine_cols] = r.WA[row_set, 1152:1536]
        swap.start(4, lambda: (r.WA.at[other_set, pl.ds(1152, QUARTER)], r.WO.at[:, mine_cols], p.sibling))

    def project(j):
        query_bias, value_bias = r.VEC[0:1, mine_cols], r.VEC[1:2, mine_cols]
        bias = jnp.concatenate([query_bias, jnp.zeros_like(query_bias), value_bias], axis=1)
        for part in (0, 1):
            rows = pl.ds(at_128((2 * j + part) * CHIP_ROWS), CHIP_ROWS)
            r.QKV[rows, :] = (nn(r.X[rows, :], r.WA[:, 0:1152]) + bias).astype(BF16)

    def attend(pair):
        query_doc = r.QE[chip, :]
        queries = r.QKV[chip, pair_cols(0, pair)]
        keys = jnp.concatenate([r.QKV[:, pair_cols(QUARTER, pair)], r.KE[...]], axis=1)
        values = r.QKV[:, pair_cols(2 * QUARTER, pair)]
        outputs = []
        for e in (0, 1):
            query = jnp.concatenate([masked(queries, e, 0.125), query_doc], axis=1)
            scores = nt(query, keys)
            top = jnp.max(scores, axis=1, keepdims=True)
            weights = jnp.exp(scores - top)
            total = jnp.sum(weights, axis=1, keepdims=True)
            outputs.append(nn(weights.astype(BF16), values) / total)
            log_total = top + jnp.log(total)
            r.LSE[...] = jnp.where(lanes128 == 2 * pair + e, log_total, r.LSE[...])
        r.ATT[:, pair_cols(0, pair)] = jnp.where(in_head[0], outputs[0], outputs[1]).astype(BF16)

    def first_norm():
        swap.arrived(4)
        swap.arrived(3)

        branch = nn(r.ATT[...], r.WO[...])
        exchange(0, branch)
        swap.arrived(6)
        branch = branch + r.PX_R[0].astype(F32) + vector(2)
        normed, kept_values["inverse"] = normed_of(r.X[chip, :].astype(F32) + branch)
        r.N1[...] = normed
        hidden = normed * vector(3) + vector(4)
        r.HID[...] = hidden
        r.HL[...] = hidden.astype(BF16)

    def inner_layer():
        def inner_block(j, carry):
            where = pl.ds(at_128(j * QUARTER), QUARTER)
            value = nn(r.HL[...], r.WI[:, where]) + r.BIN[0:1, where]
            phi = 0.5 + 0.5 * lax.erf(value * (0.5**0.5))
            r.ACT[:, where] = (value * phi).astype(BF16)
            density = jnp.exp(value * value * -0.5) * 0.3989422804014327
            r.GP[:, where] = phi + value * density
            return carry

        lax.fori_loop(0, 4, inner_block, 0)

    def second_norm():
        swap.start(5, lambda: (r.WT.at[other_outer], r.WTR.at[:, mine_cols], p.sibling))
        r.WTR[:, mine_cols] = r.WT[outer_set, :]
        swap.arrived(5)

        def outer_block(j, carry):
            where = pl.ds(at_128(j * 256), 256)
            r.PART[:, where] = nn(r.ACT[...], r.WTR[:, where])
            return carry

        lax.fori_loop(0, 3, outer_block, 0)
        exchange(1, r.PART[...])
        swap.arrived(7)
        outer = r.PART[...] + r.PX_R[1].astype(F32) + vector(5)
        normed2, inverse2 = normed_of(r.HID[...] + outer)
        r.HID[...] = normed2 * vector(6) + vector(7)
        r.out[...] = r.HID[own_half, :].astype(BF16)
        grad_out = r.OG[...].astype(F32)
        grad_resid2 = normed_back(grad_out * vector(6), normed2, inverse2)
        r.HID[...] = grad_resid2
        grad_outer = grad_resid2.astype(BF16)
        r.GO[...] = grad_outer

        r.SV[...] = jnp.zeros_like(r.SV)
        r.SV[6:7, :] = column_sum(grad_out * normed2)
        r.SV[7:8, :] = column_sum(grad_out)
        r.SV[5:6, :] = column_sum(grad_outer.astype(F32))

    ri = Reduce(p, sems, r.GI, 48, "y", (r.GI1, r.GI2, r.GI3))
    rt = Reduce(p, sems, r.GT, 192, "x", (r.GT1, r.GT2, r.GT3))
    rw = Reduce(p, sems, r.GW, 48, "x", (r.GW1, r.GW2, r.GW3))
    rq = Reduce(p, sems, r.GQ, 48, "x", (r.GQ1, r.GQ2, r.GQ3))
    rk = Reduce(p, sems, r.GK, 48, "x", (r.GK1, r.GK2, r.GK3))
    rs = Reduce(p, sems, r.SG, 32, "y", (r.SG1, r.SG2, r.SG3))

    def back_piece(z, across):
        y = 1 - p.y if across else p.y
        return r.DO.at[pl.ds(at_128((y * 4 + z) * CHIP_ROWS), CHIP_ROWS)]

    def stat_piece(z, across):
        y = 1 - p.y if across else p.y
        return r.STAT.at[:, pl.ds(at_128((y * 4 + z) * CHIP_ROWS), CHIP_ROWS)]

    back = Gather(p, sems, back_piece, p.side["y"])
    stat = Gather(p, sems, stat_piece, p.side["y"])
    def outer_gradient():
        def outer_grads(j, carry):
            where = pl.ds(at_128(j * QUARTER), QUARTER)
            mine_rows = pl.ds(at_128(FF_CORE * c + j * QUARTER), QUARTER)
            r.GT_S[where, :] = tn(r.ACT[:, where], r.GO[:, other_cols]).astype(BF16)
            r.GT[mine_rows, :] = tn(r.ACT[:, where], r.GO[:, mine_cols]).astype(BF16)
            return carry

        lax.fori_loop(0, 4, outer_grads, 0)
        swap.start(10, lambda: (r.GT_S, r.GT.at[outer_set], p.sibling))

    def inner_back():
        def inner_back(j, carry):
            where = pl.ds(at_128(j * QUARTER), QUARTER)
            grad = (nt(r.GO[...], r.WTR[where, :]) * r.GP[:, where]).astype(BF16)
            r.GIN[:, where] = grad
            r.BIN[1:2, where] = jnp.sum(grad.astype(F32), axis=0, keepdims=True)
            return carry

        lax.fori_loop(0, 4, inner_back, 0)
        for u in (0, 1):
            r.SV[pl.ds(8 + 2 * c + u, 1), :] = r.BIN[1:2, D * u : D * (u + 1)]

    def inner_gradient():
        def inner_grads(j, carry):
            where = pl.ds(at_128(j * QUARTER), QUARTER)
            r.GI[:, where] = tn(r.HL[...], r.GIN[:, where]).astype(BF16)
            return carry

        lax.fori_loop(0, 4, inner_grads, 0)

    def hidden_back():
        def hidden_back(j, carry):
            where = pl.ds(at_128(j * 256), 256)
            r.PART[:, where] = nt(r.GIN[...], r.WI[where, :])
            return carry

        lax.fori_loop(0, 3, hidden_back, 0)
        exchange(2, r.PART[...])

    def first_norm_back():
        swap.arrived(8)
        grad_hidden = r.HID[...] + r.PART[...] + r.PX_R[2].astype(F32)
        normed = r.N1[...]
        grad_resid1 = normed_back(grad_hidden * vector(3), normed, kept_values["inverse"])
        r.SV[3:4, :] = column_sum(grad_hidden * normed)
        r.SV[4:5, :] = column_sum(grad_hidden)
        r.HID[...] = grad_resid1
        grad_branch = grad_resid1.astype(BF16)
        r.GB[...] = grad_branch
        r.SV[2:3, :] = column_sum(grad_branch.astype(F32))
        grad_attended = nt(grad_branch, r.WO[...]).astype(BF16)
        r.DO[chip, :] = grad_attended
        attended = r.ATT[...].astype(F32)
        product = grad_attended.astype(F32) * attended
        for head in range(CORE_HEADS):
            pair = slice(128 * (head // 2), 128 * (head // 2) + 128)
            delta = jnp.sum(jnp.where(in_head[head % 2], product[:, pair], 0.0), axis=1, keepdims=True)
            r.DELTA[...] = jnp.where(lanes128 == head, delta, r.DELTA[...])
        chip_lanes = pl.ds(at_128(chip_base), CHIP_ROWS)
        r.STAT[0:8, chip_lanes] = jnp.transpose(r.LSE[...])[0:8, :]
        r.STAT[8:16, chip_lanes] = jnp.transpose(r.DELTA[...])[0:8, :]

        back.begin()
        stat.begin()

    def output_gradient():
        r.GW_S[...] = tn(r.ATT[...], r.GB[:, other_cols]).astype(BF16)
        r.GW[row_set, :] = tn(r.ATT[...], r.GB[:, mine_cols]).astype(BF16)
        swap.start(11, lambda: (r.GW_S, r.GW.at[row_set], p.sibling))

    def query_back(pair):
        query_doc = r.QE[chip, :]
        queries = r.QKV[chip, pair_cols(0, pair)]
        keys = r.QKV[:, pair_cols(QUARTER, pair)]
        keys_doc = jnp.concatenate([keys, r.KE[...]], axis=1)
        values = r.QKV[:, pair_cols(2 * QUARTER, pair)]
        grads = r.DO[chip, pair_cols(0, pair)]
        outputs = []
        for e in (0, 1):
            pick = lanes128 == 2 * pair + e
            log_total = jnp.sum(jnp.where(pick, r.LSE[...], 0.0), axis=1, keepdims=True)
            delta = jnp.sum(jnp.where(pick, r.DELTA[...], 0.0), axis=1, keepdims=True)
            query = jnp.concatenate([masked(queries, e, 0.125), query_doc], axis=1)
            probs = jnp.exp(nt(query, keys_doc) - log_total)
            grad_probs = nt(masked(grads, e), values)
            grad_scores = (probs * (grad_probs - delta)).astype(BF16)
            outputs.append(nn(grad_scores, keys) * 0.125)
        r.DQKV[:, pair_cols(0, pair)] = jnp.where(in_head[0], outputs[0], outputs[1]).astype(BF16)

    def query_gradient():
        r.GQ[...] = tn(r.X[chip, :], r.DQKV[:, 0:QUARTER]).astype(BF16)

    def key_back(pair):
        key_doc = r.KE[chip, :]
        keys = r.QKV[chip, pair_cols(QUARTER, pair)]
        values = r.QKV[chip, pair_cols(2 * QUARTER, pair)]
        queries = r.QKV[:, pair_cols(0, pair)]
        queries_doc = jnp.concatenate([queries, r.QE[...]], axis=1)
        grads = r.DO[:, pair_cols(0, pair)]
        key_grads, value_grads = [], []
        for e in (0, 1):
            log_total = r.STAT[pl.ds(2 * pair + e, 1), :]
            delta = r.STAT[pl.ds(8 + 2 * pair + e, 1), :]
            key = jnp.concatenate([masked(keys, e, 0.125), key_doc], axis=1)
            probs = jnp.exp(nt(key, queries_doc) - log_total)
            value_grads.append(nn(probs.astype(BF16), grads))
            grad_probs = nt(masked(values, e), grads)
            grad_scores = (probs * (grad_probs - delta)).astype(BF16)
            key_grads.append(nn(grad_scores, queries) * 0.125)
        r.DQKV[:, pair_cols(QUARTER, pair)] = jnp.where(
            in_head[0], key_grads[0], key_grads[1]
        ).astype(BF16)
        r.DQKV[:, pair_cols(2 * QUARTER, pair)] = jnp.where(
            in_head[0], value_grads[0], value_grads[1]
        ).astype(BF16)

    def key_gradients():
        def project_grads(j, carry):
            where = pl.ds(at_128(j * QUARTER), QUARTER)
            source = pl.ds(at_128((j + 1) * QUARTER), QUARTER)
            r.GK[:, where] = tn(r.X[chip, :], r.DQKV[:, source]).astype(BF16)
            return carry

        lax.fori_loop(0, 2, project_grads, 0)

    def tokens_gradient():
        def tokens_back(j, carry):
            where = pl.ds(at_128(j * 256), 256)
            r.PART[:, where] = nt(r.DQKV[...], r.WA[where, 0:1152])
            return carry

        lax.fori_loop(0, 3, tokens_back, 0)
        r.PX_S[3, 0:128, :] = r.PART[sibling_half, :].astype(BF16)
        swap.start(9, lambda: (r.PX_S.at[3, pl.ds(0, 128)], r.PX_R.at[3, pl.ds(0, 128)], p.sibling))

        r.SV[0:1, mine_cols] = jnp.sum(r.DQKV[:, 0:QUARTER].astype(F32), axis=0, keepdims=True)
        r.SV[1:2, mine_cols] = jnp.sum(r.DQKV[:, 2 * QUARTER :].astype(F32), axis=0, keepdims=True)
        by_96, in_96 = lax.div(column, 96), lax.rem(column, 96)
        gather_96 = jnp.where(row_iota((128, D)) == in_96, 1.0, 0.0).astype(BF16)
        sums = jnp.broadcast_to(r.SV[...].reshape(1, 16, D), (32, 16, D)).reshape(512, D)
        late = kind >= 8
        wanted = jnp.where(late, 8 * (kind - 8) + by_96, by_24) == owner
        sums = jnp.where(wanted, sums, 0.0)
        high = sums.astype(BF16)
        low_part = (sums - high.astype(F32)).astype(BF16)
        r.SG[...] = jnp.where(
            late,
            nt(high, gather_96) + nt(low_part, gather_96),
            nt(high, spread) + nt(low_part, spread),
        )

    r.LSE[...] = jnp.zeros_like(r.LSE)
    r.DELTA[...] = jnp.zeros_like(r.DELTA)
    forward = [
        first(tok), take_weights, second(ga, gs), z_start(ga, gs), first(gi), first(ga, gs),
        first(gt), second(tok), second(gi), z_start(gt), mark_documents, across(0, tok),
        hop(1, ga, gs), z_start(tok), hop(2, ga, gs), across(0, ga, gs), hop(1, tok),
        across(1, ga, gs), across(2, ga, gs), hop(3, ga, gs), z_start(gi), second(gt),
        across(3, ga, gs), hop(2, tok), hop(3, tok), hop(1, gi), hop(1, gt), across(1, tok),
        across(0, gi), across(2, tok), hop(2, gi), spread_vectors, across(3, tok), hop(2, gt),
        across(0, gt), tok.complete, hop(3, gi),
        loop(
            project,
            [],
            [
                hop(3, gt), across(1, gi), across(1, gt),
            ],
            [],
        ),
        loop(
            attend,
            [
                across(2, gi), across(2, gt),
            ],
            [],
        ),
        first_norm, across(3, gt), across(3, gi), gi.complete, inner_layer, gt.complete,
        second_norm,
    ]
    backward = [
        inner_back, inner_gradient, one(ri), outer_gradient, lambda: swap.arrived(10), one(rt),
        hidden_back, first_norm_back,
        loop(
            query_back,
            [
                two(ri, 2), two(ri, 1),
            ],
            [
                hop(1, back, stat),
            ],
        ),
        hop(2, back, stat), hop(3, back, stat), output_gradient, two(rt, 2), across(0, back, stat),
        two(rt, 3), two(ri, 3), two(rt, 1), three(ri, 2), three(ri, 1), lambda: swap.arrived(11),
        one(rw), across(1, back, stat), two(rt, 0), two(rw, 1), query_gradient, one(rq),
        three(ri, 3), across(2, back, stat), across(3, back, stat),
        loop(
            key_back,
            [],
            [
                three(rt, 2),
            ],
        ),
        key_gradients, one(rk), two(rw, 2), two(rw, 0), three(rt, 1), two(ri, 0), two(rw, 3),
        two(rq, 0), two(rq, 3), two(rk, 1), three(rt, 0), three(rw, 2), two(rq, 2), three(rw, 1),
        three(rt, 3), three(rw, 0), three(rq, 0), two(rk, 2), three(rq, 3), three(rq, 2),
        two(rq, 1), two(rk, 3), three(rw, 3), three(rk, 1), three(rk, 2), three(rq, 1), two(rk, 0),
        tokens_gradient, one(rs), three(rk, 0), three(ri, 0), three(rk, 3), two(rs, 1), two(rs, 2),
        two(rs, 3), two(rs, 0), three(rs, 1), three(rs, 2), three(rs, 3), three(rs, 0),
    ]
    for step in forward + backward:
        step()

    last = Mover(sems, 6)
    finals = (
        (ri, r.FI, r.FI_R, 24),
        (rt, r.FT, r.FT_R, 96),
        (rw, r.FW, r.FW_R, 24),
        (rq, r.FQ, r.FQ_R, 24),
        (rk, r.FK, r.FK_R, 24),
        (rs, r.FS, r.FS_R, 16),
    )
    for index, (reduce, total, came, rows) in enumerate(finals):
        total[...] = reduce.result()

        def part(total=total, came=came, rows=rows):
            return total.at[pl.ds(at_8(rows * other), rows)], came, p.sibling

        last.start(index, part)

    swap.arrived(9)
    r.tgrad[...] = (
        r.HID[own_half, :] + r.PART[own_half, :] + r.PX_R[3, 0:128, :].astype(F32)
    ).astype(BF16)

    kept24 = pl.ds(at_8(24 * c), 24)
    last.arrived(0)
    r.gi[:, pl.ds(at_128(FF_CORE * c), FF_CORE)] = r.FI[kept24, :]
    r.gi[:, pl.ds(at_128(FF_CORE * other), FF_CORE)] = r.FI_R[...]
    last.arrived(1)
    r.gt[:, mine_cols] = r.FT[pl.ds(at_8(96 * c), 96), :]
    r.gt[:, other_cols] = r.FT_R[...]
    last.arrived(2)
    r.go[:, mine_cols] = r.FW[kept24, :]
    r.go[:, other_cols] = r.FW_R[...]
    last.arrived(3)
    r.gq[:, mine_cols] = r.FQ[kept24, :]
    r.gq[:, other_cols] = r.FQ_R[...]
    last.arrived(4)
    for index, ref in enumerate((r.gk, r.gv)):
        where = slice(QUARTER * index, QUARTER * (index + 1))
        ref[:, mine_cols] = r.FK[kept24, where]
        ref[:, other_cols] = r.FK_R[:, where]
    last.arrived(5)
    totals = r.FS[pl.ds(at_8(16 * c), 16), :] + r.FS_R[...]
    inner_total = totals[8:9] + totals[9:10] + totals[10:11] + totals[11:12]
    r.gs[0:8, :] = totals[0:8]
    r.gs[8:16, :] = jnp.broadcast_to(inner_total, (8, 128))

    for mover in (swap, tok, gs, ga, gi, gt, back, stat, ri, rt, rw, rq, rk, rs, last):
        mover.sent()


def hand_out(*refs):
    count = len(refs) // 2
    for source, target in zip(refs[:count], refs[count:]):
        target[...] = source[...]


def slice_body(
    tokens, query_weight, query_bias, key_weight, value_weight, value_bias, output_weight, output_bias,
    first_gain, first_shift, inner_weight, inner_bias, outer_weight, outer_bias, second_gain,
    second_shift, doc_starts, out_grad,
):
    vectors = jnp.stack(
        [
            query_bias, value_bias, output_bias, first_gain, first_shift, outer_bias,
            second_gain, second_shift,
        ]
        + [inner_bias[24 * part : 24 * part + 24] for part in range(4)]
    )
    small = jnp.pad(vectors, ((0, 4), (0, 104)))
    shape = jax.ShapeDtypeStruct
    vmem = pl.BlockSpec(memory_space=pltpu.VMEM)
    out_shapes = (
        shape((128, D), BF16), shape((128, D), BF16), shape((24, D), F32), shape((24, D), F32),
        shape((24, D), F32), shape((24, D), F32), shape((24, 3072), F32), shape((96, D), F32),
        shape((16, 128), F32),
    )
    results = pl.pallas_call(
        layer_kernel,
        out_shape=out_shapes,
        in_specs=[vmem] * 9 + [pl.BlockSpec(memory_space=pltpu.SMEM)],
        out_specs=[vmem] * 9,
        scratch_shapes=[pltpu.VMEM(*entry) for entry in SCRATCH.values()]
        + [pltpu.SemaphoreType.DMA((SEM_COUNT,)), pltpu.SemaphoreType.DMA((SEM_COUNT,))],
        compiler_params=pltpu.CompilerParams(
            collective_id=0, has_side_effects=True, vmem_limit_bytes=62 * 2**20
        ),
        name="layer",
    )(
        tokens, out_grad, query_weight, key_weight, value_weight, output_weight, inner_weight,
        outer_weight, small, doc_starts,
    )
    out, tgrad, gq, gk, gv, go, gi, gt = pl.pallas_call(
        hand_out,
        out_shape=out_shapes[:8],
        in_specs=[vmem] * 8,
        out_specs=[vmem] * 8,
        name="hand_out",
    )(*results[:8])
    gs = results[8]
    v = lambda row: gs[row, :24]
    return (
        out, tgrad, gq, v(0), gk, gv, v(1), go, v(2), v(3), v(4), gi, gs[8, :96], gt, v(5), v(6), v(7)
    )


def solution(mesh):
    rows, flat = P(("head", "blk"), None), P(("head", "blk"))
    in_specs = (
        rows, rows, flat, rows, rows, flat, rows, flat, flat, flat, rows, flat, rows, flat, flat, flat,
        P(), rows,
    )
    out_specs = (
        rows, rows, rows, flat, rows, rows, flat, rows, flat, flat, flat, rows, flat, rows, flat, flat,
        flat,
    )
    small_slice = mesh.shape["head"] == 2 and mesh.shape["blk"] == 16
    return jax.shard_map(
        slice_body if small_slice else body,
        mesh=mesh,
        in_specs=in_specs,
        out_specs=out_specs,
        check_vma=False,
    )
```

```python
from functools import partial

import jax
import jax.numpy as jnp
from jax import lax
from jax.experimental import pallas as pl
from jax.experimental.pallas import tpu as pltpu
from jax.sharding import PartitionSpec as P

HEAD_DIM = 64


LN_EPS = 1e-12
MASKED_SCORE = -1e30


def doc_numbers(doc_starts, positions):
    covered = (doc_starts[None, :] <= positions[:, None]).astype(jnp.int32)
    return (jnp.sum(covered, axis=1) - 1).astype(jnp.float32)


def dense_product(left_side, right_side):
    return jnp.dot(left_side, right_side, preferred_element_type=jnp.float32)


def product_back(left_side, right_side):
    return lax.dot_general(
        left_side, right_side, (((1,), (1,)), ((), ())), preferred_element_type=jnp.float32
    )


def product_left(left_side, right_side):
    return lax.dot_general(
        left_side, right_side, (((0,), (0,)), ((), ())), preferred_element_type=jnp.float32
    )


def norm_forward(residual, scale_gain, shift_bias):
    row_mean = jnp.mean(residual, axis=-1, keepdims=True)
    centred = residual - row_mean
    variance = jnp.mean(centred * centred, axis=-1, keepdims=True)
    inverse = lax.rsqrt(variance + LN_EPS)
    normed = centred * inverse
    return (normed * scale_gain + shift_bias, normed, inverse)


def norm_backward(grad_output, normed, inverse, scale_gain):
    grad_normed = grad_output * scale_gain
    first_term = jnp.mean(grad_normed, axis=-1, keepdims=True)
    second_term = jnp.mean(grad_normed * normed, axis=-1, keepdims=True)
    grad_input = inverse * (grad_normed - first_term - normed * second_term)
    return (grad_input, jnp.sum(grad_output * normed, axis=0), jnp.sum(grad_output, axis=0))


def split_blocks(rows_array, block_rows):
    return rows_array.reshape(-1, block_rows, rows_array.shape[1] // HEAD_DIM, HEAD_DIM)


def blocks_to_rows(blocked):
    reordered = jnp.transpose(blocked, (0, 2, 1, 3))
    return reordered.reshape(-1, blocked.shape[1] * blocked.shape[3])


def block_scores(query_block, key_block, query_docs, key_docs):
    scores = jnp.einsum(
        "qhd,khd->hqk", query_block, key_block, preferred_element_type=jnp.float32
    ) * HEAD_DIM ** (-0.5)
    allowed = (query_docs[:, None] == key_docs[None, :])[None, :, :]
    return (scores, allowed)


def intersecting(first_docs, second_docs):
    return jnp.logical_and(
        jnp.max(first_docs) >= jnp.min(second_docs), jnp.min(first_docs) <= jnp.max(second_docs)
    )


def keep_state(carried):
    return carried


def forward_update(carried, query_block, query_docs, key_block, value_block, key_docs):
    running_max, row_total, accumulated = carried
    scores, allowed = block_scores(query_block, key_block, query_docs, key_docs)
    scores = jnp.where(allowed, scores, MASKED_SCORE)
    new_max = jnp.maximum(running_max, jnp.max(scores, axis=2))
    decay_factor = jnp.exp(running_max - new_max)
    weights = jnp.where(allowed, jnp.exp(scores - new_max[:, :, None]), 0.0)
    row_total = row_total * decay_factor + jnp.sum(weights, axis=2)
    update = jnp.einsum(
        "hqk,khd->hqd",
        weights.astype(jnp.bfloat16),
        value_block,
        preferred_element_type=jnp.float32,
    )
    return (new_max, row_total, accumulated * decay_factor[:, :, None] + update)


def forward_folder(query_blocks, doc_blocks):
    block_rows = query_blocks.shape[1]

    def forward_fold_step(carried_in, pieces, start_row):
        key_piece, value_piece, key_doc_piece = pieces
        key_blocks = split_blocks(key_piece, block_rows)
        value_blocks = split_blocks(value_piece, block_rows)
        key_doc_blocks = key_doc_piece.astype(jnp.float32).reshape(-1, block_rows)

        def forward_one_block(block_index, carried):
            key_docs = key_doc_blocks[block_index]
            results = []
            for query_index in range(query_blocks.shape[0]):
                current = tuple((member[query_index] for member in carried))
                update = partial(
                    forward_update,
                    query_block=query_blocks[query_index],
                    query_docs=doc_blocks[query_index],
                    key_block=key_blocks[block_index],
                    value_block=value_blocks[block_index],
                    key_docs=key_docs,
                )
                results.append(
                    lax.cond(
                        intersecting(doc_blocks[query_index], key_docs), update, keep_state, current
                    )
                )
            return tuple((jnp.stack([entry[member] for entry in results]) for member in range(3)))

        return lax.fori_loop(0, key_blocks.shape[0], forward_one_block, carried_in)

    return forward_fold_step


def query_grad_update(
    grad_query,
    query_block,
    query_docs,
    grad_block,
    log_total,
    delta_rows,
    key_block,
    value_block,
    key_docs,
):
    scores, allowed = block_scores(query_block, key_block, query_docs, key_docs)
    probs = jnp.where(allowed, jnp.exp(scores - log_total[:, :, None]), 0.0)
    grad_probs = jnp.einsum(
        "qhd,khd->hqk", grad_block, value_block, preferred_element_type=jnp.float32
    )
    grad_scores = (probs * (grad_probs - delta_rows[:, :, None])).astype(jnp.bfloat16)
    return grad_query + jnp.einsum(
        "hqk,khd->hqd", grad_scores, key_block, preferred_element_type=jnp.float32
    ) * HEAD_DIM ** (-0.5)


def query_grad_folder(query_blocks, doc_blocks, grad_blocks, log_blocks, delta_blocks):
    block_rows = query_blocks.shape[1]

    def query_fold_step(carried_in, pieces, start_row):
        key_piece, value_piece, key_doc_piece = pieces
        key_blocks = split_blocks(key_piece, block_rows)
        value_blocks = split_blocks(value_piece, block_rows)
        key_doc_blocks = key_doc_piece.astype(jnp.float32).reshape(-1, block_rows)

        def query_one_block(block_index, carried):
            key_docs = key_doc_blocks[block_index]
            results = []
            for query_index in range(query_blocks.shape[0]):
                update = partial(
                    query_grad_update,
                    query_block=query_blocks[query_index],
                    query_docs=doc_blocks[query_index],
                    grad_block=grad_blocks[query_index],
                    log_total=log_blocks[query_index],
                    delta_rows=delta_blocks[query_index],
                    key_block=key_blocks[block_index],
                    value_block=value_blocks[block_index],
                    key_docs=key_docs,
                )
                results.append(
                    lax.cond(
                        intersecting(doc_blocks[query_index], key_docs),
                        update,
                        keep_state,
                        carried[query_index],
                    )
                )
            return jnp.stack(results)

        return lax.fori_loop(0, key_blocks.shape[0], query_one_block, carried_in)

    return query_fold_step


def key_grad_update(
    carried,
    key_block,
    value_block,
    key_docs,
    query_block,
    grad_block,
    log_total,
    delta_rows,
    query_docs,
):
    grad_key, grad_value = carried
    scores, allowed = block_scores(query_block, key_block, query_docs, key_docs)
    probs = jnp.where(allowed, jnp.exp(scores - log_total[:, :, None]), 0.0)
    grad_value = grad_value + jnp.einsum(
        "hqk,qhd->hkd", probs.astype(jnp.bfloat16), grad_block, preferred_element_type=jnp.float32
    )
    grad_probs = jnp.einsum(
        "qhd,khd->hqk", grad_block, value_block, preferred_element_type=jnp.float32
    )
    grad_scores = (probs * (grad_probs - delta_rows[:, :, None])).astype(jnp.bfloat16)
    grad_key = grad_key + jnp.einsum(
        "hqk,qhd->hkd", grad_scores, query_block, preferred_element_type=jnp.float32
    ) * HEAD_DIM ** (-0.5)
    return (grad_key, grad_value)


def key_grad_folder(key_blocks, value_blocks, doc_blocks):
    block_rows = key_blocks.shape[1]

    def key_fold_step(carried_in, pieces, start_row):
        query_piece, grad_piece, log_piece, delta_piece, doc_piece = pieces
        query_blocks = split_blocks(query_piece.astype(jnp.bfloat16), block_rows)
        grad_blocks = split_blocks(grad_piece.astype(jnp.bfloat16), block_rows)
        log_blocks = jnp.transpose(log_piece.reshape(-1, block_rows, log_piece.shape[1]), (0, 2, 1))
        delta_blocks = jnp.transpose(
            delta_piece.reshape(-1, block_rows, delta_piece.shape[1]), (0, 2, 1)
        )
        query_doc_blocks = doc_piece.reshape(-1, block_rows)

        def key_one_block(block_index, carried):
            query_docs = query_doc_blocks[block_index]
            results = []
            for key_index in range(key_blocks.shape[0]):
                current = (carried[0][key_index], carried[1][key_index])
                update = partial(
                    key_grad_update,
                    key_block=key_blocks[key_index],
                    value_block=value_blocks[key_index],
                    key_docs=doc_blocks[key_index],
                    query_block=query_blocks[block_index],
                    grad_block=grad_blocks[block_index],
                    log_total=log_blocks[block_index],
                    delta_rows=delta_blocks[block_index],
                    query_docs=query_docs,
                )
                results.append(
                    lax.cond(
                        intersecting(query_docs, doc_blocks[key_index]), update, keep_state, current
                    )
                )
            return (
                jnp.stack([entry[0] for entry in results]),
                jnp.stack([entry[1] for entry in results]),
            )

        return lax.fori_loop(0, query_blocks.shape[0], key_one_block, carried_in)

    return key_fold_step


def attention_forward(query_rows, key_rows, value_rows, row_docs, block_rows):
    query_blocks = split_blocks(query_rows, block_rows)
    doc_blocks = row_docs.reshape(-1, block_rows)
    block_count = query_blocks.shape[0]
    head_count = query_blocks.shape[2]
    send_docs = row_docs.astype(jnp.bfloat16)
    start_state = (
        jnp.full((block_count, head_count, block_rows), MASKED_SCORE, jnp.float32),
        jnp.zeros((block_count, head_count, block_rows), jnp.float32),
        jnp.zeros((block_count, head_count, block_rows, HEAD_DIM), jnp.float32),
    )
    fold_forward = forward_folder(query_blocks, doc_blocks)
    running_max, row_total, accumulated = fold_forward(
        start_state,
        (
            lax.all_gather(key_rows, "blk", axis=0, tiled=True),
            lax.all_gather(value_rows, "blk", axis=0, tiled=True),
            lax.all_gather(send_docs, "blk", axis=0, tiled=True),
        ),
        jnp.int32(0),
    )
    head_outputs = blocks_to_rows(accumulated / row_total[:, :, :, None]).astype(jnp.bfloat16)
    log_total = running_max + jnp.log(row_total)
    return (head_outputs, log_total)


def attention_backward(
    grad_rows, head_outputs, log_total, query_rows, key_rows, value_rows, row_docs, block_rows
):
    query_blocks = split_blocks(query_rows, block_rows)
    key_blocks = split_blocks(key_rows, block_rows)
    value_blocks = split_blocks(value_rows, block_rows)
    doc_blocks = row_docs.reshape(-1, block_rows)
    block_count = query_blocks.shape[0]
    head_count = query_blocks.shape[2]
    send_docs = row_docs.astype(jnp.bfloat16)
    grad_blocks = split_blocks(grad_rows, block_rows)
    output_blocks = split_blocks(head_outputs, block_rows)
    delta_blocks = jnp.einsum(
        "nqhd,nqhd->nhq", grad_blocks.astype(jnp.float32), output_blocks.astype(jnp.float32)
    )
    log_rows = jnp.transpose(log_total, (0, 2, 1)).reshape(-1, head_count)
    delta_rows = jnp.transpose(delta_blocks, (0, 2, 1)).reshape(-1, head_count)
    fold_queries = query_grad_folder(query_blocks, doc_blocks, grad_blocks, log_total, delta_blocks)
    fold_keys = key_grad_folder(key_blocks, value_blocks, doc_blocks)
    query_start = jnp.zeros((block_count, head_count, block_rows, HEAD_DIM), jnp.float32)
    key_start = (query_start, query_start)
    query_send = (
        query_rows.astype(jnp.float32),
        grad_rows.astype(jnp.float32),
        log_rows,
        delta_rows,
        row_docs,
    )
    grad_query_state = fold_queries(
        query_start,
        (
            lax.all_gather(key_rows, "blk", axis=0, tiled=True),
            lax.all_gather(value_rows, "blk", axis=0, tiled=True),
            lax.all_gather(send_docs, "blk", axis=0, tiled=True),
        ),
        jnp.int32(0),
    )
    grad_key_state, grad_value_state = fold_keys(
        key_start,
        (
            lax.all_gather(query_send[0], "blk", axis=0, tiled=True),
            lax.all_gather(query_send[1], "blk", axis=0, tiled=True),
            lax.all_gather(query_send[2], "blk", axis=0, tiled=True),
            lax.all_gather(query_send[3], "blk", axis=0, tiled=True),
            lax.all_gather(query_send[4], "blk", axis=0, tiled=True),
        ),
        jnp.int32(0),
    )
    return (
        blocks_to_rows(grad_query_state).astype(jnp.bfloat16),
        blocks_to_rows(grad_key_state).astype(jnp.bfloat16),
        blocks_to_rows(grad_value_state).astype(jnp.bfloat16),
    )


def data_layer(tokens, full, row_docs, out_grad, block_rows):
    (
        full_query,
        full_query_bias,
        full_key,
        full_value,
        full_value_bias,
        full_output,
        full_output_bias,
        full_first_gain,
        full_first_shift,
        full_inner,
        full_inner_bias,
        full_outer,
        full_outer_bias,
        full_second_gain,
        full_second_shift,
    ) = full
    queries = (dense_product(tokens, full_query) + full_query_bias.astype(jnp.float32)).astype(
        jnp.bfloat16
    )
    keys_local = dense_product(tokens, full_key).astype(jnp.bfloat16)
    values_local = (dense_product(tokens, full_value) + full_value_bias.astype(jnp.float32)).astype(
        jnp.bfloat16
    )
    query_rows, key_rows, value_rows = (
        lax.all_to_all(queries, "head", split_axis=1, concat_axis=0, tiled=True),
        lax.all_to_all(keys_local, "head", split_axis=1, concat_axis=0, tiled=True),
        lax.all_to_all(values_local, "head", split_axis=1, concat_axis=0, tiled=True),
    )
    head_outputs, log_total = attention_forward(
        query_rows, key_rows, value_rows, row_docs, block_rows
    )
    attended = lax.all_to_all(head_outputs, "head", split_axis=0, concat_axis=1, tiled=True)
    branch = dense_product(attended, full_output) + full_output_bias.astype(jnp.float32)
    hidden, first_normed, first_inverse = norm_forward(
        tokens.astype(jnp.float32) + branch,
        full_first_gain.astype(jnp.float32),
        full_first_shift.astype(jnp.float32),
    )
    hidden_low = hidden.astype(jnp.bfloat16)
    inner_value = dense_product(hidden_low, full_inner) + full_inner_bias.astype(jnp.float32)
    activated_full, gelu_pullback = jax.vjp(partial(jax.nn.gelu, approximate=False), inner_value)
    activated = activated_full.astype(jnp.bfloat16)
    outer_value = dense_product(activated, full_outer) + full_outer_bias.astype(jnp.float32)
    layer_full, second_normed, second_inverse = norm_forward(
        hidden + outer_value,
        full_second_gain.astype(jnp.float32),
        full_second_shift.astype(jnp.float32),
    )
    layer_out = layer_full.astype(jnp.bfloat16)
    grad_output = out_grad.astype(jnp.float32)
    grad_resid2, second_gain_term, second_shift_term = norm_backward(
        grad_output, second_normed, second_inverse, full_second_gain.astype(jnp.float32)
    )
    grad_outer = grad_resid2.astype(jnp.bfloat16)
    outer_weight_term = product_left(activated, grad_outer)
    outer_bias_term = jnp.sum(grad_outer.astype(jnp.float32), axis=0)
    grad_inner = gelu_pullback(product_back(grad_outer, full_outer))[0].astype(jnp.bfloat16)
    inner_weight_term = product_left(hidden_low, grad_inner)
    inner_bias_term = jnp.sum(grad_inner.astype(jnp.float32), axis=0)
    grad_hidden = grad_resid2 + product_back(grad_inner, full_inner)
    grad_resid1, first_gain_term, first_shift_term = norm_backward(
        grad_hidden, first_normed, first_inverse, full_first_gain.astype(jnp.float32)
    )
    grad_branch = grad_resid1.astype(jnp.bfloat16)
    output_weight_term = product_left(attended, grad_branch)
    output_bias_term = jnp.sum(grad_branch.astype(jnp.float32), axis=0)
    grad_attended = product_back(grad_branch, full_output).astype(jnp.bfloat16)
    grad_rows = lax.all_to_all(grad_attended, "head", split_axis=1, concat_axis=0, tiled=True)
    grad_query_rows, grad_key_rows, grad_value_rows = attention_backward(
        grad_rows, head_outputs, log_total, query_rows, key_rows, value_rows, row_docs, block_rows
    )
    grad_queries, grad_keys, grad_values = (
        lax.all_to_all(grad_query_rows, "head", split_axis=0, concat_axis=1, tiled=True),
        lax.all_to_all(grad_key_rows, "head", split_axis=0, concat_axis=1, tiled=True),
        lax.all_to_all(grad_value_rows, "head", split_axis=0, concat_axis=1, tiled=True),
    )
    query_weight_term = product_left(tokens, grad_queries)
    query_bias_term = jnp.sum(grad_queries.astype(jnp.float32), axis=0)
    key_weight_term = product_left(tokens, grad_keys)
    value_weight_term = product_left(tokens, grad_values)
    value_bias_term = jnp.sum(grad_values.astype(jnp.float32), axis=0)
    tokens_grad = (
        grad_resid1
        + product_back(grad_queries, full_query)
        + product_back(grad_keys, full_key)
        + product_back(grad_values, full_value)
    ).astype(jnp.bfloat16)
    summed = (
        lax.psum_scatter(query_weight_term, ("head", "blk"), scatter_dimension=0, tiled=True),
        lax.psum_scatter(query_bias_term, ("head", "blk"), scatter_dimension=0, tiled=True),
        lax.psum_scatter(key_weight_term, ("head", "blk"), scatter_dimension=0, tiled=True),
        lax.psum_scatter(value_weight_term, ("head", "blk"), scatter_dimension=0, tiled=True),
        lax.psum_scatter(value_bias_term, ("head", "blk"), scatter_dimension=0, tiled=True),
        lax.psum_scatter(output_weight_term, ("head", "blk"), scatter_dimension=0, tiled=True),
        lax.psum_scatter(output_bias_term, ("head", "blk"), scatter_dimension=0, tiled=True),
        lax.psum_scatter(first_gain_term, ("head", "blk"), scatter_dimension=0, tiled=True),
        lax.psum_scatter(first_shift_term, ("head", "blk"), scatter_dimension=0, tiled=True),
        lax.psum_scatter(inner_weight_term, ("head", "blk"), scatter_dimension=0, tiled=True),
        lax.psum_scatter(inner_bias_term, ("head", "blk"), scatter_dimension=0, tiled=True),
        lax.psum_scatter(outer_weight_term, ("head", "blk"), scatter_dimension=0, tiled=True),
        lax.psum_scatter(outer_bias_term, ("head", "blk"), scatter_dimension=0, tiled=True),
        lax.psum_scatter(second_gain_term, ("head", "blk"), scatter_dimension=0, tiled=True),
        lax.psum_scatter(second_shift_term, ("head", "blk"), scatter_dimension=0, tiled=True),
    )
    return (layer_out, tokens_grad) + tuple(summed)


def body(
    tokens,
    query_weight,
    query_bias,
    key_weight,
    value_weight,
    value_bias,
    output_weight,
    output_bias,
    first_gain,
    first_shift,
    inner_weight,
    inner_bias,
    outer_weight,
    outer_bias,
    second_gain,
    second_shift,
    doc_starts,
    out_grad,
):
    shards = (
        query_weight,
        query_bias,
        key_weight,
        value_weight,
        value_bias,
        output_weight,
        output_bias,
        first_gain,
        first_shift,
        inner_weight,
        inner_bias,
        outer_weight,
        outer_bias,
        second_gain,
        second_shift,
    )
    full = (
        lax.all_gather(shards[0], ("head", "blk"), axis=0, tiled=True),
        lax.all_gather(shards[1], ("head", "blk"), axis=0, tiled=True),
        lax.all_gather(shards[2], ("head", "blk"), axis=0, tiled=True),
        lax.all_gather(shards[3], ("head", "blk"), axis=0, tiled=True),
        lax.all_gather(shards[4], ("head", "blk"), axis=0, tiled=True),
        lax.all_gather(shards[5], ("head", "blk"), axis=0, tiled=True),
        lax.all_gather(shards[6], ("head", "blk"), axis=0, tiled=True),
        lax.all_gather(shards[7], ("head", "blk"), axis=0, tiled=True),
        lax.all_gather(shards[8], ("head", "blk"), axis=0, tiled=True),
        lax.all_gather(shards[9], ("head", "blk"), axis=0, tiled=True),
        lax.all_gather(shards[10], ("head", "blk"), axis=0, tiled=True),
        lax.all_gather(shards[11], ("head", "blk"), axis=0, tiled=True),
        lax.all_gather(shards[12], ("head", "blk"), axis=0, tiled=True),
        lax.all_gather(shards[13], ("head", "blk"), axis=0, tiled=True),
        lax.all_gather(shards[14], ("head", "blk"), axis=0, tiled=True),
    )
    tok_rows = tokens.shape[0]
    half_length = tok_rows * lax.axis_size("blk")
    blk_place = lax.axis_index("blk")
    offsets = jnp.arange(tok_rows, dtype=jnp.int32)
    row_positions = jnp.concatenate(
        [blk_place * tok_rows + offsets, half_length + blk_place * tok_rows + offsets]
    )
    row_docs = doc_numbers(doc_starts, row_positions)
    return data_layer(tokens, full, row_docs, out_grad, tok_rows)


MESH = pl.DeviceIdType.MESH
F32 = jnp.float32
BF16 = jnp.bfloat16
D = 768
QUARTER = 384
FF_CORE = 1536
HALF_ROWS = 2048
CHIP_ROWS = 256
CORE_HEADS = 6
PENALTY = -1e30
FAR = 2**30


def nn(a, b):
    return lax.dot_general(a, b, (((1,), (0,)), ((), ())), preferred_element_type=F32)


def nt(a, b):
    return lax.dot_general(a, b, (((1,), (1,)), ((), ())), preferred_element_type=F32)


def tn(a, b):
    return lax.dot_general(a, b, (((0,), (0,)), ((), ())), preferred_element_type=F32)


def at_128(index):
    return pl.multiple_of(index, 128)


def at_16(index):
    return pl.multiple_of(index, 16)


def at_8(index):
    return pl.multiple_of(index, 8)


class Place:
    def __init__(self):
        self.x = lax.axis_index("head")
        b = lax.axis_index("blk")
        self.z = lax.div(b, 4)
        self.y = lax.rem(lax.div(b, 2), 2)
        self.c = lax.rem(b, 2)
        self.chip = self.x * 8 + self.z * 2 + self.y
        self.slot = self.y * 4 + self.z
        self.ups = [self.z] + [lax.rem(self.z + k, 4) for k in (1, 2, 3)]
        self.downs = [self.ups[0], self.ups[3], self.ups[2], self.ups[1]]
        self.above = self.device(z=jnp.minimum(self.z + 1, 3))
        self.below = self.device(z=jnp.maximum(self.z - 1, 0))
        self.can_up, self.can_down = self.z < 3, self.z > 0
        self.has_below = [None] + [self.z >= step for step in (1, 2, 3)]
        self.has_above = [None] + [self.z <= 3 - step for step in (1, 2, 3)]
        self.sibling = self.device(c=1 - self.c)
        self.side = {"x": self.device(x=1 - self.x), "y": self.device(y=1 - self.y)}

    def device(self, x=None, z=None, y=None, c=None):
        x = self.x if x is None else x
        z = self.z if z is None else z
        y = self.y if y is None else y
        c = self.c if c is None else c
        return (x, z * 4 + y * 2 + c)

    def up(self, k):
        return self.ups[k]

    def down(self, k):
        return self.downs[k]


class Sems:
    def __init__(self, send, recv):
        self.send, self.recv, self.used = send, recv, 0

    def take(self, count):
        first = self.used
        self.used += count
        assert self.used <= self.send.shape[0]
        return first


class Mover:
    def __init__(self, sems, count):
        self.sems, self.first, self.parts = sems, sems.take(count), {}

    def copy(self, index):
        place = self.first + index
        src, dst, device = self.parts[index]()
        return pltpu.make_async_remote_copy(
            src,
            dst,
            self.sems.send.at[place],
            self.sems.recv.at[place],
            device_id=device,
            device_id_type=MESH,
        )

    def start(self, index, part):
        self.parts[index] = part
        self.copy(index).start()

    def arrived(self, index):
        self.copy(index).wait_recv()

    def sent(self):
        for index in sorted(self.parts):
            self.copy(index).wait_send()


class Gather:
    def __init__(self, place, sems, piece, first, second=None):
        self.place, self.sems, self.piece = place, sems, piece
        self.device = {"up": place.above, "down": place.below, "first": first}
        if second is not None:
            self.device.update(second=second, across=second)
        self.slot = {kind: sems.take(4) for kind in self.device}

    def copy(self, kind, z):
        place = self.slot[kind] + z
        piece = self.piece(z, kind == "across")
        return pltpu.make_async_remote_copy(
            piece,
            piece,
            self.sems.send.at[place],
            self.sems.recv.at[place],
            device_id=self.device[kind],
            device_id_type=MESH,
        )

    def sideways(self, z):
        self.copy("first", z).start()
        if "second" in self.device:
            self.copy("second", z).start()

    def begin_z(self):
        p = self.place

        @pl.when(p.can_up)
        def _():
            self.copy("up", p.z).start()

        @pl.when(p.can_down)
        def _():
            self.copy("down", p.z).start()

    def begin(self):
        self.begin_z()
        self.sideways(self.place.z)

    def hop(self, step):
        p = self.place

        @pl.when(p.has_below[step])
        def _():
            z = p.z - step
            self.copy("up", z).wait_recv()

            @pl.when(p.can_up)
            def _():
                self.copy("up", z).start()

            self.sideways(z)

        @pl.when(p.has_above[step])
        def _():
            z = p.z + step
            self.copy("down", z).wait_recv()

            @pl.when(p.can_down)
            def _():
                self.copy("down", z).start()

            self.sideways(z)

    def across_one(self, z):
        self.copy("first", z).wait_recv()
        if "second" in self.device:
            self.copy("across", z).start()

    def across(self, step):
        p = self.place
        if step == 0:
            self.across_one(p.z)
            return

        @pl.when(p.has_below[step])
        def _():
            self.across_one(p.z - step)

        @pl.when(p.has_above[step])
        def _():
            self.across_one(p.z + step)

    def complete(self):
        for z in range(4):
            self.copy("second", z).wait_recv()
            self.copy("across", z).wait_recv()

    def sent(self):
        p = self.place
        for z in range(4):
            for kind in self.device:
                wait = self.copy(kind, z).wait_send
                if kind == "up":
                    pl.when(jnp.logical_and(p.can_up, p.z >= z))(wait)
                elif kind == "down":
                    pl.when(jnp.logical_and(p.can_down, p.z <= z))(wait)
                else:
                    wait()


class Reduce(Mover):
    def __init__(self, place, sems, ref, rows, first, slots):
        super().__init__(sems, 15)
        self.place, self.ref, self.rows, self.axis = place, ref, rows, first
        self.one, self.two, self.three = slots

    def rows_of(self, x, z, y, count=1):
        return pl.ds(at_8((x * 8 + z * 2 + y) * self.rows), count * self.rows)

    def send_one(self, k):
        p, R = self.place, self.rows
        if self.axis == "x":

            def part():
                where = self.rows_of(1 - p.x, p.up(k), 0, 2)
                return self.ref.at[where], self.one.at[k], p.side["x"]

            self.start(2 * k, part)
        else:
            for xx in (0, 1):

                def part(xx=xx):
                    where = self.rows_of(xx, p.up(k), 1 - p.y)
                    return self.ref.at[where], self.one.at[k, pl.ds(xx * R, R)], p.side["y"]

                self.start(2 * k + xx, part)

    def add(self, where, term):
        self.ref[where] = (self.ref[where].astype(F32) + term.astype(F32)).astype(self.ref.dtype)

    def send_two(self, k):
        p, R = self.place, self.rows
        if self.axis == "x":
            self.arrived(2 * k)
            self.add(self.rows_of(p.x, p.up(k), 0, 2), self.one[k])

            def part():
                where = self.rows_of(p.x, p.up(k), 1 - p.y)
                return self.ref.at[where], self.two.at[k], p.side["y"]

        else:
            for xx in (0, 1):
                self.arrived(2 * k + xx)
                self.add(self.rows_of(xx, p.up(k), p.y), self.one[k, xx * R : (xx + 1) * R])

            def part():
                where = self.rows_of(1 - p.x, p.up(k), p.y)
                return self.ref.at[where], self.two.at[k], p.side["x"]

        self.start(8 + k, part)

    def send_three(self, k):
        p = self.place
        self.arrived(8 + k)
        if k:
            self.add(self.rows_of(p.x, p.up(k), p.y), self.two[k])

            def part():
                where = self.rows_of(p.x, p.up(k), p.y)
                return self.ref.at[where], self.three.at[k - 1], p.device(z=p.up(k))

            self.start(12 + k - 1, part)

    def result(self):
        p = self.place
        total = self.ref[self.rows_of(p.x, p.z, p.y)].astype(F32) + self.two[0].astype(F32)
        for k in (1, 2, 3):
            self.arrived(12 + k - 1)
            total = total + self.three[k - 1].astype(F32)
        return total


def z_start(*gathers):
    return lambda: [gather.begin_z() for gather in gathers]


def first(*gathers):
    return lambda: [gather.copy("first", gather.place.z).start() for gather in gathers]


def second(*gathers):
    return lambda: [gather.copy("second", gather.place.z).start() for gather in gathers]


def hop(step, *gathers):
    return lambda: [gather.hop(step) for gather in gathers]


def across(step, *gathers):
    return lambda: [gather.across(step) for gather in gathers]


def one(*reduces):
    return lambda: [reduce.send_one(k) for k in ORDER for reduce in reduces]


def two(reduce, k):
    return lambda: reduce.send_two(k)


def three(reduce, k):
    return lambda: reduce.send_three(k)


def loop(action, *between):
    def run():
        def step(j, carry):
            for i, steps in enumerate(between):

                @pl.when(j == i + 1)
                def _(steps=steps):
                    for inside in steps:
                        inside()

            action(j)
            return carry

        lax.fori_loop(0, len(between) + 1, step, 0)

    return run


def row_mean(value):
    return jnp.sum(value, axis=1, keepdims=True) * (1.0 / D)


def normed_of(residual):
    centred = residual - row_mean(residual)
    inverse = lax.rsqrt(row_mean(centred * centred) + LN_EPS)
    return centred * inverse, inverse


def normed_back(grad_normed, normed, inverse):
    return inverse * (grad_normed - row_mean(grad_normed) - normed * row_mean(grad_normed * normed))


def lane_iota(shape):
    return lax.broadcasted_iota(jnp.int32, shape, len(shape) - 1)


def row_iota(shape):
    return lax.broadcasted_iota(jnp.int32, shape, 0)


SCRATCH = dict(
    X=((HALF_ROWS, D), BF16),
    SMALL=((16, 128), F32),
    WS=((512, 128), BF16),
    WA=((D, 1536), BF16),
    WI=((D, FF_CORE), BF16),
    WT=((2 * FF_CORE, QUARTER), BF16),
    WO=((QUARTER, D), BF16),
    WTR=((FF_CORE, D), BF16),
    OG=((CHIP_ROWS, D), BF16),
    SWAP_S=((24, 3072), F32),
    SWAP_R=((24, 3072), F32),
    QKV=((HALF_ROWS, 1152), BF16),
    QE=((HALF_ROWS, 128), BF16),
    KE=((HALF_ROWS, 128), BF16),
    ATT=((CHIP_ROWS, QUARTER), BF16),
    LSE=((CHIP_ROWS, 128), F32),
    DELTA=((CHIP_ROWS, 128), F32),
    VEC=((16, D), F32),
    BIN=((8, FF_CORE), F32),
    DO=((HALF_ROWS, QUARTER), BF16),
    STAT=((16, HALF_ROWS), F32),
    PX_S=((4, CHIP_ROWS, D), BF16),
    PX_R=((4, CHIP_ROWS, D), BF16),
    PART=((CHIP_ROWS, D), F32),
    HID=((CHIP_ROWS, D), F32),
    N1=((CHIP_ROWS, D), F32),
    HL=((CHIP_ROWS, D), BF16),
    ACT=((CHIP_ROWS, FF_CORE), BF16),
    GP=((CHIP_ROWS, FF_CORE), F32),
    GV=((CHIP_ROWS, FF_CORE), F32),
    GIN=((CHIP_ROWS, FF_CORE), BF16),
    GO=((CHIP_ROWS, D), BF16),
    GB=((CHIP_ROWS, D), BF16),
    DQKV=((CHIP_ROWS, 1152), BF16),
    SV=((16, D), F32),
    GI=((D, 1152), BF16),
    GJ=((D, QUARTER), BF16),
    GT=((2 * FF_CORE, QUARTER), BF16),
    GT_S=((FF_CORE, QUARTER), BF16),
    GW=((D, QUARTER), BF16),
    GW_S=((QUARTER, QUARTER), BF16),
    GQ=((D, QUARTER), BF16),
    GK=((D, D), BF16),
    SG=((512, 128), F32),
    GI1=((4, 96, 1152), BF16),
    GI2=((4, 48, 1152), BF16),
    GI3=((3, 48, 1152), BF16),
    GJ1=((4, 96, QUARTER), BF16),
    GJ2=((4, 48, QUARTER), BF16),
    GJ3=((3, 48, QUARTER), BF16),
    GT1=((4, 384, QUARTER), BF16),
    GT2=((4, 192, QUARTER), BF16),
    GT3=((3, 192, QUARTER), BF16),
    GW1=((4, 96, QUARTER), BF16),
    GW2=((4, 48, QUARTER), BF16),
    GW3=((3, 48, QUARTER), BF16),
    GQ1=((4, 96, QUARTER), BF16),
    GQ2=((4, 48, QUARTER), BF16),
    GQ3=((3, 48, QUARTER), BF16),
    GK1=((4, 96, D), BF16),
    GK2=((4, 48, D), BF16),
    GK3=((3, 48, D), BF16),
    SG1=((4, 64, 128), F32),
    SG2=((4, 32, 128), F32),
    SG3=((3, 32, 128), F32),
    FI=((48, 1152), F32),
    FJ=((48, QUARTER), F32),
    FT=((192, QUARTER), F32),
    FW=((48, QUARTER), F32),
    FQ=((48, QUARTER), F32),
    FK=((48, D), F32),
    FS=((32, 128), F32),
    FI_R=((24, 1152), F32),
    FJ_R=((24, QUARTER), F32),
    FT_R=((96, QUARTER), F32),
    FW_R=((24, QUARTER), F32),
    FQ_R=((24, QUARTER), F32),
    FK_R=((24, D), F32),
    FS_R=((16, 128), F32),
)
SEM_COUNT = 280
ORDER = (1, 2, 3, 0)


class Refs:
    pass


def layer_kernel(*refs):
    r = Refs()
    (
        r.tok, r.og, r.wq, r.wk, r.wv, r.wo, r.wi, r.wt, *vectors, r.docs,
        r.out, r.tgrad, r.gq, r.gk, r.gv, r.go, r.gi, r.gt, r.gs,
    ) = refs[:27]
    for name, ref in zip(SCRATCH, refs[27:]):
        setattr(r, name, ref)
    sems = Sems(refs[-2], refs[-1])
    p = Place()
    c, other = p.c, 1 - p.c

    barrier = pltpu.get_barrier_semaphore()
    partners = [p.sibling, p.side["x"], p.side["y"]] + [p.device(z=p.up(k)) for k in (1, 2, 3)]
    for partner in partners:
        pl.semaphore_signal(barrier, inc=1, device_id=partner, device_id_type=MESH)
    pl.semaphore_wait(barrier, len(partners))

    swap = Mover(sems, 16)
    chip_base = p.slot * CHIP_ROWS
    own_base = chip_base + 128 * c
    chip = pl.ds(at_128(chip_base), CHIP_ROWS)
    own_half = pl.ds(at_128(128 * c), 128)

    cols = [pl.ds(at_128(QUARTER * side), QUARTER) for side in (0, 1)]
    mine_cols = pl.ds(at_128(QUARTER * c), QUARTER)
    other_cols = pl.ds(at_128(QUARTER * other), QUARTER)
    for index, ref in enumerate((r.wq, r.wk, r.wv, r.wo)):
        r.SWAP_S[:, QUARTER * index : QUARTER * (index + 1)] = ref[:, other_cols].astype(F32)
    r.SWAP_S[:, 1536:3072] = r.wi[:, pl.ds(at_128(FF_CORE * other), FF_CORE)].astype(F32)
    swap.start(0, lambda: (r.SWAP_S, r.SWAP_R, p.sibling))
    r.X[pl.ds(at_128(own_base), 128), :] = r.tok[...]

    def tok_piece(z, across):
        y = 1 - p.y if across else p.y
        return r.X.at[pl.ds(at_128((y * 4 + z) * CHIP_ROWS + 128 * c), 128)]

    tok = Gather(p, sems, tok_piece, p.side["y"], p.sibling)

    small_rows = r.WS.at[pl.ds(at_16(32 * p.chip + 16 * c), 16)]
    r.SMALL[...] = jnp.zeros_like(r.SMALL)
    for index, ref in enumerate(vectors[:8]):
        r.SMALL[index : index + 1, 0:24] = ref[...].astype(F32)
    inner_vector = vectors[8][...].astype(F32)
    for index in range(4):
        r.SMALL[8 + index : 9 + index, 0:24] = inner_vector[:, 24 * index : 24 * index + 24]
    r.WS[pl.ds(at_16(32 * p.chip + 16 * c), 16), :] = r.SMALL[...].astype(BF16)
    swap.start(1, lambda: (small_rows, small_rows, p.sibling))
    outer_rows = pl.ds(at_16(192 * p.chip + 96 * c), 96)
    r.WT[outer_rows, :] = r.wt[:, mine_cols]
    swap.start(2, lambda: (r.wt.at[:, other_cols], r.WT.at[outer_rows], p.sibling))
    og_rows = r.OG.at[own_half]
    r.OG[own_half, :] = r.og[...]
    swap.start(3, lambda: (og_rows, og_rows, p.sibling))

    def weights(ref, rows, first):
        def piece(z, across):
            x, y = p.x, p.y
            if across:
                x, y = (x, 1 - y) if first == "y" else (1 - x, y)
            return ref.at[pl.ds(at_16((x * 8 + z * 2 + y) * rows), rows)]

        return Gather(p, sems, piece, p.side[first], p.side["y" if first == "x" else "x"])

    gs = weights(r.WS, 32, "y")
    ga = weights(r.WA, 48, "y")
    gi = weights(r.WI, 48, "y")
    gt = weights(r.WT, 192, "x")

    column = lane_iota((1, D))
    by_24, in_24 = lax.div(column, 24), lax.rem(column, 24)
    spread = jnp.where(row_iota((128, D)) == in_24, 1.0, 0.0).astype(BF16)
    row = row_iota((512, 1))
    owner, kind = lax.shift_right_logical(row, 4), jnp.bitwise_and(row, 15)
    row_set = pl.ds(at_128(QUARTER * c), QUARTER)
    other_set = pl.ds(at_128(QUARTER * other), QUARTER)
    outer_set = pl.ds(at_128(FF_CORE * c), FF_CORE)
    other_outer = pl.ds(at_128(FF_CORE * other), FF_CORE)
    lanes128 = lane_iota((1, 128))
    in_head = [jnp.logical_and(lanes128 >= 64 * e, lanes128 < 64 * e + 64) for e in (0, 1)]
    own_row = lax.shift_right_logical(row_iota((CHIP_ROWS, 1)), 7) == c
    own_is_first = c == 0
    chip_weights = pl.ds(at_16(48 * p.chip), 48)
    sibling_half = pl.ds(at_128(128 * other), 128)

    def masked(value, e, scale=1.0):
        return jnp.where(in_head[e], value.astype(F32) * scale, 0.0).astype(BF16)

    def pair_cols(base, pair):
        return pl.ds(at_128(base + 128 * pair), 128)

    def exchange(index, partial):
        r.PX_S[index] = partial.astype(BF16)
        swap.start(6 + index, lambda: (r.PX_S.at[index], r.PX_R.at[index], p.sibling))

    def column_sum(value):
        return jnp.sum(jnp.where(own_row, value, 0.0), axis=0, keepdims=True)

    def vector(index):
        return r.VEC[index : index + 1, :]

    kept_values = {}
    def take_weights():
        swap.arrived(0)
        for index, ref in enumerate((r.wq, r.wk, r.wv, r.wo)):
            where = slice(QUARTER * index, QUARTER * (index + 1))
            kept = ref[:, mine_cols].astype(F32)
            came = r.SWAP_R[:, where]
            both = jnp.concatenate(
                [jnp.where(own_is_first, kept, came), jnp.where(own_is_first, came, kept)], axis=0
            )
            r.WA[chip_weights, where] = both.astype(BF16)
        swap.arrived(1)
        kept = r.wi[:, pl.ds(at_128(FF_CORE * c), FF_CORE)].astype(F32)
        came = r.SWAP_R[:, 1536:3072]
        both = jnp.concatenate(
            [jnp.where(own_is_first, kept, came), jnp.where(own_is_first, came, kept)], axis=0
        )
        r.WI[chip_weights, :] = both.astype(BF16)
        swap.arrived(2)

    def mark_documents():
        one_row = lane_iota((1, 128))
        starts = jnp.full((1, 128), FAR, jnp.int32)
        nexts = jnp.full((1, 128), FAR, jnp.int32)
        count = r.docs.shape[0]
        for d in range(count):
            starts = jnp.where(one_row == d, r.docs[d], starts)
            if d:
                nexts = jnp.where(one_row == d - 1, r.docs[d], nexts)
        lanes = lane_iota((CHIP_ROWS, 128))
        for j in range(8):
            place = row_iota((CHIP_ROWS, 128)) + (p.x * HALF_ROWS + (j % 4) * 512 + (j // 4) * 256)
            inside = jnp.logical_and(place >= starts, place < nexts)
            rows = slice(j * CHIP_ROWS, (j + 1) * CHIP_ROWS)
            r.QE[rows, :] = jnp.where(inside, 1.0, 0.0).astype(BF16)
            r.KE[rows, :] = jnp.where(jnp.logical_or(inside, lanes >= 16), 0.0, PENALTY).astype(BF16)

    def spread_vectors():
        gs.complete()
        ga.complete()
        spread_rows = nn(r.WS[...], spread)
        chosen = jnp.where(owner == by_24, spread_rows, 0.0)
        r.VEC[...] = jnp.sum(chosen.reshape(32, 16, D), axis=0)
        part_of = jnp.where(
            jnp.logical_and(kind >= 8, kind < 12), 4 * (owner - 16 * c) + kind - 8, -1000
        )
        for u in (0, 1):
            chosen = jnp.where(part_of - 32 * u == by_24, spread_rows, 0.0)
            r.BIN[0:1, D * u : D * (u + 1)] = jnp.sum(chosen, axis=0, keepdims=True)
        r.WO[:, mine_cols] = r.WA[row_set, 1152:1536]
        swap.start(4, lambda: (r.WA.at[other_set, pl.ds(1152, QUARTER)], r.WO.at[:, mine_cols], p.sibling))

    outer_slot = sems.take(4)

    def outer_swap(z):
        rows = pl.ds(at_16((other * 8 + z * 2) * 192), QUARTER)
        return pltpu.make_async_remote_copy(
            r.WT.at[rows],
            r.WTR.at[pl.ds(at_128(z * QUARTER), QUARTER), mine_cols],
            sems.send.at[outer_slot + z],
            sems.recv.at[outer_slot + z],
            device_id=p.sibling,
            device_id_type=MESH,
        )

    def outer_rows_came(z):
        gt.copy("second", z).wait_recv()
        gt.copy("across", z).wait_recv()
        outer_swap(z).start()
        r.WTR[pl.ds(at_128(z * QUARTER), QUARTER), mine_cols] = r.WT[
            pl.ds(at_16((c * 8 + z * 2) * 192), QUARTER), :
        ]

    def outer_came(step):
        def run():
            if step == 0:
                outer_rows_came(p.z)
                return
            pl.when(p.has_below[step])(lambda: outer_rows_came(p.z - step))
            pl.when(p.has_above[step])(lambda: outer_rows_came(p.z + step))

        return run

    def project(j):
        value_bias = r.VEC[1:2, mine_cols]
        bias = jnp.concatenate([jnp.zeros_like(value_bias), value_bias], axis=1)
        for part in (0, 1):
            rows = pl.ds(at_128((2 * j + part) * CHIP_ROWS), CHIP_ROWS)
            r.QKV[rows, QUARTER:] = (nn(r.X[rows, :], r.WA[:, QUARTER:1152]) + bias).astype(BF16)

    def queries_of(rows):
        value = nn(r.X[rows, :], r.WA[:, 0:QUARTER]) + r.VEC[0:1, mine_cols]
        r.QKV[rows, 0:QUARTER] = value.astype(BF16)

    def chip_queries():
        queries_of(chip)

    def all_queries():
        def block(j, carry):
            queries_of(pl.ds(at_128(j * 512), 512))
            return carry

        lax.fori_loop(0, 4, block, 0)

    def attend(pair):
        query_doc = r.QE[chip, :]
        queries = r.QKV[chip, pair_cols(0, pair)]
        keys = jnp.concatenate([r.QKV[:, pair_cols(QUARTER, pair)], r.KE[...]], axis=1)
        values = r.QKV[:, pair_cols(2 * QUARTER, pair)]
        outputs = []
        for e in (0, 1):
            query = jnp.concatenate([masked(queries, e, 0.125), query_doc], axis=1)
            scores = nt(query, keys)
            top = jnp.max(scores, axis=1, keepdims=True)
            weights = jnp.exp(scores - top)
            total = jnp.sum(weights, axis=1, keepdims=True)
            outputs.append(nn(weights.astype(BF16), values) / total)
            log_total = top + jnp.log(total)
            r.LSE[...] = jnp.where(lanes128 == 2 * pair + e, log_total, r.LSE[...])
        r.ATT[:, pair_cols(0, pair)] = jnp.where(in_head[0], outputs[0], outputs[1]).astype(BF16)

    def first_norm():
        swap.arrived(4)
        swap.arrived(3)

        branch = nn(r.ATT[...], r.WO[...])
        exchange(0, branch)
        swap.arrived(6)
        branch = branch + r.PX_R[0].astype(F32) + vector(2)
        normed, kept_values["inverse"] = normed_of(r.X[chip, :].astype(F32) + branch)
        r.N1[...] = normed
        hidden = normed * vector(3) + vector(4)
        r.HID[...] = hidden
        r.HL[...] = hidden.astype(BF16)

    def inner_layer():
        def inner_block(j, carry):
            where = pl.ds(at_128(j * QUARTER), QUARTER)
            value = nn(r.HL[...], r.WI[:, where]) + r.BIN[0:1, where]
            phi = 0.5 + 0.5 * lax.erf(value * (0.5**0.5))
            r.ACT[:, where] = (value * phi).astype(BF16)
            r.GV[:, where] = value
            r.GP[:, where] = phi
            return carry

        lax.fori_loop(0, 4, inner_block, 0)

    def second_norm():
        for z in range(4):
            outer_swap(z).wait_recv()

        def outer_block(j, carry):
            where = pl.ds(at_128(j * 256), 256)
            r.PART[:, where] = nn(r.ACT[...], r.WTR[:, where])
            return carry

        lax.fori_loop(0, 3, outer_block, 0)
        exchange(1, r.PART[...])

        def slope_block(j, carry):
            where = pl.ds(at_128(j * QUARTER), QUARTER)
            value = r.GV[:, where]
            density = jnp.exp(value * value * -0.5) * 0.3989422804014327
            r.GP[:, where] = r.GP[:, where] + value * density
            return carry

        lax.fori_loop(0, 4, slope_block, 0)
        swap.arrived(7)
        outer = r.PART[...] + r.PX_R[1].astype(F32) + vector(5)
        normed2, inverse2 = normed_of(r.HID[...] + outer)
        r.HID[...] = normed2 * vector(6) + vector(7)
        r.out[...] = r.HID[own_half, :].astype(BF16)
        grad_out = r.OG[...].astype(F32)
        grad_resid2 = normed_back(grad_out * vector(6), normed2, inverse2)
        r.HID[...] = grad_resid2
        grad_outer = grad_resid2.astype(BF16)
        r.GO[...] = grad_outer

        r.SV[...] = jnp.zeros_like(r.SV)
        r.SV[6:7, :] = column_sum(grad_out * normed2)
        r.SV[7:8, :] = column_sum(grad_out)
        r.SV[5:6, :] = column_sum(grad_outer.astype(F32))

    ri = Reduce(p, sems, r.GI, 48, "y", (r.GI1, r.GI2, r.GI3))
    rj = Reduce(p, sems, r.GJ, 48, "x", (r.GJ1, r.GJ2, r.GJ3))
    rt = Reduce(p, sems, r.GT, 192, "x", (r.GT1, r.GT2, r.GT3))
    rw = Reduce(p, sems, r.GW, 48, "x", (r.GW1, r.GW2, r.GW3))
    rq = Reduce(p, sems, r.GQ, 48, "x", (r.GQ1, r.GQ2, r.GQ3))
    rk = Reduce(p, sems, r.GK, 48, "x", (r.GK1, r.GK2, r.GK3))
    rs = Reduce(p, sems, r.SG, 32, "y", (r.SG1, r.SG2, r.SG3))

    def back_piece(z, across):
        y = 1 - p.y if across else p.y
        return r.DO.at[pl.ds(at_128((y * 4 + z) * CHIP_ROWS), CHIP_ROWS)]

    def stat_piece(z, across):
        y = 1 - p.y if across else p.y
        return r.STAT.at[:, pl.ds(at_128((y * 4 + z) * CHIP_ROWS), CHIP_ROWS)]

    back = Gather(p, sems, back_piece, p.side["y"])
    stat = Gather(p, sems, stat_piece, p.side["y"])
    last = Mover(sems, 7)
    finals = {
        ri: (0, r.FI, r.FI_R, 24),
        rt: (1, r.FT, r.FT_R, 96),
        rw: (2, r.FW, r.FW_R, 24),
        rq: (3, r.FQ, r.FQ_R, 24),
        rk: (4, r.FK, r.FK_R, 24),
        rs: (5, r.FS, r.FS_R, 16),
        rj: (6, r.FJ, r.FJ_R, 24),
    }

    def final(reduce):
        def run():
            index, total, came, rows = finals[reduce]
            total[...] = reduce.result()
            last.start(
                index,
                lambda: (total.at[pl.ds(at_8(rows * other), rows)], came, p.sibling),
            )

        return run

    def outer_gradient():
        def outer_grads(j, carry):
            where = pl.ds(at_128(j * QUARTER), QUARTER)
            mine_rows = pl.ds(at_128(FF_CORE * c + j * QUARTER), QUARTER)
            r.GT_S[where, :] = tn(r.ACT[:, where], r.GO[:, other_cols]).astype(BF16)
            r.GT[mine_rows, :] = tn(r.ACT[:, where], r.GO[:, mine_cols]).astype(BF16)
            return carry

        lax.fori_loop(0, 4, outer_grads, 0)
        swap.start(10, lambda: (r.GT_S, r.GT.at[outer_set], p.sibling))

    def inner_back():
        def inner_back(j, carry):
            where = pl.ds(at_128(j * QUARTER), QUARTER)
            grad = (nt(r.GO[...], r.WTR[where, :]) * r.GP[:, where]).astype(BF16)
            r.GIN[:, where] = grad
            r.BIN[1:2, where] = jnp.sum(grad.astype(F32), axis=0, keepdims=True)
            return carry

        lax.fori_loop(0, 3, inner_back, 0)
        for u in (0, 1):
            r.SV[pl.ds(8 + 2 * c + u, 1), :] = r.BIN[1:2, D * u : D * (u + 1)]

    def inner_back_last():
        where = slice(1152, 1536)
        grad = (nt(r.GO[...], r.WTR[where, :]) * r.GP[:, where]).astype(BF16)
        r.GIN[:, where] = grad
        r.BIN[1:2, where] = jnp.sum(grad.astype(F32), axis=0, keepdims=True)
        r.GJ[...] = tn(r.HL[...], grad).astype(BF16)

    def inner_gradient():
        def inner_grads(j, carry):
            where = pl.ds(at_128(j * QUARTER), QUARTER)
            r.GI[:, where] = tn(r.HL[...], r.GIN[:, where]).astype(BF16)
            return carry

        lax.fori_loop(0, 3, inner_grads, 0)

    def hidden_back():
        def hidden_back(j, carry):
            where = pl.ds(at_128(j * 256), 256)
            r.PART[:, where] = nt(r.GIN[...], r.WI[where, :])
            return carry

        lax.fori_loop(0, 3, hidden_back, 0)
        exchange(2, r.PART[...])

    def first_norm_back():
        swap.arrived(8)
        grad_hidden = r.HID[...] + r.PART[...] + r.PX_R[2].astype(F32)
        normed = r.N1[...]
        grad_resid1 = normed_back(grad_hidden * vector(3), normed, kept_values["inverse"])
        r.SV[3:4, :] = column_sum(grad_hidden * normed)
        r.SV[4:5, :] = column_sum(grad_hidden)
        r.HID[...] = grad_resid1
        grad_branch = grad_resid1.astype(BF16)
        r.GB[...] = grad_branch
        r.SV[2:3, :] = column_sum(grad_branch.astype(F32))
        grad_attended = nt(grad_branch, r.WO[...]).astype(BF16)
        r.DO[chip, :] = grad_attended
        attended = r.ATT[...].astype(F32)
        product = grad_attended.astype(F32) * attended
        for head in range(CORE_HEADS):
            pair = slice(128 * (head // 2), 128 * (head // 2) + 128)
            delta = jnp.sum(jnp.where(in_head[head % 2], product[:, pair], 0.0), axis=1, keepdims=True)
            r.DELTA[...] = jnp.where(lanes128 == head, delta, r.DELTA[...])
        chip_lanes = pl.ds(at_128(chip_base), CHIP_ROWS)
        r.STAT[0:8, chip_lanes] = jnp.transpose(r.LSE[...])[0:8, :]
        r.STAT[8:16, chip_lanes] = jnp.transpose(r.DELTA[...])[0:8, :]

        back.begin()
        stat.begin()

    def output_gradient():
        r.GW_S[...] = tn(r.ATT[...], r.GB[:, other_cols]).astype(BF16)
        r.GW[row_set, :] = tn(r.ATT[...], r.GB[:, mine_cols]).astype(BF16)
        swap.start(11, lambda: (r.GW_S, r.GW.at[row_set], p.sibling))

    def query_back(pair):
        query_doc = r.QE[chip, :]
        queries = r.QKV[chip, pair_cols(0, pair)]
        keys = r.QKV[:, pair_cols(QUARTER, pair)]
        keys_doc = jnp.concatenate([keys, r.KE[...]], axis=1)
        values = r.QKV[:, pair_cols(2 * QUARTER, pair)]
        grads = r.DO[chip, pair_cols(0, pair)]
        outputs = []
        for e in (0, 1):
            pick = lanes128 == 2 * pair + e
            log_total = jnp.sum(jnp.where(pick, r.LSE[...], 0.0), axis=1, keepdims=True)
            delta = jnp.sum(jnp.where(pick, r.DELTA[...], 0.0), axis=1, keepdims=True)
            query = jnp.concatenate([masked(queries, e, 0.125), query_doc], axis=1)
            probs = jnp.exp(nt(query, keys_doc) - log_total)
            grad_probs = nt(masked(grads, e), values)
            grad_scores = (probs * (grad_probs - delta)).astype(BF16)
            outputs.append(nn(grad_scores, keys) * 0.125)
        r.DQKV[:, pair_cols(0, pair)] = jnp.where(in_head[0], outputs[0], outputs[1]).astype(BF16)

    def query_gradient():
        r.GQ[...] = tn(r.X[chip, :], r.DQKV[:, 0:QUARTER]).astype(BF16)

    def key_back(pair):
        key_doc = r.KE[chip, :]
        keys = r.QKV[chip, pair_cols(QUARTER, pair)]
        values = r.QKV[chip, pair_cols(2 * QUARTER, pair)]
        queries = r.QKV[:, pair_cols(0, pair)]
        queries_doc = jnp.concatenate([queries, r.QE[...]], axis=1)
        grads = r.DO[:, pair_cols(0, pair)]
        key_grads, value_grads = [], []
        for e in (0, 1):
            log_total = r.STAT[pl.ds(2 * pair + e, 1), :]
            delta = r.STAT[pl.ds(8 + 2 * pair + e, 1), :]
            key = jnp.concatenate([masked(keys, e, 0.125), key_doc], axis=1)
            probs = jnp.exp(nt(key, queries_doc) - log_total)
            value_grads.append(nn(probs.astype(BF16), grads))
            grad_probs = nt(masked(values, e), grads)
            grad_scores = (probs * (grad_probs - delta)).astype(BF16)
            key_grads.append(nn(grad_scores, queries) * 0.125)
        r.DQKV[:, pair_cols(QUARTER, pair)] = jnp.where(
            in_head[0], key_grads[0], key_grads[1]
        ).astype(BF16)
        r.DQKV[:, pair_cols(2 * QUARTER, pair)] = jnp.where(
            in_head[0], value_grads[0], value_grads[1]
        ).astype(BF16)

    def key_gradients():
        def project_grads(j, carry):
            where = pl.ds(at_128(j * QUARTER), QUARTER)
            source = pl.ds(at_128((j + 1) * QUARTER), QUARTER)
            r.GK[:, where] = tn(r.X[chip, :], r.DQKV[:, source]).astype(BF16)
            return carry

        lax.fori_loop(0, 2, project_grads, 0)

    def tokens_gradient():
        def tokens_back(j, carry):
            where = pl.ds(at_128(j * 256), 256)
            r.PART[:, where] = nt(r.DQKV[...], r.WA[where, 0:1152])
            return carry

        lax.fori_loop(0, 3, tokens_back, 0)
        r.PX_S[3, 0:128, :] = r.PART[sibling_half, :].astype(BF16)
        swap.start(9, lambda: (r.PX_S.at[3, pl.ds(0, 128)], r.PX_R.at[3, pl.ds(0, 128)], p.sibling))

        r.SV[0:1, mine_cols] = jnp.sum(r.DQKV[:, 0:QUARTER].astype(F32), axis=0, keepdims=True)
        r.SV[1:2, mine_cols] = jnp.sum(r.DQKV[:, 2 * QUARTER :].astype(F32), axis=0, keepdims=True)
        by_96, in_96 = lax.div(column, 96), lax.rem(column, 96)
        gather_96 = jnp.where(row_iota((128, D)) == in_96, 1.0, 0.0).astype(BF16)
        sums = jnp.broadcast_to(r.SV[...].reshape(1, 16, D), (32, 16, D)).reshape(512, D)
        late = kind >= 8
        wanted = jnp.where(late, 8 * (kind - 8) + by_96, by_24) == owner
        sums = jnp.where(wanted, sums, 0.0)
        high = sums.astype(BF16)
        low_part = (sums - high.astype(F32)).astype(BF16)
        r.SG[...] = jnp.where(
            late,
            nt(high, gather_96) + nt(low_part, gather_96),
            nt(high, spread) + nt(low_part, spread),
        )

    r.LSE[...] = jnp.zeros_like(r.LSE)
    r.DELTA[...] = jnp.zeros_like(r.DELTA)
    forward = [
        first(tok), z_start(tok), take_weights, second(gi), second(tok), first(gi), first(gt),
        first(ga, gs), z_start(ga, gs), across(0, tok), hop(1, ga, gs), z_start(gi), across(0, gt),
        across(0, ga, gs), z_start(gt), second(ga, gs), hop(2, ga, gs), across(0, gi),
        across(1, ga, gs), mark_documents, hop(1, tok), across(2, ga, gs), second(gt),
        hop(3, ga, gs), hop(2, tok), hop(3, tok), hop(1, gi), across(3, ga, gs), hop(1, gt),
        across(1, tok), hop(2, gt), across(2, tok), across(3, tok), outer_came(0), hop(2, gi),
        hop(3, gt), spread_vectors, tok.complete,
        loop(
            project,
            [],
            [],
            [],
        ),
        across(1, gi), hop(3, gi), chip_queries,
        loop(
            attend,
            [],
            [],
        ),
        across(1, gt), across(2, gt), across(3, gt), across(2, gi), first_norm, outer_came(1),
        across(3, gi), gi.complete, outer_came(2), outer_came(3), inner_layer, second_norm,
    ]
    backward = [
        inner_back_last, one(rj), inner_back, inner_gradient, one(ri), outer_gradient, hidden_back,
        all_queries, lambda: swap.arrived(10), one(rt), two(ri, 1), first_norm_back,
        loop(
            query_back,
            [
                two(rj, 2),
            ],
            [
                output_gradient, hop(1, back, stat), two(ri, 3), two(ri, 2), hop(2, back, stat),
            ],
        ),
        three(rj, 2), query_gradient, two(rt, 2), hop(3, back, stat), two(rt, 3), one(rq),
        across(0, back, stat), three(ri, 1), three(ri, 3), across(1, back, stat), three(ri, 2),
        two(rj, 1), two(rt, 1), across(2, back, stat), two(rj, 3), two(rt, 0),
        across(3, back, stat),
        loop(
            key_back,
            [
                lambda: swap.arrived(11), one(rw), three(rt, 2),
            ],
            [],
        ),
        three(rt, 1), key_gradients, one(rk), three(rj, 1), two(rw, 2), two(rq, 1), two(rj, 0),
        three(rt, 3), three(rt, 0), two(rw, 3), two(rq, 2), three(rj, 3), two(rk, 1), two(rq, 0),
        two(rw, 0), three(rw, 2), three(rq, 2), two(rq, 3), two(rk, 2), three(rk, 1), two(ri, 0),
        three(rj, 0), three(rq, 0), tokens_gradient, one(rs), three(rw, 0), two(rw, 1),
        three(rw, 3), two(rk, 3), two(rs, 1), three(rk, 2), two(rs, 2), two(rs, 0), two(rk, 0),
        final(rj), three(rw, 1), three(rq, 3), three(rq, 1), three(ri, 0), final(rt), two(rs, 3),
        three(rk, 3), three(rs, 3), three(rs, 1), final(rw), final(ri), three(rk, 0), final(rq),
        three(rs, 0), three(rs, 2), final(rk), final(rs),
    ]
    for step in forward + backward:
        step()

    swap.arrived(9)
    r.tgrad[...] = (
        r.HID[own_half, :] + r.PART[own_half, :] + r.PX_R[3, 0:128, :].astype(F32)
    ).astype(BF16)

    kept24 = pl.ds(at_8(24 * c), 24)
    last.arrived(0)
    last.arrived(6)
    r.gi[:, pl.ds(at_128(FF_CORE * c), 1152)] = r.FI[kept24, :]
    r.gi[:, pl.ds(at_128(FF_CORE * other), 1152)] = r.FI_R[...]
    r.gi[:, pl.ds(at_128(FF_CORE * c + 1152), QUARTER)] = r.FJ[kept24, :]
    r.gi[:, pl.ds(at_128(FF_CORE * other + 1152), QUARTER)] = r.FJ_R[...]
    last.arrived(1)
    r.gt[:, mine_cols] = r.FT[pl.ds(at_8(96 * c), 96), :]
    r.gt[:, other_cols] = r.FT_R[...]
    last.arrived(2)
    r.go[:, mine_cols] = r.FW[kept24, :]
    r.go[:, other_cols] = r.FW_R[...]
    last.arrived(3)
    r.gq[:, mine_cols] = r.FQ[kept24, :]
    r.gq[:, other_cols] = r.FQ_R[...]
    last.arrived(4)
    for index, ref in enumerate((r.gk, r.gv)):
        where = slice(QUARTER * index, QUARTER * (index + 1))
        ref[:, mine_cols] = r.FK[kept24, where]
        ref[:, other_cols] = r.FK_R[:, where]
    last.arrived(5)
    totals = r.FS[pl.ds(at_8(16 * c), 16), :] + r.FS_R[...]
    inner_total = totals[8:9] + totals[9:10] + totals[10:11] + totals[11:12]
    r.gs[0:8, :] = totals[0:8]
    r.gs[8:16, :] = jnp.broadcast_to(inner_total, (8, 128))

    for z in range(4):
        outer_swap(z).wait_send()
    for mover in (swap, tok, gs, ga, gi, gt, back, stat, ri, rj, rt, rw, rq, rk, rs, last):
        mover.sent()


def hand_out(*refs):
    count = 8
    for source, target in zip(refs[:count], refs[count + 1 :]):
        target[...] = source[...]
    vectors = refs[count]
    for row, target in enumerate(refs[2 * count + 1 :]):
        target[...] = vectors[row, 0 : target.shape[0]]


def slice_body(
    tokens, query_weight, query_bias, key_weight, value_weight, value_bias, output_weight, output_bias,
    first_gain, first_shift, inner_weight, inner_bias, outer_weight, outer_bias, second_gain,
    second_shift, doc_starts, out_grad,
):
    vectors = (
        query_bias, value_bias, output_bias, first_gain, first_shift, outer_bias, second_gain,
        second_shift, inner_bias,
    )
    vectors = tuple(value.reshape(1, -1) for value in vectors)
    shape = jax.ShapeDtypeStruct
    vmem = pl.BlockSpec(memory_space=pltpu.VMEM)
    out_shapes = (
        shape((128, D), BF16), shape((128, D), BF16), shape((24, D), F32), shape((24, D), F32),
        shape((24, D), F32), shape((24, D), F32), shape((24, 3072), F32), shape((96, D), F32),
        shape((16, 128), F32),
    )
    results = pl.pallas_call(
        layer_kernel,
        out_shape=out_shapes,
        in_specs=[vmem] * 17 + [pl.BlockSpec(memory_space=pltpu.SMEM)],
        out_specs=[vmem] * 9,
        scratch_shapes=[pltpu.VMEM(*entry) for entry in SCRATCH.values()]
        + [pltpu.SemaphoreType.DMA((SEM_COUNT,)), pltpu.SemaphoreType.DMA((SEM_COUNT,))],
        compiler_params=pltpu.CompilerParams(
            collective_id=0, has_side_effects=True, vmem_limit_bytes=62 * 2**20
        ),
        name="layer",
    )(
        tokens, out_grad, query_weight, key_weight, value_weight, output_weight, inner_weight,
        outer_weight, *vectors, doc_starts,
    )
    vector_shapes = (shape((24,), F32),) * 8 + (shape((96,), F32),)
    out, tgrad, gq, gk, gv, go, gi, gt, *v = pl.pallas_call(
        hand_out,
        out_shape=out_shapes[:8] + vector_shapes,
        in_specs=[vmem] * 9,
        out_specs=[vmem] * 17,
        name="hand_out",
    )(*results)
    return (
        out, tgrad, gq, v[0], gk, gv, v[1], go, v[2], v[3], v[4], gi, v[8], gt, v[5], v[6], v[7]
    )


def solution(mesh):
    rows, flat = P(("head", "blk"), None), P(("head", "blk"))
    in_specs = (
        rows, rows, flat, rows, rows, flat, rows, flat, flat, flat, rows, flat, rows, flat, flat, flat,
        P(), rows,
    )
    out_specs = (
        rows, rows, rows, flat, rows, rows, flat, rows, flat, flat, flat, rows, flat, rows, flat, flat,
        flat,
    )
    small_slice = mesh.shape["head"] == 2 and mesh.shape["blk"] == 16
    return jax.shard_map(
        slice_body if small_slice else body,
        mesh=mesh,
        in_specs=in_specs,
        out_specs=out_specs,
        check_vma=False,
    )
```

```python
from functools import partial

import jax
import jax.numpy as jnp
from jax import lax
from jax.experimental import pallas as pl
from jax.experimental.pallas import tpu as pltpu
from jax.sharding import PartitionSpec as P

HEAD_DIM = 64


LN_EPS = 1e-12
MASKED_SCORE = -1e30


def doc_numbers(doc_starts, positions):
    covered = (doc_starts[None, :] <= positions[:, None]).astype(jnp.int32)
    return (jnp.sum(covered, axis=1) - 1).astype(jnp.float32)


def dense_product(left_side, right_side):
    return jnp.dot(left_side, right_side, preferred_element_type=jnp.float32)


def product_back(left_side, right_side):
    return lax.dot_general(
        left_side, right_side, (((1,), (1,)), ((), ())), preferred_element_type=jnp.float32
    )


def product_left(left_side, right_side):
    return lax.dot_general(
        left_side, right_side, (((0,), (0,)), ((), ())), preferred_element_type=jnp.float32
    )


def norm_forward(residual, scale_gain, shift_bias):
    row_mean = jnp.mean(residual, axis=-1, keepdims=True)
    centred = residual - row_mean
    variance = jnp.mean(centred * centred, axis=-1, keepdims=True)
    inverse = lax.rsqrt(variance + LN_EPS)
    normed = centred * inverse
    return (normed * scale_gain + shift_bias, normed, inverse)


def norm_backward(grad_output, normed, inverse, scale_gain):
    grad_normed = grad_output * scale_gain
    first_term = jnp.mean(grad_normed, axis=-1, keepdims=True)
    second_term = jnp.mean(grad_normed * normed, axis=-1, keepdims=True)
    grad_input = inverse * (grad_normed - first_term - normed * second_term)
    return (grad_input, jnp.sum(grad_output * normed, axis=0), jnp.sum(grad_output, axis=0))


def split_blocks(rows_array, block_rows):
    return rows_array.reshape(-1, block_rows, rows_array.shape[1] // HEAD_DIM, HEAD_DIM)


def blocks_to_rows(blocked):
    reordered = jnp.transpose(blocked, (0, 2, 1, 3))
    return reordered.reshape(-1, blocked.shape[1] * blocked.shape[3])


def block_scores(query_block, key_block, query_docs, key_docs):
    scores = jnp.einsum(
        "qhd,khd->hqk", query_block, key_block, preferred_element_type=jnp.float32
    ) * HEAD_DIM ** (-0.5)
    allowed = (query_docs[:, None] == key_docs[None, :])[None, :, :]
    return (scores, allowed)


def intersecting(first_docs, second_docs):
    return jnp.logical_and(
        jnp.max(first_docs) >= jnp.min(second_docs), jnp.min(first_docs) <= jnp.max(second_docs)
    )


def keep_state(carried):
    return carried


def forward_update(carried, query_block, query_docs, key_block, value_block, key_docs):
    running_max, row_total, accumulated = carried
    scores, allowed = block_scores(query_block, key_block, query_docs, key_docs)
    scores = jnp.where(allowed, scores, MASKED_SCORE)
    new_max = jnp.maximum(running_max, jnp.max(scores, axis=2))
    decay_factor = jnp.exp(running_max - new_max)
    weights = jnp.where(allowed, jnp.exp(scores - new_max[:, :, None]), 0.0)
    row_total = row_total * decay_factor + jnp.sum(weights, axis=2)
    update = jnp.einsum(
        "hqk,khd->hqd",
        weights.astype(jnp.bfloat16),
        value_block,
        preferred_element_type=jnp.float32,
    )
    return (new_max, row_total, accumulated * decay_factor[:, :, None] + update)


def forward_folder(query_blocks, doc_blocks):
    block_rows = query_blocks.shape[1]

    def forward_fold_step(carried_in, pieces, start_row):
        key_piece, value_piece, key_doc_piece = pieces
        key_blocks = split_blocks(key_piece, block_rows)
        value_blocks = split_blocks(value_piece, block_rows)
        key_doc_blocks = key_doc_piece.astype(jnp.float32).reshape(-1, block_rows)

        def forward_one_block(block_index, carried):
            key_docs = key_doc_blocks[block_index]
            results = []
            for query_index in range(query_blocks.shape[0]):
                current = tuple((member[query_index] for member in carried))
                update = partial(
                    forward_update,
                    query_block=query_blocks[query_index],
                    query_docs=doc_blocks[query_index],
                    key_block=key_blocks[block_index],
                    value_block=value_blocks[block_index],
                    key_docs=key_docs,
                )
                results.append(
                    lax.cond(
                        intersecting(doc_blocks[query_index], key_docs), update, keep_state, current
                    )
                )
            return tuple((jnp.stack([entry[member] for entry in results]) for member in range(3)))

        return lax.fori_loop(0, key_blocks.shape[0], forward_one_block, carried_in)

    return forward_fold_step


def query_grad_update(
    grad_query,
    query_block,
    query_docs,
    grad_block,
    log_total,
    delta_rows,
    key_block,
    value_block,
    key_docs,
):
    scores, allowed = block_scores(query_block, key_block, query_docs, key_docs)
    probs = jnp.where(allowed, jnp.exp(scores - log_total[:, :, None]), 0.0)
    grad_probs = jnp.einsum(
        "qhd,khd->hqk", grad_block, value_block, preferred_element_type=jnp.float32
    )
    grad_scores = (probs * (grad_probs - delta_rows[:, :, None])).astype(jnp.bfloat16)
    return grad_query + jnp.einsum(
        "hqk,khd->hqd", grad_scores, key_block, preferred_element_type=jnp.float32
    ) * HEAD_DIM ** (-0.5)


def query_grad_folder(query_blocks, doc_blocks, grad_blocks, log_blocks, delta_blocks):
    block_rows = query_blocks.shape[1]

    def query_fold_step(carried_in, pieces, start_row):
        key_piece, value_piece, key_doc_piece = pieces
        key_blocks = split_blocks(key_piece, block_rows)
        value_blocks = split_blocks(value_piece, block_rows)
        key_doc_blocks = key_doc_piece.astype(jnp.float32).reshape(-1, block_rows)

        def query_one_block(block_index, carried):
            key_docs = key_doc_blocks[block_index]
            results = []
            for query_index in range(query_blocks.shape[0]):
                update = partial(
                    query_grad_update,
                    query_block=query_blocks[query_index],
                    query_docs=doc_blocks[query_index],
                    grad_block=grad_blocks[query_index],
                    log_total=log_blocks[query_index],
                    delta_rows=delta_blocks[query_index],
                    key_block=key_blocks[block_index],
                    value_block=value_blocks[block_index],
                    key_docs=key_docs,
                )
                results.append(
                    lax.cond(
                        intersecting(doc_blocks[query_index], key_docs),
                        update,
                        keep_state,
                        carried[query_index],
                    )
                )
            return jnp.stack(results)

        return lax.fori_loop(0, key_blocks.shape[0], query_one_block, carried_in)

    return query_fold_step


def key_grad_update(
    carried,
    key_block,
    value_block,
    key_docs,
    query_block,
    grad_block,
    log_total,
    delta_rows,
    query_docs,
):
    grad_key, grad_value = carried
    scores, allowed = block_scores(query_block, key_block, query_docs, key_docs)
    probs = jnp.where(allowed, jnp.exp(scores - log_total[:, :, None]), 0.0)
    grad_value = grad_value + jnp.einsum(
        "hqk,qhd->hkd", probs.astype(jnp.bfloat16), grad_block, preferred_element_type=jnp.float32
    )
    grad_probs = jnp.einsum(
        "qhd,khd->hqk", grad_block, value_block, preferred_element_type=jnp.float32
    )
    grad_scores = (probs * (grad_probs - delta_rows[:, :, None])).astype(jnp.bfloat16)
    grad_key = grad_key + jnp.einsum(
        "hqk,qhd->hkd", grad_scores, query_block, preferred_element_type=jnp.float32
    ) * HEAD_DIM ** (-0.5)
    return (grad_key, grad_value)


def key_grad_folder(key_blocks, value_blocks, doc_blocks):
    block_rows = key_blocks.shape[1]

    def key_fold_step(carried_in, pieces, start_row):
        query_piece, grad_piece, log_piece, delta_piece, doc_piece = pieces
        query_blocks = split_blocks(query_piece.astype(jnp.bfloat16), block_rows)
        grad_blocks = split_blocks(grad_piece.astype(jnp.bfloat16), block_rows)
        log_blocks = jnp.transpose(log_piece.reshape(-1, block_rows, log_piece.shape[1]), (0, 2, 1))
        delta_blocks = jnp.transpose(
            delta_piece.reshape(-1, block_rows, delta_piece.shape[1]), (0, 2, 1)
        )
        query_doc_blocks = doc_piece.reshape(-1, block_rows)

        def key_one_block(block_index, carried):
            query_docs = query_doc_blocks[block_index]
            results = []
            for key_index in range(key_blocks.shape[0]):
                current = (carried[0][key_index], carried[1][key_index])
                update = partial(
                    key_grad_update,
                    key_block=key_blocks[key_index],
                    value_block=value_blocks[key_index],
                    key_docs=doc_blocks[key_index],
                    query_block=query_blocks[block_index],
                    grad_block=grad_blocks[block_index],
                    log_total=log_blocks[block_index],
                    delta_rows=delta_blocks[block_index],
                    query_docs=query_docs,
                )
                results.append(
                    lax.cond(
                        intersecting(query_docs, doc_blocks[key_index]), update, keep_state, current
                    )
                )
            return (
                jnp.stack([entry[0] for entry in results]),
                jnp.stack([entry[1] for entry in results]),
            )

        return lax.fori_loop(0, query_blocks.shape[0], key_one_block, carried_in)

    return key_fold_step


def attention_forward(query_rows, key_rows, value_rows, row_docs, block_rows):
    query_blocks = split_blocks(query_rows, block_rows)
    doc_blocks = row_docs.reshape(-1, block_rows)
    block_count = query_blocks.shape[0]
    head_count = query_blocks.shape[2]
    send_docs = row_docs.astype(jnp.bfloat16)
    start_state = (
        jnp.full((block_count, head_count, block_rows), MASKED_SCORE, jnp.float32),
        jnp.zeros((block_count, head_count, block_rows), jnp.float32),
        jnp.zeros((block_count, head_count, block_rows, HEAD_DIM), jnp.float32),
    )
    fold_forward = forward_folder(query_blocks, doc_blocks)
    running_max, row_total, accumulated = fold_forward(
        start_state,
        (
            lax.all_gather(key_rows, "blk", axis=0, tiled=True),
            lax.all_gather(value_rows, "blk", axis=0, tiled=True),
            lax.all_gather(send_docs, "blk", axis=0, tiled=True),
        ),
        jnp.int32(0),
    )
    head_outputs = blocks_to_rows(accumulated / row_total[:, :, :, None]).astype(jnp.bfloat16)
    log_total = running_max + jnp.log(row_total)
    return (head_outputs, log_total)


def attention_backward(
    grad_rows, head_outputs, log_total, query_rows, key_rows, value_rows, row_docs, block_rows
):
    query_blocks = split_blocks(query_rows, block_rows)
    key_blocks = split_blocks(key_rows, block_rows)
    value_blocks = split_blocks(value_rows, block_rows)
    doc_blocks = row_docs.reshape(-1, block_rows)
    block_count = query_blocks.shape[0]
    head_count = query_blocks.shape[2]
    send_docs = row_docs.astype(jnp.bfloat16)
    grad_blocks = split_blocks(grad_rows, block_rows)
    output_blocks = split_blocks(head_outputs, block_rows)
    delta_blocks = jnp.einsum(
        "nqhd,nqhd->nhq", grad_blocks.astype(jnp.float32), output_blocks.astype(jnp.float32)
    )
    log_rows = jnp.transpose(log_total, (0, 2, 1)).reshape(-1, head_count)
    delta_rows = jnp.transpose(delta_blocks, (0, 2, 1)).reshape(-1, head_count)
    fold_queries = query_grad_folder(query_blocks, doc_blocks, grad_blocks, log_total, delta_blocks)
    fold_keys = key_grad_folder(key_blocks, value_blocks, doc_blocks)
    query_start = jnp.zeros((block_count, head_count, block_rows, HEAD_DIM), jnp.float32)
    key_start = (query_start, query_start)
    query_send = (
        query_rows.astype(jnp.float32),
        grad_rows.astype(jnp.float32),
        log_rows,
        delta_rows,
        row_docs,
    )
    grad_query_state = fold_queries(
        query_start,
        (
            lax.all_gather(key_rows, "blk", axis=0, tiled=True),
            lax.all_gather(value_rows, "blk", axis=0, tiled=True),
            lax.all_gather(send_docs, "blk", axis=0, tiled=True),
        ),
        jnp.int32(0),
    )
    grad_key_state, grad_value_state = fold_keys(
        key_start,
        (
            lax.all_gather(query_send[0], "blk", axis=0, tiled=True),
            lax.all_gather(query_send[1], "blk", axis=0, tiled=True),
            lax.all_gather(query_send[2], "blk", axis=0, tiled=True),
            lax.all_gather(query_send[3], "blk", axis=0, tiled=True),
            lax.all_gather(query_send[4], "blk", axis=0, tiled=True),
        ),
        jnp.int32(0),
    )
    return (
        blocks_to_rows(grad_query_state).astype(jnp.bfloat16),
        blocks_to_rows(grad_key_state).astype(jnp.bfloat16),
        blocks_to_rows(grad_value_state).astype(jnp.bfloat16),
    )


def data_layer(tokens, full, row_docs, out_grad, block_rows):
    (
        full_query,
        full_query_bias,
        full_key,
        full_value,
        full_value_bias,
        full_output,
        full_output_bias,
        full_first_gain,
        full_first_shift,
        full_inner,
        full_inner_bias,
        full_outer,
        full_outer_bias,
        full_second_gain,
        full_second_shift,
    ) = full
    queries = (dense_product(tokens, full_query) + full_query_bias.astype(jnp.float32)).astype(
        jnp.bfloat16
    )
    keys_local = dense_product(tokens, full_key).astype(jnp.bfloat16)
    values_local = (dense_product(tokens, full_value) + full_value_bias.astype(jnp.float32)).astype(
        jnp.bfloat16
    )
    query_rows, key_rows, value_rows = (
        lax.all_to_all(queries, "head", split_axis=1, concat_axis=0, tiled=True),
        lax.all_to_all(keys_local, "head", split_axis=1, concat_axis=0, tiled=True),
        lax.all_to_all(values_local, "head", split_axis=1, concat_axis=0, tiled=True),
    )
    head_outputs, log_total = attention_forward(
        query_rows, key_rows, value_rows, row_docs, block_rows
    )
    attended = lax.all_to_all(head_outputs, "head", split_axis=0, concat_axis=1, tiled=True)
    branch = dense_product(attended, full_output) + full_output_bias.astype(jnp.float32)
    hidden, first_normed, first_inverse = norm_forward(
        tokens.astype(jnp.float32) + branch,
        full_first_gain.astype(jnp.float32),
        full_first_shift.astype(jnp.float32),
    )
    hidden_low = hidden.astype(jnp.bfloat16)
    inner_value = dense_product(hidden_low, full_inner) + full_inner_bias.astype(jnp.float32)
    activated_full, gelu_pullback = jax.vjp(partial(jax.nn.gelu, approximate=False), inner_value)
    activated = activated_full.astype(jnp.bfloat16)
    outer_value = dense_product(activated, full_outer) + full_outer_bias.astype(jnp.float32)
    layer_full, second_normed, second_inverse = norm_forward(
        hidden + outer_value,
        full_second_gain.astype(jnp.float32),
        full_second_shift.astype(jnp.float32),
    )
    layer_out = layer_full.astype(jnp.bfloat16)
    grad_output = out_grad.astype(jnp.float32)
    grad_resid2, second_gain_term, second_shift_term = norm_backward(
        grad_output, second_normed, second_inverse, full_second_gain.astype(jnp.float32)
    )
    grad_outer = grad_resid2.astype(jnp.bfloat16)
    outer_weight_term = product_left(activated, grad_outer)
    outer_bias_term = jnp.sum(grad_outer.astype(jnp.float32), axis=0)
    grad_inner = gelu_pullback(product_back(grad_outer, full_outer))[0].astype(jnp.bfloat16)
    inner_weight_term = product_left(hidden_low, grad_inner)
    inner_bias_term = jnp.sum(grad_inner.astype(jnp.float32), axis=0)
    grad_hidden = grad_resid2 + product_back(grad_inner, full_inner)
    grad_resid1, first_gain_term, first_shift_term = norm_backward(
        grad_hidden, first_normed, first_inverse, full_first_gain.astype(jnp.float32)
    )
    grad_branch = grad_resid1.astype(jnp.bfloat16)
    output_weight_term = product_left(attended, grad_branch)
    output_bias_term = jnp.sum(grad_branch.astype(jnp.float32), axis=0)
    grad_attended = product_back(grad_branch, full_output).astype(jnp.bfloat16)
    grad_rows = lax.all_to_all(grad_attended, "head", split_axis=1, concat_axis=0, tiled=True)
    grad_query_rows, grad_key_rows, grad_value_rows = attention_backward(
        grad_rows, head_outputs, log_total, query_rows, key_rows, value_rows, row_docs, block_rows
    )
    grad_queries, grad_keys, grad_values = (
        lax.all_to_all(grad_query_rows, "head", split_axis=0, concat_axis=1, tiled=True),
        lax.all_to_all(grad_key_rows, "head", split_axis=0, concat_axis=1, tiled=True),
        lax.all_to_all(grad_value_rows, "head", split_axis=0, concat_axis=1, tiled=True),
    )
    query_weight_term = product_left(tokens, grad_queries)
    query_bias_term = jnp.sum(grad_queries.astype(jnp.float32), axis=0)
    key_weight_term = product_left(tokens, grad_keys)
    value_weight_term = product_left(tokens, grad_values)
    value_bias_term = jnp.sum(grad_values.astype(jnp.float32), axis=0)
    tokens_grad = (
        grad_resid1
        + product_back(grad_queries, full_query)
        + product_back(grad_keys, full_key)
        + product_back(grad_values, full_value)
    ).astype(jnp.bfloat16)
    summed = (
        lax.psum_scatter(query_weight_term, ("head", "blk"), scatter_dimension=0, tiled=True),
        lax.psum_scatter(query_bias_term, ("head", "blk"), scatter_dimension=0, tiled=True),
        lax.psum_scatter(key_weight_term, ("head", "blk"), scatter_dimension=0, tiled=True),
        lax.psum_scatter(value_weight_term, ("head", "blk"), scatter_dimension=0, tiled=True),
        lax.psum_scatter(value_bias_term, ("head", "blk"), scatter_dimension=0, tiled=True),
        lax.psum_scatter(output_weight_term, ("head", "blk"), scatter_dimension=0, tiled=True),
        lax.psum_scatter(output_bias_term, ("head", "blk"), scatter_dimension=0, tiled=True),
        lax.psum_scatter(first_gain_term, ("head", "blk"), scatter_dimension=0, tiled=True),
        lax.psum_scatter(first_shift_term, ("head", "blk"), scatter_dimension=0, tiled=True),
        lax.psum_scatter(inner_weight_term, ("head", "blk"), scatter_dimension=0, tiled=True),
        lax.psum_scatter(inner_bias_term, ("head", "blk"), scatter_dimension=0, tiled=True),
        lax.psum_scatter(outer_weight_term, ("head", "blk"), scatter_dimension=0, tiled=True),
        lax.psum_scatter(outer_bias_term, ("head", "blk"), scatter_dimension=0, tiled=True),
        lax.psum_scatter(second_gain_term, ("head", "blk"), scatter_dimension=0, tiled=True),
        lax.psum_scatter(second_shift_term, ("head", "blk"), scatter_dimension=0, tiled=True),
    )
    return (layer_out, tokens_grad) + tuple(summed)


def body(
    tokens,
    query_weight,
    query_bias,
    key_weight,
    value_weight,
    value_bias,
    output_weight,
    output_bias,
    first_gain,
    first_shift,
    inner_weight,
    inner_bias,
    outer_weight,
    outer_bias,
    second_gain,
    second_shift,
    doc_starts,
    out_grad,
):
    shards = (
        query_weight,
        query_bias,
        key_weight,
        value_weight,
        value_bias,
        output_weight,
        output_bias,
        first_gain,
        first_shift,
        inner_weight,
        inner_bias,
        outer_weight,
        outer_bias,
        second_gain,
        second_shift,
    )
    full = (
        lax.all_gather(shards[0], ("head", "blk"), axis=0, tiled=True),
        lax.all_gather(shards[1], ("head", "blk"), axis=0, tiled=True),
        lax.all_gather(shards[2], ("head", "blk"), axis=0, tiled=True),
        lax.all_gather(shards[3], ("head", "blk"), axis=0, tiled=True),
        lax.all_gather(shards[4], ("head", "blk"), axis=0, tiled=True),
        lax.all_gather(shards[5], ("head", "blk"), axis=0, tiled=True),
        lax.all_gather(shards[6], ("head", "blk"), axis=0, tiled=True),
        lax.all_gather(shards[7], ("head", "blk"), axis=0, tiled=True),
        lax.all_gather(shards[8], ("head", "blk"), axis=0, tiled=True),
        lax.all_gather(shards[9], ("head", "blk"), axis=0, tiled=True),
        lax.all_gather(shards[10], ("head", "blk"), axis=0, tiled=True),
        lax.all_gather(shards[11], ("head", "blk"), axis=0, tiled=True),
        lax.all_gather(shards[12], ("head", "blk"), axis=0, tiled=True),
        lax.all_gather(shards[13], ("head", "blk"), axis=0, tiled=True),
        lax.all_gather(shards[14], ("head", "blk"), axis=0, tiled=True),
    )
    tok_rows = tokens.shape[0]
    half_length = tok_rows * lax.axis_size("blk")
    blk_place = lax.axis_index("blk")
    offsets = jnp.arange(tok_rows, dtype=jnp.int32)
    row_positions = jnp.concatenate(
        [blk_place * tok_rows + offsets, half_length + blk_place * tok_rows + offsets]
    )
    row_docs = doc_numbers(doc_starts, row_positions)
    return data_layer(tokens, full, row_docs, out_grad, tok_rows)


MESH = pl.DeviceIdType.MESH
F32 = jnp.float32
BF16 = jnp.bfloat16
D = 768
QUARTER = 384
FF_CORE = 1536
HALF_ROWS = 2048
CHIP_ROWS = 256
CORE_HEADS = 6
PENALTY = -1e30
FAR = 2**30


def nn(a, b):
    return lax.dot_general(a, b, (((1,), (0,)), ((), ())), preferred_element_type=F32)


def nt(a, b):
    return lax.dot_general(a, b, (((1,), (1,)), ((), ())), preferred_element_type=F32)


def tn(a, b):
    return lax.dot_general(a, b, (((0,), (0,)), ((), ())), preferred_element_type=F32)


def at_128(index):
    return pl.multiple_of(index, 128)


def at_16(index):
    return pl.multiple_of(index, 16)


def at_8(index):
    return pl.multiple_of(index, 8)


class Place:
    def __init__(self):
        self.x = lax.axis_index("head")
        b = lax.axis_index("blk")
        self.z = lax.div(b, 4)
        self.y = lax.rem(lax.div(b, 2), 2)
        self.c = lax.rem(b, 2)
        self.chip = self.x * 8 + self.z * 2 + self.y
        self.slot = self.y * 4 + self.z
        self.ups = [self.z] + [lax.rem(self.z + k, 4) for k in (1, 2, 3)]
        self.downs = [self.ups[0], self.ups[3], self.ups[2], self.ups[1]]
        self.above = self.device(z=jnp.minimum(self.z + 1, 3))
        self.below = self.device(z=jnp.maximum(self.z - 1, 0))
        self.can_up, self.can_down = self.z < 3, self.z > 0
        self.has_below = [None] + [self.z >= step for step in (1, 2, 3)]
        self.has_above = [None] + [self.z <= 3 - step for step in (1, 2, 3)]
        self.sibling = self.device(c=1 - self.c)
        self.side = {"x": self.device(x=1 - self.x), "y": self.device(y=1 - self.y)}

    def device(self, x=None, z=None, y=None, c=None):
        x = self.x if x is None else x
        z = self.z if z is None else z
        y = self.y if y is None else y
        c = self.c if c is None else c
        return (x, z * 4 + y * 2 + c)

    def up(self, k):
        return self.ups[k]

    def down(self, k):
        return self.downs[k]


class Sems:
    def __init__(self, send, recv):
        self.send, self.recv, self.used = send, recv, 0

    def take(self, count):
        first = self.used
        self.used += count
        assert self.used <= self.send.shape[0]
        return first


class Mover:
    def __init__(self, sems, count):
        self.sems, self.first, self.parts = sems, sems.take(count), {}

    def copy(self, index):
        place = self.first + index
        src, dst, device = self.parts[index]()
        return pltpu.make_async_remote_copy(
            src,
            dst,
            self.sems.send.at[place],
            self.sems.recv.at[place],
            device_id=device,
            device_id_type=MESH,
        )

    def start(self, index, part):
        self.parts[index] = part
        self.copy(index).start()

    def arrived(self, index):
        self.copy(index).wait_recv()

    def sent(self):
        for index in sorted(self.parts):
            self.copy(index).wait_send()


class Gather:
    def __init__(self, place, sems, piece, first, second=None):
        self.place, self.sems, self.piece = place, sems, piece
        self.device = {"up": place.above, "down": place.below, "first": first}
        if second is not None:
            self.device.update(second=second, across=second)
        self.slot = {kind: sems.take(4) for kind in self.device}

    def copy(self, kind, z):
        place = self.slot[kind] + z
        piece = self.piece(z, kind == "across")
        return pltpu.make_async_remote_copy(
            piece,
            piece,
            self.sems.send.at[place],
            self.sems.recv.at[place],
            device_id=self.device[kind],
            device_id_type=MESH,
        )

    def sideways(self, z):
        self.copy("first", z).start()
        if "second" in self.device:
            self.copy("second", z).start()

    def begin_z(self):
        p = self.place

        @pl.when(p.can_up)
        def _():
            self.copy("up", p.z).start()

        @pl.when(p.can_down)
        def _():
            self.copy("down", p.z).start()

    def begin(self):
        self.begin_z()
        self.sideways(self.place.z)

    def hop(self, step):
        p = self.place

        @pl.when(p.has_below[step])
        def _():
            z = p.z - step
            self.copy("up", z).wait_recv()

            @pl.when(p.can_up)
            def _():
                self.copy("up", z).start()

            self.sideways(z)

        @pl.when(p.has_above[step])
        def _():
            z = p.z + step
            self.copy("down", z).wait_recv()

            @pl.when(p.can_down)
            def _():
                self.copy("down", z).start()

            self.sideways(z)

    def across_one(self, z):
        self.copy("first", z).wait_recv()
        if "second" in self.device:
            self.copy("across", z).start()

    def across(self, step):
        p = self.place
        if step == 0:
            self.across_one(p.z)
            return

        @pl.when(p.has_below[step])
        def _():
            self.across_one(p.z - step)

        @pl.when(p.has_above[step])
        def _():
            self.across_one(p.z + step)

    def complete(self):
        for z in range(4):
            self.copy("second", z).wait_recv()
            self.copy("across", z).wait_recv()

    def sent(self):
        p = self.place
        for z in range(4):
            for kind in self.device:
                wait = self.copy(kind, z).wait_send
                if kind == "up":
                    pl.when(jnp.logical_and(p.can_up, p.z >= z))(wait)
                elif kind == "down":
                    pl.when(jnp.logical_and(p.can_down, p.z <= z))(wait)
                else:
                    wait()


class Reduce(Mover):
    def __init__(self, place, sems, ref, rows, first, slots):
        super().__init__(sems, 15)
        self.place, self.ref, self.rows, self.axis = place, ref, rows, first
        self.one, self.two, self.three = slots

    def rows_of(self, x, z, y, count=1):
        return pl.ds(at_8((x * 8 + z * 2 + y) * self.rows), count * self.rows)

    def send_one(self, k):
        p, R = self.place, self.rows
        if self.axis == "x":

            def part():
                where = self.rows_of(1 - p.x, p.up(k), 0, 2)
                return self.ref.at[where], self.one.at[k], p.side["x"]

            self.start(2 * k, part)
        else:
            for xx in (0, 1):

                def part(xx=xx):
                    where = self.rows_of(xx, p.up(k), 1 - p.y)
                    return self.ref.at[where], self.one.at[k, pl.ds(xx * R, R)], p.side["y"]

                self.start(2 * k + xx, part)

    def add(self, where, term):
        self.ref[where] = (self.ref[where].astype(F32) + term.astype(F32)).astype(self.ref.dtype)

    def send_two(self, k):
        p, R = self.place, self.rows
        if self.axis == "x":
            self.arrived(2 * k)
            self.add(self.rows_of(p.x, p.up(k), 0, 2), self.one[k])

            def part():
                where = self.rows_of(p.x, p.up(k), 1 - p.y)
                return self.ref.at[where], self.two.at[k], p.side["y"]

        else:
            for xx in (0, 1):
                self.arrived(2 * k + xx)
                self.add(self.rows_of(xx, p.up(k), p.y), self.one[k, xx * R : (xx + 1) * R])

            def part():
                where = self.rows_of(1 - p.x, p.up(k), p.y)
                return self.ref.at[where], self.two.at[k], p.side["x"]

        self.start(8 + k, part)

    def send_three(self, k):
        p = self.place
        self.arrived(8 + k)
        if k:
            self.add(self.rows_of(p.x, p.up(k), p.y), self.two[k])

            def part():
                where = self.rows_of(p.x, p.up(k), p.y)
                return self.ref.at[where], self.three.at[k - 1], p.device(z=p.up(k))

            self.start(12 + k - 1, part)

    def result(self):
        p = self.place
        total = self.ref[self.rows_of(p.x, p.z, p.y)].astype(F32) + self.two[0].astype(F32)
        for k in (1, 2, 3):
            self.arrived(12 + k - 1)
            total = total + self.three[k - 1].astype(F32)
        return total


def z_start(*gathers):
    return lambda: [gather.begin_z() for gather in gathers]


def first(*gathers):
    return lambda: [gather.copy("first", gather.place.z).start() for gather in gathers]


def second(*gathers):
    return lambda: [gather.copy("second", gather.place.z).start() for gather in gathers]


def hop(step, *gathers):
    return lambda: [gather.hop(step) for gather in gathers]


def across(step, *gathers):
    return lambda: [gather.across(step) for gather in gathers]


def one(*reduces):
    return lambda: [reduce.send_one(k) for k in ORDER for reduce in reduces]


def two(reduce, k):
    return lambda: reduce.send_two(k)


def three(reduce, k):
    return lambda: reduce.send_three(k)


def loop(action, *between):
    def run():
        def step(j, carry):
            for i, steps in enumerate(between):

                @pl.when(j == i + 1)
                def _(steps=steps):
                    for inside in steps:
                        inside()

            action(j)
            return carry

        lax.fori_loop(0, len(between) + 1, step, 0)

    return run


def row_mean(value):
    return jnp.sum(value, axis=1, keepdims=True) * (1.0 / D)


def normed_of(residual):
    centred = residual - row_mean(residual)
    inverse = lax.rsqrt(row_mean(centred * centred) + LN_EPS)
    return centred * inverse, inverse


def normed_back(grad_normed, normed, inverse):
    return inverse * (grad_normed - row_mean(grad_normed) - normed * row_mean(grad_normed * normed))


def lane_iota(shape):
    return lax.broadcasted_iota(jnp.int32, shape, len(shape) - 1)


def row_iota(shape):
    return lax.broadcasted_iota(jnp.int32, shape, 0)


SCRATCH = dict(
    X=((HALF_ROWS, D), BF16),
    SMALL=((16, 128), F32),
    WS=((512, 128), BF16),
    WA=((D, 1536), BF16),
    WI=((D, FF_CORE), BF16),
    WT=((2 * FF_CORE, QUARTER), BF16),
    WO=((QUARTER, D), BF16),
    WTR=((FF_CORE, D), BF16),
    OG=((CHIP_ROWS, D), BF16),
    SWAP_S=((24, 3072), F32),
    SWAP_R=((24, 3072), F32),
    QKV=((HALF_ROWS, 1152), BF16),
    QE=((HALF_ROWS, 128), BF16),
    KE=((HALF_ROWS, 128), BF16),
    ATT=((CHIP_ROWS, QUARTER), BF16),
    LSE=((CHIP_ROWS, 128), F32),
    DELTA=((CHIP_ROWS, 128), F32),
    VEC=((16, D), F32),
    BIN=((8, FF_CORE), F32),
    DO=((HALF_ROWS, QUARTER), BF16),
    STAT=((16, HALF_ROWS), F32),
    PX_S=((4, CHIP_ROWS, D), BF16),
    PX_R=((4, CHIP_ROWS, D), BF16),
    PART=((CHIP_ROWS, D), F32),
    HID=((CHIP_ROWS, D), F32),
    N1=((CHIP_ROWS, D), F32),
    HL=((CHIP_ROWS, D), BF16),
    ACT=((CHIP_ROWS, FF_CORE), BF16),
    GP=((CHIP_ROWS, FF_CORE), F32),
    GV=((CHIP_ROWS, FF_CORE), F32),
    GIN=((CHIP_ROWS, FF_CORE), BF16),
    GO=((CHIP_ROWS, D), BF16),
    GB=((CHIP_ROWS, D), BF16),
    DQKV=((CHIP_ROWS, 1152), BF16),
    SV=((16, D), F32),
    GI=((D, 1152), BF16),
    GJ=((D, QUARTER), BF16),
    GT=((2 * FF_CORE, QUARTER), BF16),
    GT_S=((FF_CORE, QUARTER), BF16),
    GW=((D, QUARTER), BF16),
    GW_S=((QUARTER, QUARTER), BF16),
    GQ=((D, QUARTER), BF16),
    GK=((D, D), BF16),
    SG=((512, 128), F32),
    GI1=((4, 96, 1152), BF16),
    GI2=((4, 48, 1152), BF16),
    GI3=((3, 48, 1152), BF16),
    GJ1=((4, 96, QUARTER), BF16),
    GJ2=((4, 48, QUARTER), BF16),
    GJ3=((3, 48, QUARTER), BF16),
    GT1=((4, 384, QUARTER), BF16),
    GT2=((4, 192, QUARTER), BF16),
    GT3=((3, 192, QUARTER), BF16),
    GW1=((4, 96, QUARTER), BF16),
    GW2=((4, 48, QUARTER), BF16),
    GW3=((3, 48, QUARTER), BF16),
    GQ1=((4, 96, QUARTER), BF16),
    GQ2=((4, 48, QUARTER), BF16),
    GQ3=((3, 48, QUARTER), BF16),
    GK1=((4, 96, D), BF16),
    GK2=((4, 48, D), BF16),
    GK3=((3, 48, D), BF16),
    SG1=((4, 64, 128), F32),
    SG2=((4, 32, 128), F32),
    SG3=((3, 32, 128), F32),
    FI=((48, 1152), F32),
    FJ=((48, QUARTER), F32),
    FT=((192, QUARTER), F32),
    FW=((48, QUARTER), F32),
    FQ=((48, QUARTER), F32),
    FK=((48, D), F32),
    FS=((32, 128), F32),
    FI_R=((24, 1152), F32),
    FJ_R=((24, QUARTER), F32),
    FT_R=((96, QUARTER), F32),
    FW_R=((24, QUARTER), F32),
    FQ_R=((24, QUARTER), F32),
    FK_R=((24, D), F32),
    FS_R=((16, 128), F32),
)
SEM_COUNT = 310
ORDER = (1, 2, 3, 0)


class Refs:
    pass


def layer_kernel(*refs):
    r = Refs()
    (
        r.tok, r.og, r.wq, r.wk, r.wv, r.wo, r.wi, r.wt, *vectors, r.docs,
        r.out, r.tgrad, r.gq, r.gk, r.gv, r.go, r.gi, r.gt, r.gs,
    ) = refs[:27]
    for name, ref in zip(SCRATCH, refs[27:]):
        setattr(r, name, ref)
    sems = Sems(refs[-2], refs[-1])
    p = Place()
    c, other = p.c, 1 - p.c

    barrier = pltpu.get_barrier_semaphore()
    partners = [p.sibling, p.side["x"], p.side["y"]] + [p.device(z=p.up(k)) for k in (1, 2, 3)]
    for partner in partners:
        pl.semaphore_signal(barrier, inc=1, device_id=partner, device_id_type=MESH)
    pl.semaphore_wait(barrier, len(partners))

    swap = Mover(sems, 16)
    chip_base = p.slot * CHIP_ROWS
    own_base = chip_base + 128 * c
    chip = pl.ds(at_128(chip_base), CHIP_ROWS)
    own_half = pl.ds(at_128(128 * c), 128)

    cols = [pl.ds(at_128(QUARTER * side), QUARTER) for side in (0, 1)]
    mine_cols = pl.ds(at_128(QUARTER * c), QUARTER)
    other_cols = pl.ds(at_128(QUARTER * other), QUARTER)
    for index, ref in enumerate((r.wq, r.wk, r.wv, r.wo)):
        r.SWAP_S[:, QUARTER * index : QUARTER * (index + 1)] = ref[:, other_cols].astype(F32)
    r.SWAP_S[:, 1536:3072] = r.wi[:, pl.ds(at_128(FF_CORE * other), FF_CORE)].astype(F32)
    swap.start(0, lambda: (r.SWAP_S, r.SWAP_R, p.sibling))
    r.X[pl.ds(at_128(own_base), 128), :] = r.tok[...]

    def tok_piece(z, across):
        y = 1 - p.y if across else p.y
        return r.X.at[pl.ds(at_128((y * 4 + z) * CHIP_ROWS + 128 * c), 128)]

    tok = Gather(p, sems, tok_piece, p.side["y"], p.sibling)

    small_rows = r.WS.at[pl.ds(at_16(32 * p.chip + 16 * c), 16)]
    r.SMALL[...] = jnp.zeros_like(r.SMALL)
    for index, ref in enumerate(vectors[:8]):
        r.SMALL[index : index + 1, 0:24] = ref[...].astype(F32)
    inner_vector = vectors[8][...].astype(F32)
    for index in range(4):
        r.SMALL[8 + index : 9 + index, 0:24] = inner_vector[:, 24 * index : 24 * index + 24]
    r.WS[pl.ds(at_16(32 * p.chip + 16 * c), 16), :] = r.SMALL[...].astype(BF16)
    swap.start(1, lambda: (small_rows, small_rows, p.sibling))
    outer_rows = pl.ds(at_16(192 * p.chip + 96 * c), 96)
    r.WT[outer_rows, :] = r.wt[:, mine_cols]
    swap.start(2, lambda: (r.wt.at[:, other_cols], r.WT.at[outer_rows], p.sibling))
    og_rows = r.OG.at[own_half]
    r.OG[own_half, :] = r.og[...]
    swap.start(3, lambda: (og_rows, og_rows, p.sibling))

    def weights(ref, rows, first, cols=slice(None)):
        def piece(z, across):
            x, y = p.x, p.y
            if across:
                x, y = (x, 1 - y) if first == "y" else (1 - x, y)
            return ref.at[pl.ds(at_16((x * 8 + z * 2 + y) * rows), rows), cols]

        return Gather(p, sems, piece, p.side[first], p.side["y" if first == "x" else "x"])

    gs = weights(r.WS, 32, "y")
    ga = weights(r.WA, 48, "y")
    gi = weights(r.WI, 48, "y", pl.ds(0, D))
    gj = weights(r.WI, 48, "y", pl.ds(D, D))
    gt = weights(r.WT, 192, "x")

    column = lane_iota((1, D))
    by_24, in_24 = lax.div(column, 24), lax.rem(column, 24)
    spread = jnp.where(row_iota((128, D)) == in_24, 1.0, 0.0).astype(BF16)
    row = row_iota((512, 1))
    owner, kind = lax.shift_right_logical(row, 4), jnp.bitwise_and(row, 15)
    row_set = pl.ds(at_128(QUARTER * c), QUARTER)
    other_set = pl.ds(at_128(QUARTER * other), QUARTER)
    outer_set = pl.ds(at_128(FF_CORE * c), FF_CORE)
    other_outer = pl.ds(at_128(FF_CORE * other), FF_CORE)
    lanes128 = lane_iota((1, 128))
    in_head = [jnp.logical_and(lanes128 >= 64 * e, lanes128 < 64 * e + 64) for e in (0, 1)]
    own_row = lax.shift_right_logical(row_iota((CHIP_ROWS, 1)), 7) == c
    own_is_first = c == 0
    chip_weights = pl.ds(at_16(48 * p.chip), 48)
    sibling_half = pl.ds(at_128(128 * other), 128)

    def masked(value, e, scale=1.0):
        return jnp.where(in_head[e], value.astype(F32) * scale, 0.0).astype(BF16)

    def pair_cols(base, pair):
        return pl.ds(at_128(base + 128 * pair), 128)

    def exchange(index, partial):
        r.PX_S[index] = partial.astype(BF16)
        swap.start(6 + index, lambda: (r.PX_S.at[index], r.PX_R.at[index], p.sibling))

    def column_sum(value):
        return jnp.sum(jnp.where(own_row, value, 0.0), axis=0, keepdims=True)

    def vector(index):
        return r.VEC[index : index + 1, :]

    kept_values = {}
    def take_weights():
        swap.arrived(0)
        for index, ref in enumerate((r.wq, r.wk, r.wv, r.wo)):
            where = slice(QUARTER * index, QUARTER * (index + 1))
            kept = ref[:, mine_cols].astype(F32)
            came = r.SWAP_R[:, where]
            both = jnp.concatenate(
                [jnp.where(own_is_first, kept, came), jnp.where(own_is_first, came, kept)], axis=0
            )
            r.WA[chip_weights, where] = both.astype(BF16)
        swap.arrived(1)
        kept = r.wi[:, pl.ds(at_128(FF_CORE * c), FF_CORE)].astype(F32)
        came = r.SWAP_R[:, 1536:3072]
        both = jnp.concatenate(
            [jnp.where(own_is_first, kept, came), jnp.where(own_is_first, came, kept)], axis=0
        )
        r.WI[chip_weights, :] = both.astype(BF16)
        swap.arrived(2)

    def mark_documents():
        one_row = lane_iota((1, 128))
        starts = jnp.full((1, 128), FAR, jnp.int32)
        nexts = jnp.full((1, 128), FAR, jnp.int32)
        count = r.docs.shape[0]
        for d in range(count):
            starts = jnp.where(one_row == d, r.docs[d], starts)
            if d:
                nexts = jnp.where(one_row == d - 1, r.docs[d], nexts)
        lanes = lane_iota((CHIP_ROWS, 128))
        for j in range(8):
            place = row_iota((CHIP_ROWS, 128)) + (p.x * HALF_ROWS + (j % 4) * 512 + (j // 4) * 256)
            inside = jnp.logical_and(place >= starts, place < nexts)
            rows = slice(j * CHIP_ROWS, (j + 1) * CHIP_ROWS)
            r.QE[rows, :] = jnp.where(inside, 1.0, 0.0).astype(BF16)
            r.KE[rows, :] = jnp.where(jnp.logical_or(inside, lanes >= 16), 0.0, PENALTY).astype(BF16)

    def spread_vectors():
        gs.complete()
        ga.complete()
        spread_rows = nn(r.WS[...], spread)
        chosen = jnp.where(owner == by_24, spread_rows, 0.0)
        r.VEC[...] = jnp.sum(chosen.reshape(32, 16, D), axis=0)
        part_of = jnp.where(
            jnp.logical_and(kind >= 8, kind < 12), 4 * (owner - 16 * c) + kind - 8, -1000
        )
        for u in (0, 1):
            chosen = jnp.where(part_of - 32 * u == by_24, spread_rows, 0.0)
            r.BIN[0:1, D * u : D * (u + 1)] = jnp.sum(chosen, axis=0, keepdims=True)
        r.WO[:, mine_cols] = r.WA[row_set, 1152:1536]
        swap.start(4, lambda: (r.WA.at[other_set, pl.ds(1152, QUARTER)], r.WO.at[:, mine_cols], p.sibling))

    outer_slot = sems.take(4)

    def outer_swap(z):
        rows = pl.ds(at_16((other * 8 + z * 2) * 192), QUARTER)
        return pltpu.make_async_remote_copy(
            r.WT.at[rows],
            r.WTR.at[pl.ds(at_128(z * QUARTER), QUARTER), mine_cols],
            sems.send.at[outer_slot + z],
            sems.recv.at[outer_slot + z],
            device_id=p.sibling,
            device_id_type=MESH,
        )

    def outer_rows_came(z):
        gt.copy("second", z).wait_recv()
        gt.copy("across", z).wait_recv()
        outer_swap(z).start()
        r.WTR[pl.ds(at_128(z * QUARTER), QUARTER), mine_cols] = r.WT[
            pl.ds(at_16((c * 8 + z * 2) * 192), QUARTER), :
        ]

    def outer_came(step):
        def run():
            if step == 0:
                outer_rows_came(p.z)
                return
            pl.when(p.has_below[step])(lambda: outer_rows_came(p.z - step))
            pl.when(p.has_above[step])(lambda: outer_rows_came(p.z + step))

        return run

    def project(j):
        value_bias = r.VEC[1:2, mine_cols]
        bias = jnp.concatenate([jnp.zeros_like(value_bias), value_bias], axis=1)
        for part in (0, 1):
            rows = pl.ds(at_128((2 * j + part) * CHIP_ROWS), CHIP_ROWS)
            r.QKV[rows, QUARTER:] = (nn(r.X[rows, :], r.WA[:, QUARTER:1152]) + bias).astype(BF16)

    def queries_of(rows):
        value = nn(r.X[rows, :], r.WA[:, 0:QUARTER]) + r.VEC[0:1, mine_cols]
        r.QKV[rows, 0:QUARTER] = value.astype(BF16)

    def chip_queries():
        queries_of(chip)

    def all_queries():
        def block(j, carry):
            queries_of(pl.ds(at_128(j * 512), 512))
            return carry

        lax.fori_loop(0, 4, block, 0)

    def attend(pair):
        query_doc = r.QE[chip, :]
        queries = r.QKV[chip, pair_cols(0, pair)]
        keys = jnp.concatenate([r.QKV[:, pair_cols(QUARTER, pair)], r.KE[...]], axis=1)
        values = r.QKV[:, pair_cols(2 * QUARTER, pair)]
        outputs = []
        for e in (0, 1):
            query = jnp.concatenate([masked(queries, e, 0.125), query_doc], axis=1)
            scores = nt(query, keys)
            top = jnp.max(scores, axis=1, keepdims=True)
            weights = jnp.exp(scores - top)
            total = jnp.sum(weights, axis=1, keepdims=True)
            outputs.append(nn(weights.astype(BF16), values) / total)
            log_total = top + jnp.log(total)
            r.LSE[...] = jnp.where(lanes128 == 2 * pair + e, log_total, r.LSE[...])
        r.ATT[:, pair_cols(0, pair)] = jnp.where(in_head[0], outputs[0], outputs[1]).astype(BF16)

    def first_norm():
        swap.arrived(4)
        swap.arrived(3)

        branch = nn(r.ATT[...], r.WO[...])
        exchange(0, branch)
        swap.arrived(6)
        branch = branch + r.PX_R[0].astype(F32) + vector(2)
        normed, kept_values["inverse"] = normed_of(r.X[chip, :].astype(F32) + branch)
        r.N1[...] = normed
        hidden = normed * vector(3) + vector(4)
        r.HID[...] = hidden
        r.HL[...] = hidden.astype(BF16)

    def inner_layer(first_block):
        def inner_block(j, carry):
            where = pl.ds(at_128(j * QUARTER), QUARTER)
            value = nn(r.HL[...], r.WI[:, where]) + r.BIN[0:1, where]
            phi = 0.5 + 0.5 * lax.erf(value * (0.5**0.5))
            r.ACT[:, where] = (value * phi).astype(BF16)
            r.GV[:, where] = value
            r.GP[:, where] = phi
            return carry

        lax.fori_loop(first_block, first_block + 2, inner_block, 0)

    def second_norm():
        for z in range(4):
            outer_swap(z).wait_recv()

        def outer_block(j, carry):
            where = pl.ds(at_128(j * 256), 256)
            r.PART[:, where] = nn(r.ACT[...], r.WTR[:, where])
            return carry

        lax.fori_loop(0, 3, outer_block, 0)
        exchange(1, r.PART[...])

        def slope_block(j, carry):
            where = pl.ds(at_128(j * QUARTER), QUARTER)
            value = r.GV[:, where]
            density = jnp.exp(value * value * -0.5) * 0.3989422804014327
            r.GP[:, where] = r.GP[:, where] + value * density
            return carry

        lax.fori_loop(0, 4, slope_block, 0)
        swap.arrived(7)
        outer = r.PART[...] + r.PX_R[1].astype(F32) + vector(5)
        normed2, inverse2 = normed_of(r.HID[...] + outer)
        r.HID[...] = normed2 * vector(6) + vector(7)
        r.out[...] = r.HID[own_half, :].astype(BF16)
        grad_out = r.OG[...].astype(F32)
        grad_resid2 = normed_back(grad_out * vector(6), normed2, inverse2)
        r.HID[...] = grad_resid2
        grad_outer = grad_resid2.astype(BF16)
        r.GO[...] = grad_outer

        r.SV[...] = jnp.zeros_like(r.SV)
        r.SV[6:7, :] = column_sum(grad_out * normed2)
        r.SV[7:8, :] = column_sum(grad_out)
        r.SV[5:6, :] = column_sum(grad_outer.astype(F32))

    ri = Reduce(p, sems, r.GI, 48, "y", (r.GI1, r.GI2, r.GI3))
    rj = Reduce(p, sems, r.GJ, 48, "x", (r.GJ1, r.GJ2, r.GJ3))
    rt = Reduce(p, sems, r.GT, 192, "x", (r.GT1, r.GT2, r.GT3))
    rw = Reduce(p, sems, r.GW, 48, "x", (r.GW1, r.GW2, r.GW3))
    rq = Reduce(p, sems, r.GQ, 48, "x", (r.GQ1, r.GQ2, r.GQ3))
    rk = Reduce(p, sems, r.GK, 48, "x", (r.GK1, r.GK2, r.GK3))
    rs = Reduce(p, sems, r.SG, 32, "y", (r.SG1, r.SG2, r.SG3))

    def back_piece(z, across):
        y = 1 - p.y if across else p.y
        return r.DO.at[pl.ds(at_128((y * 4 + z) * CHIP_ROWS), CHIP_ROWS)]

    def stat_piece(z, across):
        y = 1 - p.y if across else p.y
        return r.STAT.at[:, pl.ds(at_128((y * 4 + z) * CHIP_ROWS), CHIP_ROWS)]

    back = Gather(p, sems, back_piece, p.side["y"])
    stat = Gather(p, sems, stat_piece, p.side["y"])
    last = Mover(sems, 7)
    finals = {
        ri: (0, r.FI, r.FI_R, 24),
        rt: (1, r.FT, r.FT_R, 96),
        rw: (2, r.FW, r.FW_R, 24),
        rq: (3, r.FQ, r.FQ_R, 24),
        rk: (4, r.FK, r.FK_R, 24),
        rs: (5, r.FS, r.FS_R, 16),
        rj: (6, r.FJ, r.FJ_R, 24),
    }

    def final(reduce):
        def run():
            index, total, came, rows = finals[reduce]
            total[...] = reduce.result()
            last.start(
                index,
                lambda: (total.at[pl.ds(at_8(rows * other), rows)], came, p.sibling),
            )

        return run

    def outer_gradient():
        def outer_grads(j, carry):
            where = pl.ds(at_128(j * QUARTER), QUARTER)
            mine_rows = pl.ds(at_128(FF_CORE * c + j * QUARTER), QUARTER)
            r.GT_S[where, :] = tn(r.ACT[:, where], r.GO[:, other_cols]).astype(BF16)
            r.GT[mine_rows, :] = tn(r.ACT[:, where], r.GO[:, mine_cols]).astype(BF16)
            return carry

        lax.fori_loop(0, 4, outer_grads, 0)
        swap.start(10, lambda: (r.GT_S, r.GT.at[outer_set], p.sibling))

    def inner_back():
        def inner_back(j, carry):
            where = pl.ds(at_128(j * QUARTER), QUARTER)
            grad = (nt(r.GO[...], r.WTR[where, :]) * r.GP[:, where]).astype(BF16)
            r.GIN[:, where] = grad
            r.BIN[1:2, where] = jnp.sum(grad.astype(F32), axis=0, keepdims=True)
            return carry

        lax.fori_loop(0, 3, inner_back, 0)
        for u in (0, 1):
            r.SV[pl.ds(8 + 2 * c + u, 1), :] = r.BIN[1:2, D * u : D * (u + 1)]

    def inner_back_last():
        where = slice(1152, 1536)
        grad = (nt(r.GO[...], r.WTR[where, :]) * r.GP[:, where]).astype(BF16)
        r.GIN[:, where] = grad
        r.BIN[1:2, where] = jnp.sum(grad.astype(F32), axis=0, keepdims=True)
        r.GJ[...] = tn(r.HL[...], grad).astype(BF16)

    def inner_gradient():
        def inner_grads(j, carry):
            where = pl.ds(at_128(j * QUARTER), QUARTER)
            r.GI[:, where] = tn(r.HL[...], r.GIN[:, where]).astype(BF16)
            return carry

        lax.fori_loop(0, 3, inner_grads, 0)

    def hidden_back():
        def hidden_back(j, carry):
            where = pl.ds(at_128(j * 256), 256)
            r.PART[:, where] = nt(r.GIN[...], r.WI[where, :])
            return carry

        lax.fori_loop(0, 3, hidden_back, 0)
        exchange(2, r.PART[...])

    def first_norm_back():
        swap.arrived(8)
        grad_hidden = r.HID[...] + r.PART[...] + r.PX_R[2].astype(F32)
        normed = r.N1[...]
        grad_resid1 = normed_back(grad_hidden * vector(3), normed, kept_values["inverse"])
        r.SV[3:4, :] = column_sum(grad_hidden * normed)
        r.SV[4:5, :] = column_sum(grad_hidden)
        r.HID[...] = grad_resid1
        grad_branch = grad_resid1.astype(BF16)
        r.GB[...] = grad_branch
        r.SV[2:3, :] = column_sum(grad_branch.astype(F32))
        grad_attended = nt(grad_branch, r.WO[...]).astype(BF16)
        r.DO[chip, :] = grad_attended
        attended = r.ATT[...].astype(F32)
        product = grad_attended.astype(F32) * attended
        for head in range(CORE_HEADS):
            pair = slice(128 * (head // 2), 128 * (head // 2) + 128)
            delta = jnp.sum(jnp.where(in_head[head % 2], product[:, pair], 0.0), axis=1, keepdims=True)
            r.DELTA[...] = jnp.where(lanes128 == head, delta, r.DELTA[...])
        chip_lanes = pl.ds(at_128(chip_base), CHIP_ROWS)
        r.STAT[0:8, chip_lanes] = jnp.transpose(r.LSE[...])[0:8, :]
        r.STAT[8:16, chip_lanes] = jnp.transpose(r.DELTA[...])[0:8, :]

        back.begin()
        stat.begin()

    def output_gradient():
        r.GW_S[...] = tn(r.ATT[...], r.GB[:, other_cols]).astype(BF16)
        r.GW[row_set, :] = tn(r.ATT[...], r.GB[:, mine_cols]).astype(BF16)
        swap.start(11, lambda: (r.GW_S, r.GW.at[row_set], p.sibling))

    def query_back(pair):
        query_doc = r.QE[chip, :]
        queries = r.QKV[chip, pair_cols(0, pair)]
        keys = r.QKV[:, pair_cols(QUARTER, pair)]
        keys_doc = jnp.concatenate([keys, r.KE[...]], axis=1)
        values = r.QKV[:, pair_cols(2 * QUARTER, pair)]
        grads = r.DO[chip, pair_cols(0, pair)]
        outputs = []
        for e in (0, 1):
            pick = lanes128 == 2 * pair + e
            log_total = jnp.sum(jnp.where(pick, r.LSE[...], 0.0), axis=1, keepdims=True)
            delta = jnp.sum(jnp.where(pick, r.DELTA[...], 0.0), axis=1, keepdims=True)
            query = jnp.concatenate([masked(queries, e, 0.125), query_doc], axis=1)
            probs = jnp.exp(nt(query, keys_doc) - log_total)
            grad_probs = nt(masked(grads, e), values)
            grad_scores = (probs * (grad_probs - delta)).astype(BF16)
            outputs.append(nn(grad_scores, keys) * 0.125)
        r.DQKV[:, pair_cols(0, pair)] = jnp.where(in_head[0], outputs[0], outputs[1]).astype(BF16)

    def query_gradient():
        r.GQ[...] = tn(r.X[chip, :], r.DQKV[:, 0:QUARTER]).astype(BF16)

    def key_back(pair):
        key_doc = r.KE[chip, :]
        keys = r.QKV[chip, pair_cols(QUARTER, pair)]
        values = r.QKV[chip, pair_cols(2 * QUARTER, pair)]
        queries = r.QKV[:, pair_cols(0, pair)]
        queries_doc = jnp.concatenate([queries, r.QE[...]], axis=1)
        grads = r.DO[:, pair_cols(0, pair)]
        key_grads, value_grads = [], []
        for e in (0, 1):
            log_total = r.STAT[pl.ds(2 * pair + e, 1), :]
            delta = r.STAT[pl.ds(8 + 2 * pair + e, 1), :]
            key = jnp.concatenate([masked(keys, e, 0.125), key_doc], axis=1)
            probs = jnp.exp(nt(key, queries_doc) - log_total)
            value_grads.append(nn(probs.astype(BF16), grads))
            grad_probs = nt(masked(values, e), grads)
            grad_scores = (probs * (grad_probs - delta)).astype(BF16)
            key_grads.append(nn(grad_scores, queries) * 0.125)
        r.DQKV[:, pair_cols(QUARTER, pair)] = jnp.where(
            in_head[0], key_grads[0], key_grads[1]
        ).astype(BF16)
        r.DQKV[:, pair_cols(2 * QUARTER, pair)] = jnp.where(
            in_head[0], value_grads[0], value_grads[1]
        ).astype(BF16)

    def key_gradients():
        def project_grads(j, carry):
            where = pl.ds(at_128(j * QUARTER), QUARTER)
            source = pl.ds(at_128((j + 1) * QUARTER), QUARTER)
            r.GK[:, where] = tn(r.X[chip, :], r.DQKV[:, source]).astype(BF16)
            return carry

        lax.fori_loop(0, 2, project_grads, 0)

    def tokens_gradient():
        def tokens_back(j, carry):
            where = pl.ds(at_128(j * 256), 256)
            r.PART[:, where] = nt(r.DQKV[...], r.WA[where, 0:1152])
            return carry

        lax.fori_loop(0, 3, tokens_back, 0)
        r.PX_S[3, 0:128, :] = r.PART[sibling_half, :].astype(BF16)
        swap.start(9, lambda: (r.PX_S.at[3, pl.ds(0, 128)], r.PX_R.at[3, pl.ds(0, 128)], p.sibling))

        r.SV[0:1, mine_cols] = jnp.sum(r.DQKV[:, 0:QUARTER].astype(F32), axis=0, keepdims=True)
        r.SV[1:2, mine_cols] = jnp.sum(r.DQKV[:, 2 * QUARTER :].astype(F32), axis=0, keepdims=True)
        by_96, in_96 = lax.div(column, 96), lax.rem(column, 96)
        gather_96 = jnp.where(row_iota((128, D)) == in_96, 1.0, 0.0).astype(BF16)
        sums = jnp.broadcast_to(r.SV[...].reshape(1, 16, D), (32, 16, D)).reshape(512, D)
        late = kind >= 8
        wanted = jnp.where(late, 8 * (kind - 8) + by_96, by_24) == owner
        sums = jnp.where(wanted, sums, 0.0)
        high = sums.astype(BF16)
        low_part = (sums - high.astype(F32)).astype(BF16)
        r.SG[...] = jnp.where(
            late,
            nt(high, gather_96) + nt(low_part, gather_96),
            nt(high, spread) + nt(low_part, spread),
        )

    r.LSE[...] = jnp.zeros_like(r.LSE)
    r.DELTA[...] = jnp.zeros_like(r.DELTA)
    kept24 = pl.ds(at_8(24 * c), 24)

    def early_outputs():
        swap.arrived(9)
        r.tgrad[...] = (
            r.HID[own_half, :] + r.PART[own_half, :] + r.PX_R[3, 0:128, :].astype(F32)
        ).astype(BF16)

        last.arrived(0)
        last.arrived(6)
        r.gi[:, pl.ds(at_128(FF_CORE * c), 1152)] = r.FI[kept24, :]
        r.gi[:, pl.ds(at_128(FF_CORE * other), 1152)] = r.FI_R[...]
        r.gi[:, pl.ds(at_128(FF_CORE * c + 1152), QUARTER)] = r.FJ[kept24, :]
        r.gi[:, pl.ds(at_128(FF_CORE * other + 1152), QUARTER)] = r.FJ_R[...]
        last.arrived(1)
        r.gt[:, mine_cols] = r.FT[pl.ds(at_8(96 * c), 96), :]
        r.gt[:, other_cols] = r.FT_R[...]
        last.arrived(2)
        r.go[:, mine_cols] = r.FW[kept24, :]
        r.go[:, other_cols] = r.FW_R[...]
        last.arrived(3)
        r.gq[:, mine_cols] = r.FQ[kept24, :]
        r.gq[:, other_cols] = r.FQ_R[...]

    forward = [
        first(tok), take_weights, first(gt), z_start(ga, gs), z_start(tok), first(gj), first(gi),
        second(ga, gs), first(ga, gs), second(tok), second(gi), across(0, gj), hop(1, ga, gs),
        across(0, ga, gs), hop(1, tok), hop(2, ga, gs), across(0, gi), across(0, tok), z_start(gi),
        z_start(gt), second(gt), hop(1, gi), second(gj), mark_documents, hop(2, tok),
        across(1, ga, gs), z_start(gj), hop(3, ga, gs), across(1, tok), across(0, gt), hop(3, tok),
        hop(2, gi), across(2, ga, gs), hop(3, gi), hop(1, gj), across(3, ga, gs), hop(1, gt),
        hop(2, gt), across(1, gi), across(2, tok), across(3, tok), tok.complete, outer_came(0),
        hop(2, gj), hop(3, gt), spread_vectors, across(2, gi),
        loop(
            project,
            [
                hop(3, gj), across(3, gi),
            ],
            [
                across(1, gj),
            ],
            [],
        ),
        chip_queries,
        loop(
            attend,
            [
                across(1, gt), across(2, gt),
            ],
            [
                across(2, gj),
            ],
        ),
        across(3, gt), first_norm, gi.complete, lambda: inner_layer(0), across(3, gj),
        outer_came(1), gj.complete, outer_came(2), outer_came(3), lambda: inner_layer(2),
        second_norm,
    ]
    backward = [
        inner_back_last, inner_back, inner_gradient, one(ri), one(rj), outer_gradient,
        lambda: swap.arrived(10), one(rt), two(ri, 1), hidden_back, first_norm_back, two(ri, 2),
        two(ri, 3), output_gradient, all_queries,
        loop(
            query_back,
            [
                two(rt, 2), hop(1, back, stat), hop(2, back, stat), three(rt, 2),
            ],
            [],
        ),
        hop(3, back, stat), two(rj, 1), across(0, back, stat), query_gradient, three(ri, 1),
        across(1, back, stat), two(rj, 2), two(rt, 1), lambda: swap.arrived(11), one(rw),
        two(rt, 3), three(ri, 2), three(ri, 3), two(rj, 3), one(rq), two(rj, 0),
        across(2, back, stat), across(3, back, stat),
        loop(
            key_back,
            [
                two(rw, 1), three(rj, 2),
            ],
            [
                three(rj, 1), three(rt, 1),
            ],
        ),
        three(rt, 3), two(rw, 2), two(rw, 3), key_gradients, one(rk), two(rq, 1), three(rj, 0),
        two(rq, 2), two(rq, 3), three(rw, 2), two(rw, 0), three(rw, 1), tokens_gradient, one(rs),
        three(rw, 3), two(rk, 1), three(rj, 3), two(rs, 1), three(rq, 3), three(rq, 2), two(rs, 2),
        three(rw, 0), final(rw), two(rk, 2), three(rq, 1), two(rs, 3), two(rq, 0), three(rk, 1),
        two(rk, 3), three(rk, 2), two(ri, 0), two(rs, 0), two(rt, 0), two(rk, 0), three(rk, 3),
        three(rq, 0), final(rq), final(rj), three(rs, 1), three(rs, 3), three(rs, 2), three(rt, 0),
        three(ri, 0), final(ri), three(rs, 0), final(rt), three(rk, 0), final(rs), early_outputs,
        final(rk),
    ]
    for step in forward + backward:
        step()

    last.arrived(4)
    for index, ref in enumerate((r.gk, r.gv)):
        where = slice(QUARTER * index, QUARTER * (index + 1))
        ref[:, mine_cols] = r.FK[kept24, where]
        ref[:, other_cols] = r.FK_R[:, where]
    last.arrived(5)
    totals = r.FS[pl.ds(at_8(16 * c), 16), :] + r.FS_R[...]
    inner_total = totals[8:9] + totals[9:10] + totals[10:11] + totals[11:12]
    r.gs[0:8, :] = totals[0:8]
    r.gs[8:16, :] = jnp.broadcast_to(inner_total, (8, 128))

    for z in range(4):
        outer_swap(z).wait_send()
    for mover in (swap, tok, gs, ga, gi, gj, gt, back, stat, ri, rj, rt, rw, rq, rk, rs, last):
        mover.sent()


def hand_out(*refs):
    count = 8
    for source, target in zip(refs[:count], refs[count + 1 :]):
        target[...] = source[...]
    vectors = refs[count]
    for row, target in enumerate(refs[2 * count + 1 :]):
        target[...] = vectors[row, 0 : target.shape[0]]


def slice_body(
    tokens, query_weight, query_bias, key_weight, value_weight, value_bias, output_weight, output_bias,
    first_gain, first_shift, inner_weight, inner_bias, outer_weight, outer_bias, second_gain,
    second_shift, doc_starts, out_grad,
):
    vectors = (
        query_bias, value_bias, output_bias, first_gain, first_shift, outer_bias, second_gain,
        second_shift, inner_bias,
    )
    vectors = tuple(value.reshape(1, -1) for value in vectors)
    shape = jax.ShapeDtypeStruct
    vmem = pl.BlockSpec(memory_space=pltpu.VMEM)
    out_shapes = (
        shape((128, D), BF16), shape((128, D), BF16), shape((24, D), F32), shape((24, D), F32),
        shape((24, D), F32), shape((24, D), F32), shape((24, 3072), F32), shape((96, D), F32),
        shape((16, 128), F32),
    )
    results = pl.pallas_call(
        layer_kernel,
        out_shape=out_shapes,
        in_specs=[vmem] * 17 + [pl.BlockSpec(memory_space=pltpu.SMEM)],
        out_specs=[vmem] * 9,
        scratch_shapes=[pltpu.VMEM(*entry) for entry in SCRATCH.values()]
        + [pltpu.SemaphoreType.DMA((SEM_COUNT,)), pltpu.SemaphoreType.DMA((SEM_COUNT,))],
        compiler_params=pltpu.CompilerParams(
            collective_id=0, has_side_effects=True, vmem_limit_bytes=62 * 2**20
        ),
        name="layer",
    )(
        tokens, out_grad, query_weight, key_weight, value_weight, output_weight, inner_weight,
        outer_weight, *vectors, doc_starts,
    )
    vector_shapes = (shape((24,), F32),) * 8 + (shape((96,), F32),)
    out, tgrad, gq, gk, gv, go, gi, gt, *v = pl.pallas_call(
        hand_out,
        out_shape=out_shapes[:8] + vector_shapes,
        in_specs=[vmem] * 9,
        out_specs=[vmem] * 17,
        name="hand_out",
    )(*results)
    return (
        out, tgrad, gq, v[0], gk, gv, v[1], go, v[2], v[3], v[4], gi, v[8], gt, v[5], v[6], v[7]
    )


def solution(mesh):
    rows, flat = P(("head", "blk"), None), P(("head", "blk"))
    in_specs = (
        rows, rows, flat, rows, rows, flat, rows, flat, flat, flat, rows, flat, rows, flat, flat, flat,
        P(), rows,
    )
    out_specs = (
        rows, rows, rows, flat, rows, rows, flat, rows, flat, flat, flat, rows, flat, rows, flat, flat,
        flat,
    )
    small_slice = mesh.shape["head"] == 2 and mesh.shape["blk"] == 16
    return jax.shard_map(
        slice_body if small_slice else body,
        mesh=mesh,
        in_specs=in_specs,
        out_specs=out_specs,
        check_vma=False,
    )
```

```python
from functools import partial

import jax
import jax.numpy as jnp
from jax import lax
from jax.experimental import pallas as pl
from jax.experimental.pallas import tpu as pltpu
from jax.sharding import PartitionSpec as P

HEAD_DIM = 64


LN_EPS = 1e-12
MASKED_SCORE = -1e30


def doc_numbers(doc_starts, positions):
    covered = (doc_starts[None, :] <= positions[:, None]).astype(jnp.int32)
    return (jnp.sum(covered, axis=1) - 1).astype(jnp.float32)


def dense_product(left_side, right_side):
    return jnp.dot(left_side, right_side, preferred_element_type=jnp.float32)


def product_back(left_side, right_side):
    return lax.dot_general(
        left_side, right_side, (((1,), (1,)), ((), ())), preferred_element_type=jnp.float32
    )


def product_left(left_side, right_side):
    return lax.dot_general(
        left_side, right_side, (((0,), (0,)), ((), ())), preferred_element_type=jnp.float32
    )


def norm_forward(residual, scale_gain, shift_bias):
    row_mean = jnp.mean(residual, axis=-1, keepdims=True)
    centred = residual - row_mean
    variance = jnp.mean(centred * centred, axis=-1, keepdims=True)
    inverse = lax.rsqrt(variance + LN_EPS)
    normed = centred * inverse
    return (normed * scale_gain + shift_bias, normed, inverse)


def norm_backward(grad_output, normed, inverse, scale_gain):
    grad_normed = grad_output * scale_gain
    first_term = jnp.mean(grad_normed, axis=-1, keepdims=True)
    second_term = jnp.mean(grad_normed * normed, axis=-1, keepdims=True)
    grad_input = inverse * (grad_normed - first_term - normed * second_term)
    return (grad_input, jnp.sum(grad_output * normed, axis=0), jnp.sum(grad_output, axis=0))


def split_blocks(rows_array, block_rows):
    return rows_array.reshape(-1, block_rows, rows_array.shape[1] // HEAD_DIM, HEAD_DIM)


def blocks_to_rows(blocked):
    reordered = jnp.transpose(blocked, (0, 2, 1, 3))
    return reordered.reshape(-1, blocked.shape[1] * blocked.shape[3])


def block_scores(query_block, key_block, query_docs, key_docs):
    scores = jnp.einsum(
        "qhd,khd->hqk", query_block, key_block, preferred_element_type=jnp.float32
    ) * HEAD_DIM ** (-0.5)
    allowed = (query_docs[:, None] == key_docs[None, :])[None, :, :]
    return (scores, allowed)


def intersecting(first_docs, second_docs):
    return jnp.logical_and(
        jnp.max(first_docs) >= jnp.min(second_docs), jnp.min(first_docs) <= jnp.max(second_docs)
    )


def keep_state(carried):
    return carried


def forward_update(carried, query_block, query_docs, key_block, value_block, key_docs):
    running_max, row_total, accumulated = carried
    scores, allowed = block_scores(query_block, key_block, query_docs, key_docs)
    scores = jnp.where(allowed, scores, MASKED_SCORE)
    new_max = jnp.maximum(running_max, jnp.max(scores, axis=2))
    decay_factor = jnp.exp(running_max - new_max)
    weights = jnp.where(allowed, jnp.exp(scores - new_max[:, :, None]), 0.0)
    row_total = row_total * decay_factor + jnp.sum(weights, axis=2)
    update = jnp.einsum(
        "hqk,khd->hqd",
        weights.astype(jnp.bfloat16),
        value_block,
        preferred_element_type=jnp.float32,
    )
    return (new_max, row_total, accumulated * decay_factor[:, :, None] + update)


def forward_folder(query_blocks, doc_blocks):
    block_rows = query_blocks.shape[1]

    def forward_fold_step(carried_in, pieces, start_row):
        key_piece, value_piece, key_doc_piece = pieces
        key_blocks = split_blocks(key_piece, block_rows)
        value_blocks = split_blocks(value_piece, block_rows)
        key_doc_blocks = key_doc_piece.astype(jnp.float32).reshape(-1, block_rows)

        def forward_one_block(block_index, carried):
            key_docs = key_doc_blocks[block_index]
            results = []
            for query_index in range(query_blocks.shape[0]):
                current = tuple((member[query_index] for member in carried))
                update = partial(
                    forward_update,
                    query_block=query_blocks[query_index],
                    query_docs=doc_blocks[query_index],
                    key_block=key_blocks[block_index],
                    value_block=value_blocks[block_index],
                    key_docs=key_docs,
                )
                results.append(
                    lax.cond(
                        intersecting(doc_blocks[query_index], key_docs), update, keep_state, current
                    )
                )
            return tuple((jnp.stack([entry[member] for entry in results]) for member in range(3)))

        return lax.fori_loop(0, key_blocks.shape[0], forward_one_block, carried_in)

    return forward_fold_step


def query_grad_update(
    grad_query,
    query_block,
    query_docs,
    grad_block,
    log_total,
    delta_rows,
    key_block,
    value_block,
    key_docs,
):
    scores, allowed = block_scores(query_block, key_block, query_docs, key_docs)
    probs = jnp.where(allowed, jnp.exp(scores - log_total[:, :, None]), 0.0)
    grad_probs = jnp.einsum(
        "qhd,khd->hqk", grad_block, value_block, preferred_element_type=jnp.float32
    )
    grad_scores = (probs * (grad_probs - delta_rows[:, :, None])).astype(jnp.bfloat16)
    return grad_query + jnp.einsum(
        "hqk,khd->hqd", grad_scores, key_block, preferred_element_type=jnp.float32
    ) * HEAD_DIM ** (-0.5)


def query_grad_folder(query_blocks, doc_blocks, grad_blocks, log_blocks, delta_blocks):
    block_rows = query_blocks.shape[1]

    def query_fold_step(carried_in, pieces, start_row):
        key_piece, value_piece, key_doc_piece = pieces
        key_blocks = split_blocks(key_piece, block_rows)
        value_blocks = split_blocks(value_piece, block_rows)
        key_doc_blocks = key_doc_piece.astype(jnp.float32).reshape(-1, block_rows)

        def query_one_block(block_index, carried):
            key_docs = key_doc_blocks[block_index]
            results = []
            for query_index in range(query_blocks.shape[0]):
                update = partial(
                    query_grad_update,
                    query_block=query_blocks[query_index],
                    query_docs=doc_blocks[query_index],
                    grad_block=grad_blocks[query_index],
                    log_total=log_blocks[query_index],
                    delta_rows=delta_blocks[query_index],
                    key_block=key_blocks[block_index],
                    value_block=value_blocks[block_index],
                    key_docs=key_docs,
                )
                results.append(
                    lax.cond(
                        intersecting(doc_blocks[query_index], key_docs),
                        update,
                        keep_state,
                        carried[query_index],
                    )
                )
            return jnp.stack(results)

        return lax.fori_loop(0, key_blocks.shape[0], query_one_block, carried_in)

    return query_fold_step


def key_grad_update(
    carried,
    key_block,
    value_block,
    key_docs,
    query_block,
    grad_block,
    log_total,
    delta_rows,
    query_docs,
):
    grad_key, grad_value = carried
    scores, allowed = block_scores(query_block, key_block, query_docs, key_docs)
    probs = jnp.where(allowed, jnp.exp(scores - log_total[:, :, None]), 0.0)
    grad_value = grad_value + jnp.einsum(
        "hqk,qhd->hkd", probs.astype(jnp.bfloat16), grad_block, preferred_element_type=jnp.float32
    )
    grad_probs = jnp.einsum(
        "qhd,khd->hqk", grad_block, value_block, preferred_element_type=jnp.float32
    )
    grad_scores = (probs * (grad_probs - delta_rows[:, :, None])).astype(jnp.bfloat16)
    grad_key = grad_key + jnp.einsum(
        "hqk,qhd->hkd", grad_scores, query_block, preferred_element_type=jnp.float32
    ) * HEAD_DIM ** (-0.5)
    return (grad_key, grad_value)


def key_grad_folder(key_blocks, value_blocks, doc_blocks):
    block_rows = key_blocks.shape[1]

    def key_fold_step(carried_in, pieces, start_row):
        query_piece, grad_piece, log_piece, delta_piece, doc_piece = pieces
        query_blocks = split_blocks(query_piece.astype(jnp.bfloat16), block_rows)
        grad_blocks = split_blocks(grad_piece.astype(jnp.bfloat16), block_rows)
        log_blocks = jnp.transpose(log_piece.reshape(-1, block_rows, log_piece.shape[1]), (0, 2, 1))
        delta_blocks = jnp.transpose(
            delta_piece.reshape(-1, block_rows, delta_piece.shape[1]), (0, 2, 1)
        )
        query_doc_blocks = doc_piece.reshape(-1, block_rows)

        def key_one_block(block_index, carried):
            query_docs = query_doc_blocks[block_index]
            results = []
            for key_index in range(key_blocks.shape[0]):
                current = (carried[0][key_index], carried[1][key_index])
                update = partial(
                    key_grad_update,
                    key_block=key_blocks[key_index],
                    value_block=value_blocks[key_index],
                    key_docs=doc_blocks[key_index],
                    query_block=query_blocks[block_index],
                    grad_block=grad_blocks[block_index],
                    log_total=log_blocks[block_index],
                    delta_rows=delta_blocks[block_index],
                    query_docs=query_docs,
                )
                results.append(
                    lax.cond(
                        intersecting(query_docs, doc_blocks[key_index]), update, keep_state, current
                    )
                )
            return (
                jnp.stack([entry[0] for entry in results]),
                jnp.stack([entry[1] for entry in results]),
            )

        return lax.fori_loop(0, query_blocks.shape[0], key_one_block, carried_in)

    return key_fold_step


def attention_forward(query_rows, key_rows, value_rows, row_docs, block_rows):
    query_blocks = split_blocks(query_rows, block_rows)
    doc_blocks = row_docs.reshape(-1, block_rows)
    block_count = query_blocks.shape[0]
    head_count = query_blocks.shape[2]
    send_docs = row_docs.astype(jnp.bfloat16)
    start_state = (
        jnp.full((block_count, head_count, block_rows), MASKED_SCORE, jnp.float32),
        jnp.zeros((block_count, head_count, block_rows), jnp.float32),
        jnp.zeros((block_count, head_count, block_rows, HEAD_DIM), jnp.float32),
    )
    fold_forward = forward_folder(query_blocks, doc_blocks)
    running_max, row_total, accumulated = fold_forward(
        start_state,
        (
            lax.all_gather(key_rows, "blk", axis=0, tiled=True),
            lax.all_gather(value_rows, "blk", axis=0, tiled=True),
            lax.all_gather(send_docs, "blk", axis=0, tiled=True),
        ),
        jnp.int32(0),
    )
    head_outputs = blocks_to_rows(accumulated / row_total[:, :, :, None]).astype(jnp.bfloat16)
    log_total = running_max + jnp.log(row_total)
    return (head_outputs, log_total)


def attention_backward(
    grad_rows, head_outputs, log_total, query_rows, key_rows, value_rows, row_docs, block_rows
):
    query_blocks = split_blocks(query_rows, block_rows)
    key_blocks = split_blocks(key_rows, block_rows)
    value_blocks = split_blocks(value_rows, block_rows)
    doc_blocks = row_docs.reshape(-1, block_rows)
    block_count = query_blocks.shape[0]
    head_count = query_blocks.shape[2]
    send_docs = row_docs.astype(jnp.bfloat16)
    grad_blocks = split_blocks(grad_rows, block_rows)
    output_blocks = split_blocks(head_outputs, block_rows)
    delta_blocks = jnp.einsum(
        "nqhd,nqhd->nhq", grad_blocks.astype(jnp.float32), output_blocks.astype(jnp.float32)
    )
    log_rows = jnp.transpose(log_total, (0, 2, 1)).reshape(-1, head_count)
    delta_rows = jnp.transpose(delta_blocks, (0, 2, 1)).reshape(-1, head_count)
    fold_queries = query_grad_folder(query_blocks, doc_blocks, grad_blocks, log_total, delta_blocks)
    fold_keys = key_grad_folder(key_blocks, value_blocks, doc_blocks)
    query_start = jnp.zeros((block_count, head_count, block_rows, HEAD_DIM), jnp.float32)
    key_start = (query_start, query_start)
    query_send = (
        query_rows.astype(jnp.float32),
        grad_rows.astype(jnp.float32),
        log_rows,
        delta_rows,
        row_docs,
    )
    grad_query_state = fold_queries(
        query_start,
        (
            lax.all_gather(key_rows, "blk", axis=0, tiled=True),
            lax.all_gather(value_rows, "blk", axis=0, tiled=True),
            lax.all_gather(send_docs, "blk", axis=0, tiled=True),
        ),
        jnp.int32(0),
    )
    grad_key_state, grad_value_state = fold_keys(
        key_start,
        (
            lax.all_gather(query_send[0], "blk", axis=0, tiled=True),
            lax.all_gather(query_send[1], "blk", axis=0, tiled=True),
            lax.all_gather(query_send[2], "blk", axis=0, tiled=True),
            lax.all_gather(query_send[3], "blk", axis=0, tiled=True),
            lax.all_gather(query_send[4], "blk", axis=0, tiled=True),
        ),
        jnp.int32(0),
    )
    return (
        blocks_to_rows(grad_query_state).astype(jnp.bfloat16),
        blocks_to_rows(grad_key_state).astype(jnp.bfloat16),
        blocks_to_rows(grad_value_state).astype(jnp.bfloat16),
    )


def data_layer(tokens, full, row_docs, out_grad, block_rows):
    (
        full_query,
        full_query_bias,
        full_key,
        full_value,
        full_value_bias,
        full_output,
        full_output_bias,
        full_first_gain,
        full_first_shift,
        full_inner,
        full_inner_bias,
        full_outer,
        full_outer_bias,
        full_second_gain,
        full_second_shift,
    ) = full
    queries = (dense_product(tokens, full_query) + full_query_bias.astype(jnp.float32)).astype(
        jnp.bfloat16
    )
    keys_local = dense_product(tokens, full_key).astype(jnp.bfloat16)
    values_local = (dense_product(tokens, full_value) + full_value_bias.astype(jnp.float32)).astype(
        jnp.bfloat16
    )
    query_rows, key_rows, value_rows = (
        lax.all_to_all(queries, "head", split_axis=1, concat_axis=0, tiled=True),
        lax.all_to_all(keys_local, "head", split_axis=1, concat_axis=0, tiled=True),
        lax.all_to_all(values_local, "head", split_axis=1, concat_axis=0, tiled=True),
    )
    head_outputs, log_total = attention_forward(
        query_rows, key_rows, value_rows, row_docs, block_rows
    )
    attended = lax.all_to_all(head_outputs, "head", split_axis=0, concat_axis=1, tiled=True)
    branch = dense_product(attended, full_output) + full_output_bias.astype(jnp.float32)
    hidden, first_normed, first_inverse = norm_forward(
        tokens.astype(jnp.float32) + branch,
        full_first_gain.astype(jnp.float32),
        full_first_shift.astype(jnp.float32),
    )
    hidden_low = hidden.astype(jnp.bfloat16)
    inner_value = dense_product(hidden_low, full_inner) + full_inner_bias.astype(jnp.float32)
    activated_full, gelu_pullback = jax.vjp(partial(jax.nn.gelu, approximate=False), inner_value)
    activated = activated_full.astype(jnp.bfloat16)
    outer_value = dense_product(activated, full_outer) + full_outer_bias.astype(jnp.float32)
    layer_full, second_normed, second_inverse = norm_forward(
        hidden + outer_value,
        full_second_gain.astype(jnp.float32),
        full_second_shift.astype(jnp.float32),
    )
    layer_out = layer_full.astype(jnp.bfloat16)
    grad_output = out_grad.astype(jnp.float32)
    grad_resid2, second_gain_term, second_shift_term = norm_backward(
        grad_output, second_normed, second_inverse, full_second_gain.astype(jnp.float32)
    )
    grad_outer = grad_resid2.astype(jnp.bfloat16)
    outer_weight_term = product_left(activated, grad_outer)
    outer_bias_term = jnp.sum(grad_outer.astype(jnp.float32), axis=0)
    grad_inner = gelu_pullback(product_back(grad_outer, full_outer))[0].astype(jnp.bfloat16)
    inner_weight_term = product_left(hidden_low, grad_inner)
    inner_bias_term = jnp.sum(grad_inner.astype(jnp.float32), axis=0)
    grad_hidden = grad_resid2 + product_back(grad_inner, full_inner)
    grad_resid1, first_gain_term, first_shift_term = norm_backward(
        grad_hidden, first_normed, first_inverse, full_first_gain.astype(jnp.float32)
    )
    grad_branch = grad_resid1.astype(jnp.bfloat16)
    output_weight_term = product_left(attended, grad_branch)
    output_bias_term = jnp.sum(grad_branch.astype(jnp.float32), axis=0)
    grad_attended = product_back(grad_branch, full_output).astype(jnp.bfloat16)
    grad_rows = lax.all_to_all(grad_attended, "head", split_axis=1, concat_axis=0, tiled=True)
    grad_query_rows, grad_key_rows, grad_value_rows = attention_backward(
        grad_rows, head_outputs, log_total, query_rows, key_rows, value_rows, row_docs, block_rows
    )
    grad_queries, grad_keys, grad_values = (
        lax.all_to_all(grad_query_rows, "head", split_axis=0, concat_axis=1, tiled=True),
        lax.all_to_all(grad_key_rows, "head", split_axis=0, concat_axis=1, tiled=True),
        lax.all_to_all(grad_value_rows, "head", split_axis=0, concat_axis=1, tiled=True),
    )
    query_weight_term = product_left(tokens, grad_queries)
    query_bias_term = jnp.sum(grad_queries.astype(jnp.float32), axis=0)
    key_weight_term = product_left(tokens, grad_keys)
    value_weight_term = product_left(tokens, grad_values)
    value_bias_term = jnp.sum(grad_values.astype(jnp.float32), axis=0)
    tokens_grad = (
        grad_resid1
        + product_back(grad_queries, full_query)
        + product_back(grad_keys, full_key)
        + product_back(grad_values, full_value)
    ).astype(jnp.bfloat16)
    summed = (
        lax.psum_scatter(query_weight_term, ("head", "blk"), scatter_dimension=0, tiled=True),
        lax.psum_scatter(query_bias_term, ("head", "blk"), scatter_dimension=0, tiled=True),
        lax.psum_scatter(key_weight_term, ("head", "blk"), scatter_dimension=0, tiled=True),
        lax.psum_scatter(value_weight_term, ("head", "blk"), scatter_dimension=0, tiled=True),
        lax.psum_scatter(value_bias_term, ("head", "blk"), scatter_dimension=0, tiled=True),
        lax.psum_scatter(output_weight_term, ("head", "blk"), scatter_dimension=0, tiled=True),
        lax.psum_scatter(output_bias_term, ("head", "blk"), scatter_dimension=0, tiled=True),
        lax.psum_scatter(first_gain_term, ("head", "blk"), scatter_dimension=0, tiled=True),
        lax.psum_scatter(first_shift_term, ("head", "blk"), scatter_dimension=0, tiled=True),
        lax.psum_scatter(inner_weight_term, ("head", "blk"), scatter_dimension=0, tiled=True),
        lax.psum_scatter(inner_bias_term, ("head", "blk"), scatter_dimension=0, tiled=True),
        lax.psum_scatter(outer_weight_term, ("head", "blk"), scatter_dimension=0, tiled=True),
        lax.psum_scatter(outer_bias_term, ("head", "blk"), scatter_dimension=0, tiled=True),
        lax.psum_scatter(second_gain_term, ("head", "blk"), scatter_dimension=0, tiled=True),
        lax.psum_scatter(second_shift_term, ("head", "blk"), scatter_dimension=0, tiled=True),
    )
    return (layer_out, tokens_grad) + tuple(summed)


def body(
    tokens,
    query_weight,
    query_bias,
    key_weight,
    value_weight,
    value_bias,
    output_weight,
    output_bias,
    first_gain,
    first_shift,
    inner_weight,
    inner_bias,
    outer_weight,
    outer_bias,
    second_gain,
    second_shift,
    doc_starts,
    out_grad,
):
    shards = (
        query_weight,
        query_bias,
        key_weight,
        value_weight,
        value_bias,
        output_weight,
        output_bias,
        first_gain,
        first_shift,
        inner_weight,
        inner_bias,
        outer_weight,
        outer_bias,
        second_gain,
        second_shift,
    )
    full = (
        lax.all_gather(shards[0], ("head", "blk"), axis=0, tiled=True),
        lax.all_gather(shards[1], ("head", "blk"), axis=0, tiled=True),
        lax.all_gather(shards[2], ("head", "blk"), axis=0, tiled=True),
        lax.all_gather(shards[3], ("head", "blk"), axis=0, tiled=True),
        lax.all_gather(shards[4], ("head", "blk"), axis=0, tiled=True),
        lax.all_gather(shards[5], ("head", "blk"), axis=0, tiled=True),
        lax.all_gather(shards[6], ("head", "blk"), axis=0, tiled=True),
        lax.all_gather(shards[7], ("head", "blk"), axis=0, tiled=True),
        lax.all_gather(shards[8], ("head", "blk"), axis=0, tiled=True),
        lax.all_gather(shards[9], ("head", "blk"), axis=0, tiled=True),
        lax.all_gather(shards[10], ("head", "blk"), axis=0, tiled=True),
        lax.all_gather(shards[11], ("head", "blk"), axis=0, tiled=True),
        lax.all_gather(shards[12], ("head", "blk"), axis=0, tiled=True),
        lax.all_gather(shards[13], ("head", "blk"), axis=0, tiled=True),
        lax.all_gather(shards[14], ("head", "blk"), axis=0, tiled=True),
    )
    tok_rows = tokens.shape[0]
    half_length = tok_rows * lax.axis_size("blk")
    blk_place = lax.axis_index("blk")
    offsets = jnp.arange(tok_rows, dtype=jnp.int32)
    row_positions = jnp.concatenate(
        [blk_place * tok_rows + offsets, half_length + blk_place * tok_rows + offsets]
    )
    row_docs = doc_numbers(doc_starts, row_positions)
    return data_layer(tokens, full, row_docs, out_grad, tok_rows)


MESH = pl.DeviceIdType.MESH
F32 = jnp.float32
BF16 = jnp.bfloat16
D = 768
QUARTER = 384
FF_CORE = 1536
HALF_ROWS = 2048
CHIP_ROWS = 256
CORE_HEADS = 6
PENALTY = -1e30
FAR = 2**30


def nn(a, b):
    return lax.dot_general(a, b, (((1,), (0,)), ((), ())), preferred_element_type=F32)


def nt(a, b):
    return lax.dot_general(a, b, (((1,), (1,)), ((), ())), preferred_element_type=F32)


def tn(a, b):
    return lax.dot_general(a, b, (((0,), (0,)), ((), ())), preferred_element_type=F32)


def at_128(index):
    return pl.multiple_of(index, 128)


def at_16(index):
    return pl.multiple_of(index, 16)


def at_8(index):
    return pl.multiple_of(index, 8)


class Place:
    def __init__(self):
        self.x = lax.axis_index("head")
        b = lax.axis_index("blk")
        self.z = lax.div(b, 4)
        self.y = lax.rem(lax.div(b, 2), 2)
        self.c = lax.rem(b, 2)
        self.chip = self.x * 8 + self.z * 2 + self.y
        self.slot = self.y * 4 + self.z
        self.ups = [self.z] + [lax.rem(self.z + k, 4) for k in (1, 2, 3)]
        self.downs = [self.ups[0], self.ups[3], self.ups[2], self.ups[1]]
        self.above = self.device(z=jnp.minimum(self.z + 1, 3))
        self.below = self.device(z=jnp.maximum(self.z - 1, 0))
        self.can_up, self.can_down = self.z < 3, self.z > 0
        self.has_below = [None] + [self.z >= step for step in (1, 2, 3)]
        self.has_above = [None] + [self.z <= 3 - step for step in (1, 2, 3)]
        self.sibling = self.device(c=1 - self.c)
        self.side = {"x": self.device(x=1 - self.x), "y": self.device(y=1 - self.y)}

    def device(self, x=None, z=None, y=None, c=None):
        x = self.x if x is None else x
        z = self.z if z is None else z
        y = self.y if y is None else y
        c = self.c if c is None else c
        return (x, z * 4 + y * 2 + c)

    def up(self, k):
        return self.ups[k]

    def down(self, k):
        return self.downs[k]


class Sems:
    def __init__(self, send, recv):
        self.send, self.recv, self.used = send, recv, 0

    def take(self, count):
        first = self.used
        self.used += count
        assert self.used <= self.send.shape[0]
        return first


class Mover:
    def __init__(self, sems, count):
        self.sems, self.first, self.parts = sems, sems.take(count), {}

    def copy(self, index):
        place = self.first + index
        src, dst, device = self.parts[index]()
        return pltpu.make_async_remote_copy(
            src,
            dst,
            self.sems.send.at[place],
            self.sems.recv.at[place],
            device_id=device,
            device_id_type=MESH,
        )

    def start(self, index, part):
        self.parts[index] = part
        self.copy(index).start()

    def arrived(self, index):
        self.copy(index).wait_recv()

    def sent(self):
        for index in sorted(self.parts):
            self.copy(index).wait_send()


class Gather:
    def __init__(self, place, sems, piece, first, second=None):
        self.place, self.sems, self.piece = place, sems, piece
        self.device = {"up": place.above, "down": place.below, "first": first}
        if second is not None:
            self.device.update(second=second, across=second)
        self.slot = {kind: sems.take(4) for kind in self.device}

    def copy(self, kind, z):
        place = self.slot[kind] + z
        piece = self.piece(z, kind == "across")
        return pltpu.make_async_remote_copy(
            piece,
            piece,
            self.sems.send.at[place],
            self.sems.recv.at[place],
            device_id=self.device[kind],
            device_id_type=MESH,
        )

    def sideways(self, z):
        self.copy("first", z).start()
        if "second" in self.device:
            self.copy("second", z).start()

    def begin_z(self):
        p = self.place

        @pl.when(p.can_up)
        def _():
            self.copy("up", p.z).start()

        @pl.when(p.can_down)
        def _():
            self.copy("down", p.z).start()

    def begin(self):
        self.begin_z()
        self.sideways(self.place.z)

    def hop(self, step):
        p = self.place

        @pl.when(p.has_below[step])
        def _():
            z = p.z - step
            self.copy("up", z).wait_recv()

            @pl.when(p.can_up)
            def _():
                self.copy("up", z).start()

            self.sideways(z)

        @pl.when(p.has_above[step])
        def _():
            z = p.z + step
            self.copy("down", z).wait_recv()

            @pl.when(p.can_down)
            def _():
                self.copy("down", z).start()

            self.sideways(z)

    def across_one(self, z):
        self.copy("first", z).wait_recv()
        if "second" in self.device:
            self.copy("across", z).start()

    def across(self, step):
        p = self.place
        if step == 0:
            self.across_one(p.z)
            return

        @pl.when(p.has_below[step])
        def _():
            self.across_one(p.z - step)

        @pl.when(p.has_above[step])
        def _():
            self.across_one(p.z + step)

    def complete(self):
        for z in range(4):
            self.copy("second", z).wait_recv()
            self.copy("across", z).wait_recv()

    def sent(self):
        p = self.place
        for z in range(4):
            for kind in self.device:
                wait = self.copy(kind, z).wait_send
                if kind == "up":
                    pl.when(jnp.logical_and(p.can_up, p.z >= z))(wait)
                elif kind == "down":
                    pl.when(jnp.logical_and(p.can_down, p.z <= z))(wait)
                else:
                    wait()


class Reduce(Mover):
    def __init__(self, place, sems, ref, rows, first, slots):
        super().__init__(sems, 15)
        self.place, self.ref, self.rows, self.axis = place, ref, rows, first
        self.one, self.two, self.three = slots

    def rows_of(self, x, z, y, count=1):
        return pl.ds(at_8((x * 8 + z * 2 + y) * self.rows), count * self.rows)

    def send_one(self, k):
        p, R = self.place, self.rows
        if self.axis == "x":

            def part():
                where = self.rows_of(1 - p.x, p.up(k), 0, 2)
                return self.ref.at[where], self.one.at[k], p.side["x"]

            self.start(2 * k, part)
        else:
            for xx in (0, 1):

                def part(xx=xx):
                    where = self.rows_of(xx, p.up(k), 1 - p.y)
                    return self.ref.at[where], self.one.at[k, pl.ds(xx * R, R)], p.side["y"]

                self.start(2 * k + xx, part)

    def add(self, where, term):
        self.ref[where] = (self.ref[where].astype(F32) + term.astype(F32)).astype(self.ref.dtype)

    def send_two(self, k):
        p, R = self.place, self.rows
        if self.axis == "x":
            self.arrived(2 * k)
            self.add(self.rows_of(p.x, p.up(k), 0, 2), self.one[k])

            def part():
                where = self.rows_of(p.x, p.up(k), 1 - p.y)
                return self.ref.at[where], self.two.at[k], p.side["y"]

        else:
            for xx in (0, 1):
                self.arrived(2 * k + xx)
                self.add(self.rows_of(xx, p.up(k), p.y), self.one[k, xx * R : (xx + 1) * R])

            def part():
                where = self.rows_of(1 - p.x, p.up(k), p.y)
                return self.ref.at[where], self.two.at[k], p.side["x"]

        self.start(8 + k, part)

    def send_three(self, k):
        p = self.place
        self.arrived(8 + k)
        if k:
            self.add(self.rows_of(p.x, p.up(k), p.y), self.two[k])

            def part():
                where = self.rows_of(p.x, p.up(k), p.y)
                return self.ref.at[where], self.three.at[k - 1], p.device(z=p.up(k))

            self.start(12 + k - 1, part)

    def result(self):
        p = self.place
        total = self.ref[self.rows_of(p.x, p.z, p.y)].astype(F32) + self.two[0].astype(F32)
        for k in (1, 2, 3):
            self.arrived(12 + k - 1)
            total = total + self.three[k - 1].astype(F32)
        return total


def z_start(*gathers):
    return lambda: [gather.begin_z() for gather in gathers]


def first(*gathers):
    return lambda: [gather.copy("first", gather.place.z).start() for gather in gathers]


def second(*gathers):
    return lambda: [gather.copy("second", gather.place.z).start() for gather in gathers]


def hop(step, *gathers):
    return lambda: [gather.hop(step) for gather in gathers]


def across(step, *gathers):
    return lambda: [gather.across(step) for gather in gathers]


def one(*reduces):
    return lambda: [reduce.send_one(k) for k in ORDER for reduce in reduces]


def two(reduce, k):
    return lambda: reduce.send_two(k)


def three(reduce, k):
    return lambda: reduce.send_three(k)


def loop(action, *between):
    def run():
        def step(j, carry):
            for i, steps in enumerate(between):

                @pl.when(j == i + 1)
                def _(steps=steps):
                    for inside in steps:
                        inside()

            action(j)
            return carry

        lax.fori_loop(0, len(between) + 1, step, 0)

    return run


def row_mean(value):
    return jnp.sum(value, axis=1, keepdims=True) * (1.0 / D)


def normed_of(residual):
    centred = residual - row_mean(residual)
    inverse = lax.rsqrt(row_mean(centred * centred) + LN_EPS)
    return centred * inverse, inverse


def normed_back(grad_normed, normed, inverse):
    return inverse * (grad_normed - row_mean(grad_normed) - normed * row_mean(grad_normed * normed))


def lane_iota(shape):
    return lax.broadcasted_iota(jnp.int32, shape, len(shape) - 1)


def row_iota(shape):
    return lax.broadcasted_iota(jnp.int32, shape, 0)


SCRATCH = dict(
    X=((HALF_ROWS, D), BF16),
    SMALL=((16, 128), F32),
    WS=((512, 128), BF16),
    WA=((D, 1536), BF16),
    WI=((D, FF_CORE), BF16),
    WT=((2 * FF_CORE, QUARTER), BF16),
    WO=((QUARTER, D), BF16),
    WTR=((FF_CORE, D), BF16),
    OG=((CHIP_ROWS, D), BF16),
    SWAP_S=((24, 3072), F32),
    SWAP_R=((24, 3072), F32),
    QKV=((HALF_ROWS, 1152), BF16),
    QE=((HALF_ROWS, 128), BF16),
    KE=((HALF_ROWS, 128), BF16),
    ATT=((CHIP_ROWS, QUARTER), BF16),
    LSE=((CHIP_ROWS, 128), F32),
    DELTA=((CHIP_ROWS, 128), F32),
    VEC=((16, D), F32),
    BIN=((8, FF_CORE), F32),
    DO=((HALF_ROWS, QUARTER), BF16),
    STAT=((16, HALF_ROWS), F32),
    PX_S=((4, CHIP_ROWS, D), BF16),
    PX_R=((4, CHIP_ROWS, D), BF16),
    PART=((CHIP_ROWS, D), F32),
    HID=((CHIP_ROWS, D), F32),
    N1=((CHIP_ROWS, D), F32),
    N2=((CHIP_ROWS, D), F32),
    GH=((CHIP_ROWS, D), F32),
    HL=((CHIP_ROWS, D), BF16),
    ACT=((CHIP_ROWS, FF_CORE), BF16),
    GP=((CHIP_ROWS, FF_CORE), F32),
    GV=((CHIP_ROWS, FF_CORE), F32),
    GIN=((CHIP_ROWS, FF_CORE), BF16),
    GO=((CHIP_ROWS, D), BF16),
    GB=((CHIP_ROWS, D), BF16),
    DQKV=((CHIP_ROWS, 1152), BF16),
    SV=((16, D), F32),
    GI=((D, 1152), BF16),
    GJ=((D, QUARTER), BF16),
    GT=((2 * FF_CORE, QUARTER), BF16),
    GT_S=((FF_CORE, QUARTER), BF16),
    GW=((D, QUARTER), BF16),
    GW_S=((QUARTER, QUARTER), BF16),
    GQ=((D, QUARTER), BF16),
    GK=((D, D), BF16),
    SG=((512, 128), F32),
    GI1=((4, 96, 1152), BF16),
    GI2=((4, 48, 1152), BF16),
    GI3=((3, 48, 1152), BF16),
    GJ1=((4, 96, QUARTER), BF16),
    GJ2=((4, 48, QUARTER), BF16),
    GJ3=((3, 48, QUARTER), BF16),
    GT1=((4, 384, QUARTER), BF16),
    GT2=((4, 192, QUARTER), BF16),
    GT3=((3, 192, QUARTER), BF16),
    GW1=((4, 96, QUARTER), BF16),
    GW2=((4, 48, QUARTER), BF16),
    GW3=((3, 48, QUARTER), BF16),
    GQ1=((4, 96, QUARTER), BF16),
    GQ2=((4, 48, QUARTER), BF16),
    GQ3=((3, 48, QUARTER), BF16),
    GK1=((4, 96, D), BF16),
    GK2=((4, 48, D), BF16),
    GK3=((3, 48, D), BF16),
    SG1=((4, 64, 128), F32),
    SG2=((4, 32, 128), F32),
    SG3=((3, 32, 128), F32),
    FI=((48, 1152), F32),
    FJ=((48, QUARTER), F32),
    FT=((192, QUARTER), F32),
    FW=((48, QUARTER), F32),
    FQ=((48, QUARTER), F32),
    FK=((48, D), F32),
    FS=((32, 128), F32),
    FI_R=((24, 1152), F32),
    FJ_R=((24, QUARTER), F32),
    FT_R=((96, QUARTER), F32),
    FW_R=((24, QUARTER), F32),
    FQ_R=((24, QUARTER), F32),
    FK_R=((24, D), F32),
    FS_R=((16, 128), F32),
)
SEM_COUNT = 310
ORDER = (1, 2, 3, 0)


class Refs:
    pass


def layer_kernel(*refs):
    r = Refs()
    (
        r.tok, r.og, r.wq, r.wk, r.wv, r.wo, r.wi, r.wt, *vectors, r.docs,
        r.out, r.tgrad, r.gq, r.gk, r.gv, r.go, r.gi, r.gt, r.gs,
    ) = refs[:27]
    for name, ref in zip(SCRATCH, refs[27:]):
        setattr(r, name, ref)
    sems = Sems(refs[-2], refs[-1])
    p = Place()
    c, other = p.c, 1 - p.c

    barrier = pltpu.get_barrier_semaphore()
    partners = [p.sibling, p.side["x"], p.side["y"]] + [p.device(z=p.up(k)) for k in (1, 2, 3)]
    for partner in partners:
        pl.semaphore_signal(barrier, inc=1, device_id=partner, device_id_type=MESH)
    pl.semaphore_wait(barrier, len(partners))

    swap = Mover(sems, 16)
    chip_base = p.slot * CHIP_ROWS
    own_base = chip_base + 128 * c
    chip = pl.ds(at_128(chip_base), CHIP_ROWS)
    own_half = pl.ds(at_128(128 * c), 128)

    cols = [pl.ds(at_128(QUARTER * side), QUARTER) for side in (0, 1)]
    mine_cols = pl.ds(at_128(QUARTER * c), QUARTER)
    other_cols = pl.ds(at_128(QUARTER * other), QUARTER)
    for index, ref in enumerate((r.wq, r.wk, r.wv, r.wo)):
        r.SWAP_S[:, QUARTER * index : QUARTER * (index + 1)] = ref[:, other_cols].astype(F32)
    r.SWAP_S[:, 1536:3072] = r.wi[:, pl.ds(at_128(FF_CORE * other), FF_CORE)].astype(F32)
    swap.start(0, lambda: (r.SWAP_S, r.SWAP_R, p.sibling))
    r.X[pl.ds(at_128(own_base), 128), :] = r.tok[...]

    def tok_piece(z, across):
        y = 1 - p.y if across else p.y
        return r.X.at[pl.ds(at_128((y * 4 + z) * CHIP_ROWS + 128 * c), 128)]

    tok = Gather(p, sems, tok_piece, p.side["y"], p.sibling)

    small_rows = r.WS.at[pl.ds(at_16(32 * p.chip + 16 * c), 16)]
    r.SMALL[...] = jnp.zeros_like(r.SMALL)
    for index, ref in enumerate(vectors[:8]):
        r.SMALL[index : index + 1, 0:24] = ref[...].astype(F32)
    inner_vector = vectors[8][...].astype(F32)
    for index in range(4):
        r.SMALL[8 + index : 9 + index, 0:24] = inner_vector[:, 24 * index : 24 * index + 24]
    r.WS[pl.ds(at_16(32 * p.chip + 16 * c), 16), :] = r.SMALL[...].astype(BF16)
    swap.start(1, lambda: (small_rows, small_rows, p.sibling))
    outer_rows = pl.ds(at_16(192 * p.chip + 96 * c), 96)
    r.WT[outer_rows, :] = r.wt[:, mine_cols]
    swap.start(2, lambda: (r.wt.at[:, other_cols], r.WT.at[outer_rows], p.sibling))
    og_rows = r.OG.at[own_half]
    r.OG[own_half, :] = r.og[...]
    swap.start(3, lambda: (og_rows, og_rows, p.sibling))

    def weights(ref, rows, first, cols=slice(None)):
        def piece(z, across):
            x, y = p.x, p.y
            if across:
                x, y = (x, 1 - y) if first == "y" else (1 - x, y)
            return ref.at[pl.ds(at_16((x * 8 + z * 2 + y) * rows), rows), cols]

        return Gather(p, sems, piece, p.side[first], p.side["y" if first == "x" else "x"])

    gs = weights(r.WS, 32, "y")
    ga = weights(r.WA, 48, "y")
    gi = weights(r.WI, 48, "y", pl.ds(0, D))
    gj = weights(r.WI, 48, "y", pl.ds(D, D))
    gt = weights(r.WT, 192, "x")

    column = lane_iota((1, D))
    by_24, in_24 = lax.div(column, 24), lax.rem(column, 24)
    spread = jnp.where(row_iota((128, D)) == in_24, 1.0, 0.0).astype(BF16)
    row = row_iota((512, 1))
    owner, kind = lax.shift_right_logical(row, 4), jnp.bitwise_and(row, 15)
    row_set = pl.ds(at_128(QUARTER * c), QUARTER)
    other_set = pl.ds(at_128(QUARTER * other), QUARTER)
    outer_set = pl.ds(at_128(FF_CORE * c), FF_CORE)
    other_outer = pl.ds(at_128(FF_CORE * other), FF_CORE)
    lanes128 = lane_iota((1, 128))
    in_head = [jnp.logical_and(lanes128 >= 64 * e, lanes128 < 64 * e + 64) for e in (0, 1)]
    own_is_first = c == 0
    chip_weights = pl.ds(at_16(48 * p.chip), 48)
    sibling_half = pl.ds(at_128(128 * other), 128)

    def masked(value, e, scale=1.0):
        return jnp.where(in_head[e], value.astype(F32) * scale, 0.0).astype(BF16)

    def pair_cols(base, pair):
        return pl.ds(at_128(base + 128 * pair), 128)

    def exchange(index, partial):
        r.PX_S[index] = partial.astype(BF16)
        swap.start(6 + index, lambda: (r.PX_S.at[index], r.PX_R.at[index], p.sibling))

    def vector(index):
        return r.VEC[index : index + 1, :]

    kept_values = {}
    def take_weights():
        swap.arrived(0)
        for index, ref in enumerate((r.wq, r.wk, r.wv, r.wo)):
            where = slice(QUARTER * index, QUARTER * (index + 1))
            kept = ref[:, mine_cols].astype(F32)
            came = r.SWAP_R[:, where]
            both = jnp.concatenate(
                [jnp.where(own_is_first, kept, came), jnp.where(own_is_first, came, kept)], axis=0
            )
            r.WA[chip_weights, where] = both.astype(BF16)
        swap.arrived(1)
        kept = r.wi[:, pl.ds(at_128(FF_CORE * c), FF_CORE)].astype(F32)
        came = r.SWAP_R[:, 1536:3072]
        both = jnp.concatenate(
            [jnp.where(own_is_first, kept, came), jnp.where(own_is_first, came, kept)], axis=0
        )
        r.WI[chip_weights, :] = both.astype(BF16)
        swap.arrived(2)

    def mark_documents():
        one_row = lane_iota((1, 128))
        starts = jnp.full((1, 128), FAR, jnp.int32)
        nexts = jnp.full((1, 128), FAR, jnp.int32)
        count = r.docs.shape[0]
        for d in range(count):
            starts = jnp.where(one_row == d, r.docs[d], starts)
            if d:
                nexts = jnp.where(one_row == d - 1, r.docs[d], nexts)
        lanes = lane_iota((CHIP_ROWS, 128))
        for j in range(8):
            place = row_iota((CHIP_ROWS, 128)) + (p.x * HALF_ROWS + (j % 4) * 512 + (j // 4) * 256)
            inside = jnp.logical_and(place >= starts, place < nexts)
            rows = slice(j * CHIP_ROWS, (j + 1) * CHIP_ROWS)
            r.QE[rows, :] = jnp.where(inside, 1.0, 0.0).astype(BF16)
            r.KE[rows, :] = jnp.where(jnp.logical_or(inside, lanes >= 16), 0.0, PENALTY).astype(BF16)

    def spread_vectors():
        gs.complete()
        ga.complete()
        spread_rows = nn(r.WS[...], spread)
        chosen = jnp.where(owner == by_24, spread_rows, 0.0)
        r.VEC[...] = jnp.sum(chosen.reshape(32, 16, D), axis=0)
        part_of = jnp.where(
            jnp.logical_and(kind >= 8, kind < 12), 4 * (owner - 16 * c) + kind - 8, -1000
        )
        for u in (0, 1):
            chosen = jnp.where(part_of - 32 * u == by_24, spread_rows, 0.0)
            r.BIN[0:1, D * u : D * (u + 1)] = jnp.sum(chosen, axis=0, keepdims=True)
        r.WO[:, mine_cols] = r.WA[row_set, 1152:1536]
        swap.start(4, lambda: (r.WA.at[other_set, pl.ds(1152, QUARTER)], r.WO.at[:, mine_cols], p.sibling))

    outer_slot = sems.take(4)

    def outer_swap(z):
        rows = pl.ds(at_16((other * 8 + z * 2) * 192), QUARTER)
        return pltpu.make_async_remote_copy(
            r.WT.at[rows],
            r.WTR.at[pl.ds(at_128(z * QUARTER), QUARTER), mine_cols],
            sems.send.at[outer_slot + z],
            sems.recv.at[outer_slot + z],
            device_id=p.sibling,
            device_id_type=MESH,
        )

    def outer_rows_came(z):
        gt.copy("second", z).wait_recv()
        gt.copy("across", z).wait_recv()
        outer_swap(z).start()
        r.WTR[pl.ds(at_128(z * QUARTER), QUARTER), mine_cols] = r.WT[
            pl.ds(at_16((c * 8 + z * 2) * 192), QUARTER), :
        ]

    def outer_came(step):
        def run():
            if step == 0:
                outer_rows_came(p.z)
                return
            pl.when(p.has_below[step])(lambda: outer_rows_came(p.z - step))
            pl.when(p.has_above[step])(lambda: outer_rows_came(p.z + step))

        return run

    def project(j):
        value_bias = r.VEC[1:2, mine_cols]
        bias = jnp.concatenate([jnp.zeros_like(value_bias), value_bias], axis=1)
        for part in (0, 1):
            rows = pl.ds(at_128((2 * j + part) * CHIP_ROWS), CHIP_ROWS)
            r.QKV[rows, QUARTER:] = (nn(r.X[rows, :], r.WA[:, QUARTER:1152]) + bias).astype(BF16)

    def queries_of(rows):
        value = nn(r.X[rows, :], r.WA[:, 0:QUARTER]) + r.VEC[0:1, mine_cols]
        r.QKV[rows, 0:QUARTER] = value.astype(BF16)

    def chip_queries():
        queries_of(chip)

    def all_queries():
        def block(j, carry):
            queries_of(pl.ds(at_128(j * 512), 512))
            return carry

        lax.fori_loop(0, 4, block, 0)

    def attend(pair):
        query_doc = r.QE[chip, :]
        queries = r.QKV[chip, pair_cols(0, pair)]
        keys = jnp.concatenate([r.QKV[:, pair_cols(QUARTER, pair)], r.KE[...]], axis=1)
        values = r.QKV[:, pair_cols(2 * QUARTER, pair)]
        outputs = []
        for e in (0, 1):
            query = jnp.concatenate([masked(queries, e, 0.125), query_doc], axis=1)
            scores = nt(query, keys)
            top = jnp.max(scores, axis=1, keepdims=True)
            weights = jnp.exp(scores - top)
            total = jnp.sum(weights, axis=1, keepdims=True)
            outputs.append(nn(weights.astype(BF16), values) / total)
            log_total = top + jnp.log(total)
            r.LSE[...] = jnp.where(lanes128 == 2 * pair + e, log_total, r.LSE[...])
        r.ATT[:, pair_cols(0, pair)] = jnp.where(in_head[0], outputs[0], outputs[1]).astype(BF16)

    def first_norm():
        swap.arrived(4)
        swap.arrived(3)

        branch = nn(r.ATT[...], r.WO[...])
        exchange(0, branch)
        swap.arrived(6)
        branch = branch + r.PX_R[0].astype(F32) + vector(2)
        normed, kept_values["inverse"] = normed_of(r.X[chip, :].astype(F32) + branch)
        r.N1[...] = normed
        hidden = normed * vector(3) + vector(4)
        r.HID[...] = hidden
        r.HL[...] = hidden.astype(BF16)

    def inner_layer(first_block):
        def inner_block(j, carry):
            where = pl.ds(at_128(j * QUARTER), QUARTER)
            value = nn(r.HL[...], r.WI[:, where]) + r.BIN[0:1, where]
            phi = 0.5 + 0.5 * lax.erf(value * (0.5**0.5))
            r.ACT[:, where] = (value * phi).astype(BF16)
            r.GV[:, where] = value
            r.GP[:, where] = phi
            return carry

        lax.fori_loop(first_block, first_block + 2, inner_block, 0)

    def second_norm():
        for z in range(4):
            outer_swap(z).wait_recv()

        def outer_block(j, carry):
            where = pl.ds(at_128(j * 256), 256)
            r.PART[:, where] = nn(r.ACT[...], r.WTR[:, where])
            return carry

        lax.fori_loop(0, 3, outer_block, 0)
        exchange(1, r.PART[...])

        def slope_block(j, carry):
            where = pl.ds(at_128(j * QUARTER), QUARTER)
            value = r.GV[:, where]
            density = jnp.exp(value * value * -0.5) * 0.3989422804014327
            r.GP[:, where] = r.GP[:, where] + value * density
            return carry

        lax.fori_loop(0, 4, slope_block, 0)
        swap.arrived(7)
        outer = r.PART[...] + r.PX_R[1].astype(F32) + vector(5)
        normed2, inverse2 = normed_of(r.HID[...] + outer)
        r.N2[...] = normed2
        grad_out = r.OG[...].astype(F32)
        grad_resid2 = normed_back(grad_out * vector(6), normed2, inverse2)
        r.HID[...] = grad_resid2
        grad_outer = grad_resid2.astype(BF16)
        r.GO[...] = grad_outer

    def late_sums():
        normed2 = r.N2[own_half, :]
        r.out[...] = (normed2 * vector(6) + vector(7)).astype(BF16)
        grad_out = r.OG[own_half, :].astype(F32)
        grad_hidden = r.GH[own_half, :]
        for index, value in (
            (6, grad_out * normed2),
            (7, grad_out),
            (5, r.GO[own_half, :].astype(F32)),
            (3, grad_hidden * r.N1[own_half, :]),
            (4, grad_hidden),
            (2, r.GB[own_half, :].astype(F32)),
        ):
            r.SV[index : index + 1, :] = jnp.sum(value, axis=0, keepdims=True)

    ri = Reduce(p, sems, r.GI, 48, "y", (r.GI1, r.GI2, r.GI3))
    rj = Reduce(p, sems, r.GJ, 48, "x", (r.GJ1, r.GJ2, r.GJ3))
    rt = Reduce(p, sems, r.GT, 192, "x", (r.GT1, r.GT2, r.GT3))
    rw = Reduce(p, sems, r.GW, 48, "x", (r.GW1, r.GW2, r.GW3))
    rq = Reduce(p, sems, r.GQ, 48, "x", (r.GQ1, r.GQ2, r.GQ3))
    rk = Reduce(p, sems, r.GK, 48, "x", (r.GK1, r.GK2, r.GK3))
    rs = Reduce(p, sems, r.SG, 32, "y", (r.SG1, r.SG2, r.SG3))

    def back_piece(z, across):
        y = 1 - p.y if across else p.y
        return r.DO.at[pl.ds(at_128((y * 4 + z) * CHIP_ROWS), CHIP_ROWS)]

    def stat_piece(z, across):
        y = 1 - p.y if across else p.y
        return r.STAT.at[:, pl.ds(at_128((y * 4 + z) * CHIP_ROWS), CHIP_ROWS)]

    back = Gather(p, sems, back_piece, p.side["y"])
    stat = Gather(p, sems, stat_piece, p.side["y"])
    last = Mover(sems, 7)
    finals = {
        ri: (0, r.FI, r.FI_R, 24),
        rt: (1, r.FT, r.FT_R, 96),
        rw: (2, r.FW, r.FW_R, 24),
        rq: (3, r.FQ, r.FQ_R, 24),
        rk: (4, r.FK, r.FK_R, 24),
        rs: (5, r.FS, r.FS_R, 16),
        rj: (6, r.FJ, r.FJ_R, 24),
    }

    def final(reduce):
        def run():
            index, total, came, rows = finals[reduce]
            total[...] = reduce.result()
            last.start(
                index,
                lambda: (total.at[pl.ds(at_8(rows * other), rows)], came, p.sibling),
            )

        return run

    def outer_gradient():
        def outer_grads(j, carry):
            where = pl.ds(at_128(j * QUARTER), QUARTER)
            mine_rows = pl.ds(at_128(FF_CORE * c + j * QUARTER), QUARTER)
            r.GT_S[where, :] = tn(r.ACT[:, where], r.GO[:, other_cols]).astype(BF16)
            r.GT[mine_rows, :] = tn(r.ACT[:, where], r.GO[:, mine_cols]).astype(BF16)
            return carry

        lax.fori_loop(0, 4, outer_grads, 0)
        swap.start(10, lambda: (r.GT_S, r.GT.at[outer_set], p.sibling))

    def inner_back():
        def inner_back(j, carry):
            where = pl.ds(at_128(j * QUARTER), QUARTER)
            grad = (nt(r.GO[...], r.WTR[where, :]) * r.GP[:, where]).astype(BF16)
            r.GIN[:, where] = grad
            r.BIN[1:2, where] = jnp.sum(grad.astype(F32), axis=0, keepdims=True)
            return carry

        lax.fori_loop(0, 3, inner_back, 0)
        for u in (0, 1):
            r.SV[pl.ds(8 + 2 * c + u, 1), :] = r.BIN[1:2, D * u : D * (u + 1)]

    def inner_back_last():
        where = slice(1152, 1536)
        grad = (nt(r.GO[...], r.WTR[where, :]) * r.GP[:, where]).astype(BF16)
        r.GIN[:, where] = grad
        r.BIN[1:2, where] = jnp.sum(grad.astype(F32), axis=0, keepdims=True)
        r.GJ[...] = tn(r.HL[...], grad).astype(BF16)

    def inner_gradient():
        def inner_grads(j, carry):
            where = pl.ds(at_128(j * QUARTER), QUARTER)
            r.GI[:, where] = tn(r.HL[...], r.GIN[:, where]).astype(BF16)
            return carry

        lax.fori_loop(0, 3, inner_grads, 0)

    def hidden_back():
        def hidden_back(j, carry):
            where = pl.ds(at_128(j * 256), 256)
            r.PART[:, where] = nt(r.GIN[...], r.WI[where, :])
            return carry

        lax.fori_loop(0, 3, hidden_back, 0)
        exchange(2, r.PART[...])

    def first_norm_back():
        swap.arrived(8)
        grad_hidden = r.HID[...] + r.PART[...] + r.PX_R[2].astype(F32)
        normed = r.N1[...]
        grad_resid1 = normed_back(grad_hidden * vector(3), normed, kept_values["inverse"])
        r.GH[...] = grad_hidden
        r.HID[...] = grad_resid1
        grad_branch = grad_resid1.astype(BF16)
        r.GB[...] = grad_branch
        grad_attended = nt(grad_branch, r.WO[...]).astype(BF16)
        r.DO[chip, :] = grad_attended
        attended = r.ATT[...].astype(F32)
        product = grad_attended.astype(F32) * attended
        for head in range(CORE_HEADS):
            pair = slice(128 * (head // 2), 128 * (head // 2) + 128)
            delta = jnp.sum(jnp.where(in_head[head % 2], product[:, pair], 0.0), axis=1, keepdims=True)
            r.DELTA[...] = jnp.where(lanes128 == head, delta, r.DELTA[...])
        chip_lanes = pl.ds(at_128(chip_base), CHIP_ROWS)
        r.STAT[0:8, chip_lanes] = jnp.transpose(r.LSE[...])[0:8, :]
        r.STAT[8:16, chip_lanes] = jnp.transpose(r.DELTA[...])[0:8, :]

        back.begin()
        stat.begin()

    def output_gradient():
        r.GW_S[...] = tn(r.ATT[...], r.GB[:, other_cols]).astype(BF16)
        r.GW[row_set, :] = tn(r.ATT[...], r.GB[:, mine_cols]).astype(BF16)
        swap.start(11, lambda: (r.GW_S, r.GW.at[row_set], p.sibling))

    def query_back(pair):
        query_doc = r.QE[chip, :]
        queries = r.QKV[chip, pair_cols(0, pair)]
        keys = r.QKV[:, pair_cols(QUARTER, pair)]
        keys_doc = jnp.concatenate([keys, r.KE[...]], axis=1)
        values = r.QKV[:, pair_cols(2 * QUARTER, pair)]
        grads = r.DO[chip, pair_cols(0, pair)]
        outputs = []
        for e in (0, 1):
            pick = lanes128 == 2 * pair + e
            log_total = jnp.sum(jnp.where(pick, r.LSE[...], 0.0), axis=1, keepdims=True)
            delta = jnp.sum(jnp.where(pick, r.DELTA[...], 0.0), axis=1, keepdims=True)
            query = jnp.concatenate([masked(queries, e, 0.125), query_doc], axis=1)
            probs = jnp.exp(nt(query, keys_doc) - log_total)
            grad_probs = nt(masked(grads, e), values)
            grad_scores = (probs * (grad_probs - delta)).astype(BF16)
            outputs.append(nn(grad_scores, keys) * 0.125)
        r.DQKV[:, pair_cols(0, pair)] = jnp.where(in_head[0], outputs[0], outputs[1]).astype(BF16)

    def query_gradient():
        r.GQ[...] = tn(r.X[chip, :], r.DQKV[:, 0:QUARTER]).astype(BF16)

    def key_back(pair):
        key_doc = r.KE[chip, :]
        keys = r.QKV[chip, pair_cols(QUARTER, pair)]
        values = r.QKV[chip, pair_cols(2 * QUARTER, pair)]
        queries = r.QKV[:, pair_cols(0, pair)]
        queries_doc = jnp.concatenate([queries, r.QE[...]], axis=1)
        grads = r.DO[:, pair_cols(0, pair)]
        key_grads, value_grads = [], []
        for e in (0, 1):
            log_total = r.STAT[pl.ds(2 * pair + e, 1), :]
            delta = r.STAT[pl.ds(8 + 2 * pair + e, 1), :]
            key = jnp.concatenate([masked(keys, e, 0.125), key_doc], axis=1)
            probs = jnp.exp(nt(key, queries_doc) - log_total)
            value_grads.append(nn(probs.astype(BF16), grads))
            grad_probs = nt(masked(values, e), grads)
            grad_scores = (probs * (grad_probs - delta)).astype(BF16)
            key_grads.append(nn(grad_scores, queries) * 0.125)
        r.DQKV[:, pair_cols(QUARTER, pair)] = jnp.where(
            in_head[0], key_grads[0], key_grads[1]
        ).astype(BF16)
        r.DQKV[:, pair_cols(2 * QUARTER, pair)] = jnp.where(
            in_head[0], value_grads[0], value_grads[1]
        ).astype(BF16)

    def key_gradients():
        def project_grads(j, carry):
            where = pl.ds(at_128(j * QUARTER), QUARTER)
            source = pl.ds(at_128((j + 1) * QUARTER), QUARTER)
            r.GK[:, where] = tn(r.X[chip, :], r.DQKV[:, source]).astype(BF16)
            return carry

        lax.fori_loop(0, 2, project_grads, 0)

    def tokens_gradient():
        def tokens_back(j, carry):
            where = pl.ds(at_128(j * 256), 256)
            r.PART[:, where] = nt(r.DQKV[...], r.WA[where, 0:1152])
            return carry

        lax.fori_loop(0, 3, tokens_back, 0)
        r.PX_S[3, 0:128, :] = r.PART[sibling_half, :].astype(BF16)
        swap.start(9, lambda: (r.PX_S.at[3, pl.ds(0, 128)], r.PX_R.at[3, pl.ds(0, 128)], p.sibling))

        r.SV[0:1, mine_cols] = jnp.sum(r.DQKV[:, 0:QUARTER].astype(F32), axis=0, keepdims=True)
        r.SV[1:2, mine_cols] = jnp.sum(r.DQKV[:, 2 * QUARTER :].astype(F32), axis=0, keepdims=True)
        by_96, in_96 = lax.div(column, 96), lax.rem(column, 96)
        gather_96 = jnp.where(row_iota((128, D)) == in_96, 1.0, 0.0).astype(BF16)
        sums = jnp.broadcast_to(r.SV[...].reshape(1, 16, D), (32, 16, D)).reshape(512, D)
        late = kind >= 8
        wanted = jnp.where(late, 8 * (kind - 8) + by_96, by_24) == owner
        sums = jnp.where(wanted, sums, 0.0)
        high = sums.astype(BF16)
        low_part = (sums - high.astype(F32)).astype(BF16)
        r.SG[...] = jnp.where(
            late,
            nt(high, gather_96) + nt(low_part, gather_96),
            nt(high, spread) + nt(low_part, spread),
        )

    r.SV[...] = jnp.zeros_like(r.SV)
    r.LSE[...] = jnp.zeros_like(r.LSE)
    r.DELTA[...] = jnp.zeros_like(r.DELTA)
    kept24 = pl.ds(at_8(24 * c), 24)

    def early_outputs():
        swap.arrived(9)
        r.tgrad[...] = (
            r.HID[own_half, :] + r.PART[own_half, :] + r.PX_R[3, 0:128, :].astype(F32)
        ).astype(BF16)

        last.arrived(0)
        last.arrived(6)
        r.gi[:, pl.ds(at_128(FF_CORE * c), 1152)] = r.FI[kept24, :]
        r.gi[:, pl.ds(at_128(FF_CORE * other), 1152)] = r.FI_R[...]
        r.gi[:, pl.ds(at_128(FF_CORE * c + 1152), QUARTER)] = r.FJ[kept24, :]
        r.gi[:, pl.ds(at_128(FF_CORE * other + 1152), QUARTER)] = r.FJ_R[...]
        last.arrived(1)
        r.gt[:, mine_cols] = r.FT[pl.ds(at_8(96 * c), 96), :]
        r.gt[:, other_cols] = r.FT_R[...]
        last.arrived(2)
        r.go[:, mine_cols] = r.FW[kept24, :]
        r.go[:, other_cols] = r.FW_R[...]
        last.arrived(3)
        r.gq[:, mine_cols] = r.FQ[kept24, :]
        r.gq[:, other_cols] = r.FQ_R[...]

    forward = [
        first(tok), take_weights, first(gt), z_start(ga, gs), z_start(tok), first(gj), first(gi),
        second(ga, gs), first(ga, gs), second(tok), second(gi), across(0, gj), hop(1, ga, gs),
        across(0, ga, gs), hop(1, tok), hop(2, ga, gs), across(0, gi), across(0, tok), z_start(gi),
        z_start(gt), second(gt), hop(1, gi), second(gj), mark_documents, hop(2, tok),
        across(1, ga, gs), z_start(gj), hop(3, ga, gs), across(1, tok), across(0, gt), hop(3, tok),
        hop(2, gi), across(2, ga, gs), hop(3, gi), hop(1, gj), across(3, ga, gs), hop(1, gt),
        hop(2, gt), across(1, gi), across(2, tok), across(3, tok), tok.complete, outer_came(0),
        hop(2, gj), hop(3, gt), spread_vectors, across(2, gi),
        loop(
            project,
            [
                hop(3, gj), across(3, gi),
            ],
            [
                across(1, gj),
            ],
            [],
        ),
        chip_queries,
        loop(
            attend,
            [
                across(1, gt), across(2, gt),
            ],
            [
                across(2, gj),
            ],
        ),
        across(3, gt), first_norm, gi.complete, lambda: inner_layer(0), across(3, gj),
        outer_came(1), gj.complete, outer_came(2), outer_came(3), lambda: inner_layer(2),
        second_norm,
    ]
    backward = [
        inner_back_last, inner_back, inner_gradient, one(ri), one(rj), outer_gradient,
        lambda: swap.arrived(10), one(rt), two(ri, 1), hidden_back, first_norm_back, two(ri, 2),
        two(ri, 3), output_gradient, all_queries,
        loop(
            query_back,
            [
                two(rt, 2), hop(1, back, stat), hop(2, back, stat), three(rt, 2),
            ],
            [],
        ),
        hop(3, back, stat), two(rj, 1), across(0, back, stat), late_sums, query_gradient,
        three(ri, 1), across(1, back, stat), two(rj, 2), two(rt, 1), lambda: swap.arrived(11),
        one(rw), two(rt, 3), three(ri, 2), three(ri, 3), two(rj, 3), one(rq), two(rj, 0),
        across(2, back, stat), across(3, back, stat),
        loop(
            key_back,
            [
                two(rw, 1), three(rj, 2),
            ],
            [
                three(rj, 1), three(rt, 1),
            ],
        ),
        three(rt, 3), two(rw, 2), two(rw, 3), key_gradients, one(rk), two(rq, 1), three(rj, 0),
        two(rq, 2), two(rq, 3), three(rw, 2), two(rw, 0), three(rw, 1), tokens_gradient, one(rs),
        three(rw, 3), two(rk, 1), three(rj, 3), two(rs, 1), three(rq, 3), three(rq, 2), two(rs, 2),
        three(rw, 0), final(rw), two(rk, 2), three(rq, 1), two(rs, 3), two(rq, 0), three(rk, 1),
        two(rk, 3), three(rk, 2), two(ri, 0), two(rs, 0), two(rt, 0), two(rk, 0), three(rk, 3),
        three(rq, 0), final(rq), final(rj), three(rs, 1), three(rs, 3), three(rs, 2), three(rt, 0),
        three(ri, 0), final(ri), three(rs, 0), final(rt), three(rk, 0), final(rs), early_outputs,
        final(rk),
    ]
    for step in forward + backward:
        step()

    last.arrived(4)
    for index, ref in enumerate((r.gk, r.gv)):
        where = slice(QUARTER * index, QUARTER * (index + 1))
        ref[:, mine_cols] = r.FK[kept24, where]
        ref[:, other_cols] = r.FK_R[:, where]
    last.arrived(5)
    totals = r.FS[pl.ds(at_8(16 * c), 16), :] + r.FS_R[...]
    inner_total = totals[8:9] + totals[9:10] + totals[10:11] + totals[11:12]
    r.gs[0:8, :] = totals[0:8]
    r.gs[8:16, :] = jnp.broadcast_to(inner_total, (8, 128))

    for z in range(4):
        outer_swap(z).wait_send()
    for mover in (swap, tok, gs, ga, gi, gj, gt, back, stat, ri, rj, rt, rw, rq, rk, rs, last):
        mover.sent()


def hand_out(*refs):
    count = 8
    for source, target in zip(refs[:count], refs[count + 1 :]):
        target[...] = source[...]
    vectors = refs[count]
    for row, target in enumerate(refs[2 * count + 1 :]):
        target[...] = vectors[row, 0 : target.shape[0]]


def slice_body(
    tokens, query_weight, query_bias, key_weight, value_weight, value_bias, output_weight, output_bias,
    first_gain, first_shift, inner_weight, inner_bias, outer_weight, outer_bias, second_gain,
    second_shift, doc_starts, out_grad,
):
    vectors = (
        query_bias, value_bias, output_bias, first_gain, first_shift, outer_bias, second_gain,
        second_shift, inner_bias,
    )
    vectors = tuple(value.reshape(1, -1) for value in vectors)
    shape = jax.ShapeDtypeStruct
    vmem = pl.BlockSpec(memory_space=pltpu.VMEM)
    out_shapes = (
        shape((128, D), BF16), shape((128, D), BF16), shape((24, D), F32), shape((24, D), F32),
        shape((24, D), F32), shape((24, D), F32), shape((24, 3072), F32), shape((96, D), F32),
        shape((16, 128), F32),
    )
    results = pl.pallas_call(
        layer_kernel,
        out_shape=out_shapes,
        in_specs=[vmem] * 17 + [pl.BlockSpec(memory_space=pltpu.SMEM)],
        out_specs=[vmem] * 9,
        scratch_shapes=[pltpu.VMEM(*entry) for entry in SCRATCH.values()]
        + [pltpu.SemaphoreType.DMA((SEM_COUNT,)), pltpu.SemaphoreType.DMA((SEM_COUNT,))],
        compiler_params=pltpu.CompilerParams(
            collective_id=0, has_side_effects=True, vmem_limit_bytes=62 * 2**20
        ),
        name="layer",
    )(
        tokens, out_grad, query_weight, key_weight, value_weight, output_weight, inner_weight,
        outer_weight, *vectors, doc_starts,
    )
    vector_shapes = (shape((24,), F32),) * 8 + (shape((96,), F32),)
    out, tgrad, gq, gk, gv, go, gi, gt, *v = pl.pallas_call(
        hand_out,
        out_shape=out_shapes[:8] + vector_shapes,
        in_specs=[vmem] * 9,
        out_specs=[vmem] * 17,
        name="hand_out",
    )(*results)
    return (
        out, tgrad, gq, v[0], gk, gv, v[1], go, v[2], v[3], v[4], gi, v[8], gt, v[5], v[6], v[7]
    )


def solution(mesh):
    rows, flat = P(("head", "blk"), None), P(("head", "blk"))
    in_specs = (
        rows, rows, flat, rows, rows, flat, rows, flat, flat, flat, rows, flat, rows, flat, flat, flat,
        P(), rows,
    )
    out_specs = (
        rows, rows, rows, flat, rows, rows, flat, rows, flat, flat, flat, rows, flat, rows, flat, flat,
        flat,
    )
    small_slice = mesh.shape["head"] == 2 and mesh.shape["blk"] == 16
    return jax.shard_map(
        slice_body if small_slice else body,
        mesh=mesh,
        in_specs=in_specs,
        out_specs=out_specs,
        check_vma=False,
    )
```
